512 devices in a mesh: outer: 8 (over y), chip: 64 (over z, x, core).
Axes of the slice: x: 4, y: 8, z: 8, core: 2. Of those that a mesh axis runs over, the one named last changes fastest.
Arguments:
- block_input: bfloat16 [8, 24, 24, 1536], P('outer', None, None, 'chip'), may hold values from -6 to 6
- depth_kernel: float32 [7, 7, 1536], replicated, may hold values from -0.875 to 0.875
- w_expand: bfloat16 [1536, 8192], P(None, 'chip'), may hold values from -0.15625 to 0.15625
- grad_hidden: bfloat16 [8, 24, 24, 8192], P('outer', None, None, 'chip'), may hold values from -0.119628906 to 0.119628906
- error_old: float32 [8, 1536, 8192], P('outer', None, 'chip'), may hold values from -3 to 3
- right_init: float32 [8192, 32], P('chip'), may hold values from -6 to 6
Outputs:
- kernel_grad: float32 [7, 7, 1536], P(None, None, 'chip')
- factor_left: float32 [1536, 32], replicated
- factor_right: float32 [8192, 32], P('chip')
- error_new: float32 [8, 1536, 8192], P('outer', None, 'chip')
The draws below stay inside these ranges and needn't reach their ends.
All inputs are finite; a program needn't handle non-finite values.
Results may differ from the reference program's by a relative error of at most 0.0023.
Values may be sent and summed in bfloat16 or wider, within the bound.
A program may use at most 64 MiB of HBM per device.

```python
import jax
import jax.numpy as jnp
from jax import lax

C = 1536
HID = 8192
RANK = 32
SIDE = 24
KSIZE = 7
WORKERS = 8
IMAGES = 8
N_OUTER = 8


def shard_levels(key, dims, pieces, smallest, largest):
    level, own = 1.0, jax.random.fold_in(key, 6)
    for position, parts in pieces:
        draws = jnp.exp(jax.random.uniform(jax.random.fold_in(own, position), (parts,), jnp.float32, smallest / len(pieces), largest / len(pieces)))
        level = level * jnp.repeat(draws, dims[position] // parts).reshape([-1 if axis == position else 1 for axis in range(len(dims))])
    return level


def noise(stream_key, dims, deviation, most, shards=(), held_as=jnp.bfloat16):
    array = deviation * jax.random.normal(stream_key, dims, jnp.float32)
    if shards:
        array = array * shard_levels(stream_key, dims, shards, -0.22, 0.18)
    return jnp.clip(array, -most, most).astype(held_as)


def setup_inputs(seed: int = 0) -> dict:
    key_list = jax.random.split(jax.random.key(seed), 7)
    block_input = noise(key_list[0], (IMAGES, SIDE, SIDE, C), 1.0, 6.0, ((0, 8), (3, 64)))
    depth_kernel = noise(key_list[1], (KSIZE, KSIZE, C), (KSIZE * KSIZE) ** -0.5, 0.875, (), jnp.float32)
    w_expand = noise(key_list[2], (C, HID), C ** -0.5, 0.15625, ((1, 64),))
    grad_hidden = noise(key_list[3], (IMAGES, SIDE, SIDE, HID), 0.02, 0.119628906, ((0, 8), (3, 64)))
    error_old = noise(key_list[4], (WORKERS, C, HID), 0.5, 3.0, ((0, 8), (2, 64)), jnp.float32)
    right_init = noise(key_list[5], (HID, RANK), 1.0, 6.0, ((0, 64),), jnp.float32)
    return {"block_input": block_input, "depth_kernel": depth_kernel, "w_expand": w_expand, "grad_hidden": grad_hidden, "error_old": error_old, "right_init": right_init}


HIGH = lax.Precision.HIGHEST

def depthwise(maps, kern):
    half = kern.shape[0] // 2
    side = maps.shape[1]
    padded = jnp.pad(maps, ((0, 0), (half, half), (half, half), (0, 0)))
    total = jnp.zeros(maps.shape, jnp.float32)
    for row in range(kern.shape[0]):
        for col in range(kern.shape[1]):
            total = total + padded[:, row:row + side, col:col + side, :].astype(jnp.float32) * kern[row, col]
    return total.astype(jnp.bfloat16)

def kernel_terms(maps, grad_conv, ksize):
    half = ksize // 2
    side = maps.shape[1]
    padded = jnp.pad(maps, ((0, 0), (half, half), (half, half), (0, 0)))
    rows = []
    for row in range(ksize):
        cols = []
        for col in range(ksize):
            window = padded[:, row:row + side, col:col + side, :].astype(jnp.float32)
            cols.append(jnp.sum(grad_conv * window, axis=(0, 1, 2)))
        rows.append(jnp.stack(cols))
    return jnp.stack(rows)

def worker(maps, grads, error, depth_kernel, w_expand, right_init):
    conv = depthwise(maps, depth_kernel)
    flat_conv = conv.reshape(-1, conv.shape[-1])
    flat_grad = grads.reshape(-1, grads.shape[-1])
    local_grad = lax.dot_general(flat_conv.astype(jnp.float32), flat_grad.astype(jnp.float32), (((0,), (0,)), ((), ())), preferred_element_type=jnp.float32)
    grad_conv = lax.dot_general(flat_grad.astype(jnp.float32), w_expand.astype(jnp.float32), (((1,), (1,)), ((), ())), preferred_element_type=jnp.float32)
    grad_conv = grad_conv.reshape(maps.shape)
    kern_term = kernel_terms(maps, grad_conv, depth_kernel.shape[0])
    corrected = local_grad + error
    left_term = jnp.dot(corrected, right_init, precision=HIGH)
    return (corrected, left_term, kern_term)

def reference(block_input, depth_kernel, w_expand, grad_hidden, error_old, right_init):
    count = N_OUTER
    maps = block_input.reshape((count, -1) + block_input.shape[1:])
    grads = grad_hidden.reshape((count, -1) + grad_hidden.shape[1:])

    def one(items):
        return worker(items[0], items[1], items[2], depth_kernel, w_expand, right_init)
    corrected, left_terms, kern_terms = lax.map(one, (maps, grads, error_old))
    kernel_grad = jnp.sum(kern_terms, axis=0)
    left_sum = jnp.sum(left_terms, axis=0)
    gram = jnp.dot(left_sum.T, left_sum, precision=HIGH)
    chol = jnp.linalg.cholesky(gram)
    factor_left = lax.linalg.triangular_solve(chol, left_sum, left_side=False, lower=True, transpose_a=True)
    factor_right = jnp.sum(jnp.einsum('wch,cr->whr', corrected, factor_left, precision=HIGH), axis=0)
    approx = jnp.dot(factor_left, factor_right.T, precision=HIGH) / count
    error_new = corrected - approx[None, :, :]
    return (kernel_grad, factor_left, factor_right, error_new)
```

```python
import functools

import jax
import jax.numpy as jnp
from jax import lax
from jax.experimental import pallas as pl
from jax.experimental.pallas import tpu as pltpu
from jax.sharding import PartitionSpec as P

F32 = jnp.float32
BF16 = jnp.bfloat16
HIGH = lax.Precision.HIGHEST
MESH = pl.DeviceIdType.MESH

NX = 4
SIDE = 24
POS = SIDE * SIDE
LP = 640
LX = 896
OWN = 24
RANK = 32


def dot(a, b, dims, precision=None):
    return lax.dot_general(a, b, (dims, ((), ())), precision=precision, preferred_element_type=F32)


NN = ((1,), (0,))
NT = ((1,), (1,))
TN = ((0,), (0,))


def loop(lo, hi, body, unroll=1):
    def step(i, carry):
        body(i)
        return carry

    lax.fori_loop(lo, hi, step, 0, unroll=unroll)


def split2(v):
    hi = v.astype(BF16)
    return hi, (v - hi.astype(F32)).astype(BF16)


def split3(v):
    hi = v.astype(BF16)
    rest = v - hi.astype(F32)
    mid = rest.astype(BF16)
    return hi, mid, (rest - mid.astype(F32)).astype(BF16)


def kernel(
    ny, nz, nx,
    x_hbm, k_hbm, w_hbm, gh_hbm, err_hbm, r_hbm,
    kg_out, left_out, right_out, w_out, ls4, cor,
    x_ref, k_ref, w_ref, err_ref, r_ref,
    ghp, ghs, ws, rs, wf, x2, xz, xp, xs, mk, kflat, kt, conv32, cvf, gr, gb, rh1, rh2, g32,
    eg, gg, es, cs, gt, st, rz, ys, ll, chl, rp, kgt, rk, yk, lsn,
    s_in,
    s_xz, r_xz, s_es, r_es, s_cs, r_cs, s_gt, r_gt, s_rz, r_rz, s_ys, r_ys, s_lx, r_lx, s_lz, r_lz,
    s_lk, r_lk, s_rp, r_rp, s_rk, r_rk, s_yk, r_yk, s_in2, r_in2, s_gx, r_gx, s_cx, r_cx, s_cc, r_cc,
):
    nxk = 2 * nx
    ch = OWN * nz
    channels = ch * nxk
    tpz = 8 // nz
    half = ch // 2
    workers = ny
    y = lax.axis_index("outer")
    chip = lax.axis_index("chip")
    z = chip // nxk
    xk = lax.rem(chip, nxk)
    x = xk // 2
    k = lax.rem(xk, 2)

    def zpeer(s):
        return lax.rem(z + s, nz)

    def at_z(zz):
        return (y, zz * nxk + xk)

    def at_x(xx):
        return (y, z * nxk + xx * 2 + k)

    right_x = lax.rem(x + 1, nx)
    left_x = lax.rem(x + nx - 1, nx)
    far_x = lax.rem(x + 2, nx)

    def at_y(yy):
        return (yy, chip)

    sibling = (y, z * nxk + x * 2 + (1 - k))

    def copy(src, dst, ssem, rsem, dev):
        return pltpu.make_async_remote_copy(
            src_ref=src, dst_ref=dst, send_sem=ssem, recv_sem=rsem,
            device_id=dev, device_id_type=MESH,
        )

    load_x = pltpu.make_async_copy(x_hbm, x_ref, s_in.at[0])
    load_r = pltpu.make_async_copy(r_hbm, r_ref, s_in.at[1])
    load_err = pltpu.make_async_copy(err_hbm, err_ref, s_in.at[2])
    load_gh = pltpu.make_async_copy(gh_hbm, ghp.at[pl.ds(0, POS)], s_in.at[3])
    load_w = pltpu.make_async_copy(w_hbm, w_ref, s_in.at[4])
    load_k = pltpu.make_async_copy(k_hbm, k_ref, s_in.at[5])
    for load in (load_x, load_r, load_err, load_gh, load_w, load_k):
        load.start()

    barrier = pltpu.get_barrier_semaphore()

    def greet(dev):
        pl.semaphore_signal(barrier, inc=1, device_id=dev, device_id_type=MESH)

    loop(1, nz, lambda s: greet(at_z(zpeer(s))))
    loop(1, nx, lambda s: greet(at_x(lax.rem(x + s, nx))))
    greet(sibling)
    loop(1, ny, lambda s: greet(at_y(lax.rem(y + s, ny))))

    x2[...] = jnp.zeros((3, LX, OWN), F32)
    load_x.wait()
    for i in range(SIDE):
        image_row = x_ref[i].astype(F32)
        x2[0, SIDE * i : SIDE * (i + 1), :] = image_row
        late = i >= SIDE // 2
        at = POS + SIDE * (i % (SIDE // 2))
        x2[2 if late else 1, at : at + SIDE, :] = image_row
    out_row = lax.broadcasted_iota(jnp.int32, (16, OWN), 0)
    channel = lax.broadcasted_iota(jnp.int32, (16, OWN), 1)
    picks = (
        channel == out_row,
        (channel == out_row + 16) & (out_row < 8),
        (channel == out_row + 8) & (out_row >= 8),
    )
    packed = None
    for j in range(3):
        term = dot(picks[j].astype(F32).astype(BF16), x2[j].astype(BF16), NT)
        packed = term if packed is None else packed + term
    xz[z] = packed.astype(BF16)
    ghp[POS:, :] = jnp.zeros((LP - POS, 128), BF16)
    ghs[POS:, :] = jnp.zeros((LP - POS, 128), BF16)

    load_r.wait()
    load_err.wait()
    rh, rl = split2(r_ref[...])
    four = jnp.concatenate(
        [jnp.concatenate([rh, rh], axis=1), jnp.concatenate([rl, rl], axis=1)], axis=0
    )
    for q in range(nxk):
        eh, el = split2(err_ref[:, q].reshape(ch, 128))
        rows = jnp.concatenate([eh, el], axis=1)
        if ch < 256:
            rows = jnp.concatenate([rows, jnp.zeros((256 - ch, 256), BF16)], axis=0)
        e = dot(four, rows, NT)
        e = e[0:32] + e[32:64]
        for rg in range(4):
            for part in range(2):
                eg[q // 2, q % 2, 2 * rg + part] = e[8 * rg : 8 * rg + 8, 128 * part : 128 * part + 128]

    pl.semaphore_wait(barrier, (nz - 1) + (nx - 1) + (ny - 1) + 1)

    es_copy = copy(eg.at[:, 1 - k], es, s_es.at[0], r_es.at[0], sibling)
    in_gh = copy(gh_hbm, ghs.at[pl.ds(0, POS)], s_in2.at[0], r_in2.at[0], sibling)
    in_r = copy(r_hbm, rs, s_in2.at[1], r_in2.at[1], sibling)
    in_w = copy(w_hbm, ws, s_in2.at[2], r_in2.at[2], sibling)

    def xz_copy(s):
        return copy(xz.at[z], xz.at[z], s_xz.at[s], r_xz.at[s], at_z(zpeer(s)))

    loop(1, nz, lambda s: xz_copy(s).start())
    for one in (in_r, in_gh, es_copy, in_w):
        one.start()

    load_k.wait()
    for a in range(7):
        kflat[8 * a : 8 * a + 7, :] = k_ref[a]
        kflat[8 * a + 7 : 8 * a + 8, :] = jnp.zeros((1, channels), F32)
    kflat[56:64, :] = jnp.zeros((8, channels), F32)
    row = lax.broadcasted_iota(jnp.int32, (OWN, channels), 0)
    lane = lax.broadcasted_iota(jnp.int32, (OWN, channels), 1)
    apart = lane - row - xk * OWN
    pick = jnp.concatenate([(apart == zz * nxk * OWN).astype(F32) for zz in range(nz)], axis=0)
    three = jnp.concatenate(split3(kflat[...]), axis=0)
    taps3 = dot(pick.astype(BF16), three, NT)
    kt[...] = taps3[:, 0:64] + taps3[:, 64:128] + taps3[:, 128:192]
    pos = lax.broadcasted_iota(jnp.int32, (8, LP), 1)
    col = lax.rem(pos, SIDE) + lax.broadcasted_iota(jnp.int32, (8, LP), 0) - 3
    mk[...] = ((col >= 0) & (col < SIDE) & (pos < POS)).astype(F32)
    xp[:, 0:128] = jnp.zeros((ch, 128), F32)
    xp[:, 128 + LP :] = jnp.zeros((ch, LX - 128 - LP), F32)

    load_gh.wait()
    in_gh.wait_recv()
    in_r.wait_recv()
    sh, sl = split2(rs[...])
    both = jnp.concatenate([ghp[...], ghs[...]], axis=1)
    g = dot(
        jnp.concatenate([rh, sh, rl, sl], axis=1), jnp.concatenate([both, both], axis=1), NT
    )
    for rg in range(4):
        for j in range(5):
            gg[rg // 2, (rg % 2) * 5 + j] = g[8 * rg : 8 * rg + 8, 128 * j : 128 * j + 128]

    es_copy.wait_recv()

    def chip_sum(xx):
        cs[xx, 0, 0:8] = eg[xx, k] + es[xx]
        cs[xx, 0, 8:18] = gg[k]

    loop(0, nx, chip_sum)
    cs[x, 1] = cs[x, 0]

    def cs_copy(s):
        xx = lax.rem(x + s, nx)
        return copy(cs.at[xx, 0], cs.at[x, 1], s_cs.at[s], r_cs.at[s], at_x(xx))

    loop(1, nx, lambda s: cs_copy(s).start())

    load_w.wait()
    in_w.wait_recv()
    wf[:, :, :, :, 0:128] = w_ref[...].astype(F32).reshape(nz, nx, 2, OWN, 128)
    wf[:, :, :, :, 128:256] = ws[...].astype(F32).reshape(nz, nx, 2, OWN, 128)

    def grad_rows(xx):
        rows = wf[:, xx, k].reshape(ch, 256).astype(BF16)
        return dot(rows, jnp.concatenate([ghp[...], ghs[...]], axis=1), NT)

    gb[0] = grad_rows(far_x).astype(BF16)
    far_right = copy(
        gb.at[0, pl.ds(0, half)], rh1.at[0], s_gx.at[0], r_gx.at[0], at_x(right_x)
    )
    far_left = copy(
        gb.at[0, pl.ds(half, half)], rh1.at[1], s_gx.at[1], r_gx.at[1], at_x(left_x)
    )
    far_right.start()
    far_left.start()
    gr[0] = grad_rows(right_x)
    gr[1] = grad_rows(left_x)
    g32[...] = grad_rows(x)

    loop(1, nx, lambda s: cs_copy(s).wait_recv())
    total = cs[0, 1]
    for q in range(1, nx):
        total = total + cs[q, 1]
    st[...] = total[0:8]
    gt[k] = total[8:18]
    gt_copy = copy(gt.at[k], gt.at[k], s_gt.at[0], r_gt.at[0], sibling)
    gt_copy.start()

    loop(1, nz, lambda s: xz_copy(s).wait_recv())
    lane_x = lax.broadcasted_iota(jnp.int32, (16, LX), 1)
    for zz in range(nz):
        v = xz[zz].astype(F32)
        xp[OWN * zz : OWN * zz + 16, 128 : 128 + LP] = jnp.where(lane_x < POS, v, 0.0)[:, 0:LP]
        early = pltpu.roll(v[0:8], LX - POS, 1)
        late = pltpu.roll(v[8:16], LX - POS // 2, 1)
        last = jnp.where(
            lane_x[0:8] < POS // 2, early, jnp.where(lane_x[0:8] < POS, late, 0.0)
        )
        xp[OWN * zz + 16 : OWN * zz + 24, 128 : 128 + LP] = last[:, 0:LP]

    def conv_rows(t):
        rows = pl.ds(pl.multiple_of(t * 8, 8), 8)
        v = xp[rows, :]
        taps = kt[rows, :]
        moved = [pltpu.roll(v, LX - (96 + SIDE * (a - 3)), 1)[:, 0:LP] for a in range(7)]
        for a in range(7):
            xs[a, rows, :] = moved[a]
        out = None
        for b in range(7):
            part = None
            for a in range(7):
                term = taps[:, 8 * a + b : 8 * a + b + 1] * moved[a]
                part = term if a == 0 else part + term
            part = pltpu.roll(part, LP - (32 + b - 3), 1) * mk[b : b + 1, :]
            out = part if b == 0 else out + part
        conv32[rows, :] = out

    loop(0, ch // 8, conv_rows, 2)
    cvf[x, k] = conv32[...].astype(BF16)

    mine = cvf.at[x, k]
    cx_copies = [
        copy(mine, mine, s_cx.at[0], r_cx.at[0], at_x(right_x)),
        copy(mine, mine, s_cx.at[1], r_cx.at[1], at_x(left_x)),
    ]
    for s in range(2):
        cx_copies[s].start()

    sources = (x, left_x, right_x, far_x)

    def cc_copy(s):
        block = cvf.at[sources[s], k]
        return copy(block, block, s_cc.at[s], r_cc.at[s], sibling)

    cc_copy(0).start()

    gt_copy.wait_recv()
    groups = []
    for rg in range(4):
        groups.append(
            jnp.concatenate([gt[rg // 2, (rg % 2) * 5 + j] for j in range(5)], axis=1)
        )
    gsplit = jnp.concatenate(split2(jnp.concatenate(groups, axis=0)), axis=0)
    conv_pad = cvf[x, k]
    if ch < 256:
        conv_pad = jnp.concatenate([conv_pad, jnp.zeros((256 - ch, LP), BF16)], axis=0)
    left = dot(gsplit, conv_pad, NT)
    left = left[0:32] + left[32:64]
    for rg in range(4):
        for part in range(2):
            st[2 * rg + part] += left[8 * rg : 8 * rg + 8, 128 * part : 128 * part + 128]

    def rz_copy(s):
        zz = zpeer(s)
        return copy(st.at[pl.ds(zz * tpz, tpz)], rz.at[z], s_rz.at[s], r_rz.at[s], at_z(zz))

    loop(1, nz, lambda s: rz_copy(s).start())
    rz[z] = st[pl.ds(z * tpz, tpz)]

    far_right.wait_recv()
    gb[1, 0:half, :] = (gr[0, 0:half, :] + rh1[0].astype(F32)).astype(BF16)
    gb[1, half:, :] = gr[0, half:, :].astype(BF16)
    near_right = copy(gb.at[1], rh2.at[0], s_gx.at[2], r_gx.at[2], at_x(right_x))
    near_right.start()
    far_left.wait_recv()
    gb[2, 0:half, :] = gr[1, 0:half, :].astype(BF16)
    gb[2, half:, :] = (gr[1, half:, :] + rh1[1].astype(F32)).astype(BF16)
    near_left = copy(gb.at[2], rh2.at[1], s_gx.at[3], r_gx.at[3], at_x(left_x))
    near_left.start()

    loop(1, nz, lambda s: rz_copy(s).wait_recv())
    total = rz[0]
    for q in range(1, nz):
        total = total + rz[q]
    ys[y] = total

    def ys_copy(s):
        return copy(ys.at[y], ys.at[y], s_ys.at[s], r_ys.at[s], at_y(lax.rem(y + s, ny)))

    loop(1, ny, lambda s: ys_copy(s).start())

    def local_grad(xx, kk):
        q = xx * 2 + kk
        part = dot(cvf[xx, kk], ghp[...], NN) + err_ref[:, q].reshape(ch, 128)
        cor[:, q] = part.reshape(nz, OWN, 128)
        chl[q, 0:ch, :] = jnp.concatenate(split2(part), axis=1)

    if ch < 256:
        chl[:, ch:, :] = jnp.zeros((nxk, 256 - ch, 256), BF16)
    local_grad(x, k)

    loop(1, ny, lambda s: ys_copy(s).wait_recv())
    total = ys[0]
    for q in range(1, ny):
        total = total + ys[q]
    ll[k, z, x] = total

    def lx_copy(s):
        own = ll.at[k, z, x]
        return copy(own, own, s_lx.at[s], r_lx.at[s], at_x(lax.rem(x + s, nx)))

    loop(1, nx, lambda s: lx_copy(s).start())

    cx_copies[0].wait_recv()
    part0 = cvf.at[left_x, k, pl.ds(0, half)]
    cx_copies.append(copy(part0, part0, s_cx.at[2], r_cx.at[2], at_x(right_x)))
    cx_copies[2].start()
    cc_copy(1).start()
    cx_copies[1].wait_recv()
    part1 = cvf.at[right_x, k, pl.ds(half, half)]
    cx_copies.append(copy(part1, part1, s_cx.at[3], r_cx.at[3], at_x(left_x)))
    cx_copies[3].start()
    cc_copy(2).start()
    local_grad(left_x, k)
    local_grad(right_x, k)

    def lx_wait(s):
        got = ll.at[k, z, lax.rem(x - s + nx, nx)]
        copy(got, got, s_lx.at[s], r_lx.at[s], at_x(lax.rem(x + s, nx))).wait_recv()

    loop(1, nx, lx_wait)

    def lz_copy(s):
        own = ll.at[k, z]
        return copy(own, own, s_lz.at[s], r_lz.at[s], at_z(zpeer(s)))

    loop(1, nz, lambda s: lz_copy(s).start())
    for s in range(3):
        cc_copy(s).wait_recv()
        local_grad(sources[s], 1 - k)

    def lz_wait(s):
        got = ll.at[k, lax.rem(z - s + nz, nz)]
        copy(got, got, s_lz.at[s], r_lz.at[s], at_z(zpeer(s))).wait_recv()

    near_right.wait_recv()
    near_left.wait_recv()
    g32[...] += rh2[0].astype(F32) + rh2[1].astype(F32)
    lane128 = lax.broadcasted_iota(jnp.int32, (8, 128), 1)

    def kernel_terms(t):
        rows = pl.ds(pl.multiple_of(t * 8, 8), 8)
        gt = g32[rows, :]
        out = jnp.zeros((8, 128), F32)
        for b in range(7):
            gm = pltpu.roll(gt * mk[b : b + 1, :], 32 + b - 3, 1)
            for a in range(7):
                one = jnp.sum(gm * xs[a, rows, :], axis=1, keepdims=True)
                out = jnp.where(lane128 == 7 * a + b, one, out)
        kgt[t // 3, pl.ds(pl.multiple_of(lax.rem(t, 3) * 8, 8), 8), :] = out

    loop(0, ch // 8, kernel_terms, 2)

    def rk_copy(s):
        zz = zpeer(s)
        return copy(kgt.at[zz], rk.at[z], s_rk.at[s], r_rk.at[s], at_z(zz))

    loop(1, nz, lambda s: rk_copy(s).start())
    rk[z] = kgt[z]

    loop(1, nz, lz_wait)
    lk_copy = copy(ll.at[k], ll.at[k], s_lk.at[0], r_lk.at[0], sibling)
    lk_copy.start()

    cx_copies[2].wait_recv()
    cx_copies[3].wait_recv()
    cc_copy(3).start()
    local_grad(far_x, k)
    lk_copy.wait_recv()

    def left_of(q):
        rows = []
        for rg in range(4):
            tiles = [ll[q % 2, t // tpz, q // 2, t % tpz] for t in (2 * rg, 2 * rg + 1)]
            rows.append(jnp.concatenate(tiles, axis=1))
        return jnp.concatenate(rows, axis=0)

    lefts = [left_of(q) for q in range(nxk)]
    wide3 = split3(jnp.concatenate(lefts, axis=1))
    stack3 = jnp.concatenate(wide3, axis=0)
    gram = None
    for part in wide3:
        term = dot(stack3, part, NT)
        term = term[0:32] + term[32:64] + term[64:96]
        gram = term if gram is None else gram + term
    for q in range(nxk):
        lsn[:, q] = lefts[q].T[0:ch].reshape(nz, OWN, RANK)
    natural = lsn[...].reshape(channels, RANK).T
    nh, nm, nl = split3(natural)
    ls4[...] = jnp.concatenate([nh, nm, nh, nm], axis=0).T

    row_id = lax.broadcasted_iota(jnp.int32, (RANK, RANK), 0)
    lane_id = lax.broadcasted_iota(jnp.int32, (RANK, RANK), 1)
    same = row_id == lane_id
    aug = jnp.concatenate([gram, same.astype(F32)], axis=1)
    row_col = lax.broadcasted_iota(jnp.int32, (RANK, 2 * RANK), 0)

    def full(v):
        return jnp.broadcast_to(v, (RANK, 2 * RANK))

    for i in range(0, RANK, 2):
        c0 = full(aug[:, i : i + 1])
        c1 = full(aug[:, i + 1 : i + 2])
        r0 = full(aug[i : i + 1, :])
        r1 = full(aug[i + 1 : i + 2, :])
        p00 = full(c0[i : i + 1, :])
        p01 = full(c1[i : i + 1, :])
        p11 = full(c1[i + 1 : i + 2, :])
        inv = 1.0 / (p00 * p11 - p01 * p01)
        u0 = (p11 * c0 - p01 * c1) * inv
        u1 = (p00 * c1 - p01 * c0) * inv
        u0 = jnp.where(row_col > i + 1, u0, jnp.where(row_col == i + 1, p01 / p00, 0.0))
        u1 = jnp.where(row_col > i + 1, u1, 0.0)
        aug = aug - u0 * r0 - u1 * r1
    diag = jnp.sum(jnp.where(same, aug[:, 0:RANK], 0.0), axis=1, keepdims=True)
    scale = lax.rsqrt(diag)
    scale = scale * (1.5 - 0.5 * diag * scale * scale)
    linv = aug[:, RANK:] * scale
    ih, im, il = split3(linv)
    left_out[...] = dot(
        jnp.concatenate([ih, ih, ih, im, im, il], axis=1),
        jnp.concatenate([nh, nm, nl, nh, nm, nh], axis=0),
        NN,
    )

    cc_copy(3).wait_recv()
    local_grad(far_x, 1 - k)

    loop(1, nz, lambda s: rk_copy(s).wait_recv())
    total = rk[0]
    for q in range(1, nz):
        total = total + rk[q]
    yk[y] = total

    def yk_copy(s):
        return copy(yk.at[y], yk.at[y], s_yk.at[s], r_yk.at[s], at_y(lax.rem(y + s, ny)))

    loop(1, ny, lambda s: yk_copy(s).start())

    right = None
    for q in range(nxk):
        term = dot(jnp.concatenate(split2(left_of(q)), axis=0), chl[q], NN)
        right = term if q == 0 else right + term
    right = right[0:32] + right[32:64]
    rp[y] = right[:, 0:128] + right[:, 128:256]

    def rp_copy(s):
        return copy(rp.at[y], rp.at[y], s_rp.at[s], r_rp.at[s], at_y(lax.rem(y + s, ny)))

    loop(1, ny, lambda s: rp_copy(s).start())

    loop(1, ny, lambda s: rp_copy(s).wait_recv())
    total = rp[0]
    for q in range(1, ny):
        total = total + rp[q]
    fright = dot(linv, total, NN, HIGH)
    right_out[...] = fright
    wh, wl = split2(dot(linv.T, fright, NN, HIGH) * (1.0 / workers))
    w_out[...] = jnp.concatenate([wh, wh, wl, wl], axis=0)

    loop(1, ny, lambda s: yk_copy(s).wait_recv())
    total = yk[0]
    for q in range(1, ny):
        total = total + yk[q]
    total = total.T
    for a in range(7):
        kg_out[a] = total[7 * a : 7 * a + 7]

    loop(1, nz, lambda s: xz_copy(s).wait_send())
    es_copy.wait_send()
    for one in (in_r, in_gh, in_w):
        one.wait_send()
    loop(1, nx, lambda s: cs_copy(s).wait_send())
    gt_copy.wait_send()
    loop(1, nz, lambda s: rz_copy(s).wait_send())
    loop(1, ny, lambda s: ys_copy(s).wait_send())
    loop(1, nx, lambda s: lx_copy(s).wait_send())
    loop(1, nz, lambda s: lz_copy(s).wait_send())
    lk_copy.wait_send()
    loop(1, ny, lambda s: rp_copy(s).wait_send())
    loop(1, nz, lambda s: rk_copy(s).wait_send())
    loop(1, ny, lambda s: yk_copy(s).wait_send())
    for s in range(4):
        cx_copies[s].wait_send()
        cc_copy(s).wait_send()
    for one in (far_right, far_left, near_right, near_left):
        one.wait_send()


def finish(kg_ref, left_ref, right_ref, w_ref, ls_ref, cor_ref, kg_out, left_out, right_out, err_out):
    kg_out[...] = kg_ref[...]
    left_out[...] = left_ref[...]
    right_out[...] = right_ref[...]
    approx = dot(ls_ref[...], w_ref[...], NN)
    err_out[...] = cor_ref[...] - approx.reshape(cor_ref.shape)


def on_device(ny, nz, nx, block_input, depth_kernel, w_expand, grad_hidden, error_old, right_init):
    nxk = 2 * nx
    ch = OWN * nz
    channels = nz * nxk * OWN
    tpz = 8 // nz
    hid = right_init.shape[0]
    vmem = pltpu.VMEM
    scratch = [
        vmem((SIDE, SIDE, OWN), BF16),
        vmem((7, 7, channels), F32),
        vmem((channels, 128), BF16),
        vmem((nz, nxk, OWN, 128), F32),
        vmem((RANK, 128), F32),
        vmem((LP, 128), BF16),
        vmem((LP, 128), BF16),
        vmem((channels, 128), BF16),
        vmem((RANK, 128), F32),
        vmem((nz, nx, 2, OWN, 256), F32),
        vmem((3, LX, OWN), F32),
        vmem((nz, 16, LX), BF16),
        vmem((ch, LX), F32),
        vmem((7, ch, LP), F32),
        vmem((8, LP), F32),
        vmem((64, channels), F32),
        vmem((ch, 64), F32),
        vmem((ch, LP), F32),
        vmem((nx, 2, ch, LP), BF16),
        vmem((2, ch, LP), F32),
        vmem((3, ch, LP), BF16),
        vmem((2, ch // 2, LP), BF16),
        vmem((2, ch, LP), BF16),
        vmem((ch, LP), F32),
        vmem((nx, 2, 8, 8, 128), F32),
        vmem((2, 10, 8, 128), F32),
        vmem((nx, 8, 8, 128), F32),
        vmem((nx, 2, 18, 8, 128), F32),
        vmem((2, 10, 8, 128), F32),
        vmem((8, 8, 128), F32),
        vmem((nz, tpz, 8, 128), F32),
        vmem((ny, tpz, 8, 128), F32),
        vmem((2, nz, nx, tpz, 8, 128), F32),
        vmem((nxk, 256, 256), BF16),
        vmem((ny, RANK, 128), F32),
        vmem((nz, OWN, 128), F32),
        vmem((nz, OWN, 128), F32),
        vmem((ny, OWN, 128), F32),
        vmem((nz, nxk, OWN, RANK), F32),
    ]
    sems = [pltpu.SemaphoreType.DMA((6,))]
    for count in (nz, 2, nx, 1, nz, ny, nx, nz, 1, ny, nz, ny, 4, 4, 4, 4):
        sems += [pltpu.SemaphoreType.DMA((count,))] * 2
    spec = pl.BlockSpec(memory_space=pltpu.VMEM)
    cor_shape = jax.ShapeDtypeStruct((nz, nxk, OWN, 128), F32)
    mids = (
        jax.ShapeDtypeStruct((7, 7, OWN), F32),
        jax.ShapeDtypeStruct((RANK, channels), F32),
        jax.ShapeDtypeStruct((RANK, 128), F32),
        jax.ShapeDtypeStruct((4 * RANK, 128), BF16),
        jax.ShapeDtypeStruct((channels, 4 * RANK), BF16),
        cor_shape,
    )
    parts = pl.pallas_call(
        functools.partial(kernel, ny, nz, nx),
        out_shape=mids,
        in_specs=[pl.BlockSpec(memory_space=pl.ANY)] * 6,
        out_specs=(spec,) * 6,
        scratch_shapes=scratch + sems,
        compiler_params=pltpu.CompilerParams(
            collective_id=0, has_side_effects=True, vmem_limit_bytes=60 * 1024 * 1024
        ),
        cost_estimate=pl.CostEstimate(
            flops=600_000_000, bytes_accessed=4_000_000, transcendentals=0
        ),
    )(
        block_input.reshape(SIDE, SIDE, OWN),
        depth_kernel,
        w_expand,
        grad_hidden.reshape(POS, 128),
        error_old.reshape(nz, nxk, OWN, 128),
        right_init.T,
    )
    kg, left, right, err = pl.pallas_call(
        finish,
        out_shape=mids[0:3] + (cor_shape,),
        in_specs=[spec] * 6,
        out_specs=(spec,) * 4,
        compiler_params=pltpu.CompilerParams(vmem_limit_bytes=60 * 1024 * 1024),
        cost_estimate=pl.CostEstimate(
            flops=60_000_000, bytes_accessed=2_500_000, transcendentals=0
        ),
    )(*parts)
    return (
        kg,
        left.T,
        right.T,
        err.reshape(1, channels, 128),
    )


def solution(mesh, nx=NX):
    ny = mesh.shape["outer"]
    nz = mesh.shape["chip"] // (2 * nx)
    placed = (
        P("outer", None, None, "chip"),
        P(),
        P(None, "chip"),
        P("outer", None, None, "chip"),
        P("outer", None, "chip"),
        P("chip", None),
    )
    return jax.shard_map(
        functools.partial(on_device, ny, nz, nx),
        mesh=mesh,
        in_specs=placed,
        out_specs=(P(None, None, "chip"), P(), P("chip", None), P("outer", None, "chip")),
        check_vma=False,
    )
```

```python
import functools

import jax
import jax.numpy as jnp
from jax import lax
from jax.experimental import pallas as pl
from jax.experimental.pallas import tpu as pltpu
from jax.sharding import PartitionSpec as P

F32 = jnp.float32
BF16 = jnp.bfloat16
HIGH = lax.Precision.HIGHEST
MESH = pl.DeviceIdType.MESH

NX = 4
SIDE = 24
POS = SIDE * SIDE
LP = 640
LX = 896
OWN = 24
RANK = 32


def dot(a, b, dims, precision=None):
    return lax.dot_general(a, b, (dims, ((), ())), precision=precision, preferred_element_type=F32)


NN = ((1,), (0,))
NT = ((1,), (1,))
TN = ((0,), (0,))


def loop(lo, hi, body, unroll=1):
    def step(i, carry):
        body(i)
        return carry

    lax.fori_loop(lo, hi, step, 0, unroll=unroll)


def split2(v):
    hi = v.astype(BF16)
    return hi, (v - hi.astype(F32)).astype(BF16)


def split3(v):
    hi = v.astype(BF16)
    rest = v - hi.astype(F32)
    mid = rest.astype(BF16)
    return hi, mid, (rest - mid.astype(F32)).astype(BF16)


def kernel(
    ny, nz, nx,
    x_hbm, k_hbm, w_hbm, gh_hbm, err_hbm, r_hbm,
    kg_out, left_out, right_out, w_out, ls4_out, cor_out,
    x_ref, k_ref, w_ref, err_ref, r_ref,
    ghp, ghs, ws, rs, wf, x2, xz, xp, xs, mk, kflat, kt, conv32, cvf, gr, gb, rh1, rh2, g32,
    eg, gg, es, cs, gt, st, rz, ys, ll, chl, rp, kgt, rk, yk, lsn, ls4, cor, left,
    s_in,
    s_xz, r_xz, s_es, r_es, s_cs, r_cs, s_gt, r_gt, s_rz, r_rz, s_ys, r_ys, s_lx, r_lx, s_lz, r_lz,
    s_lk, r_lk, s_rp, r_rp, s_rk, r_rk, s_yk, r_yk, s_in2, r_in2, s_gx, r_gx, s_cx, r_cx, s_cc, r_cc,
):
    nxk = 2 * nx
    ch = OWN * nz
    channels = ch * nxk
    tpz = 8 // nz
    half = ch // 2
    workers = ny
    y = lax.axis_index("outer")
    chip = lax.axis_index("chip")
    z = chip // nxk
    xk = lax.rem(chip, nxk)
    x = xk // 2
    k = lax.rem(xk, 2)

    def zpeer(s):
        return lax.rem(z + s, nz)

    def at_z(zz):
        return (y, zz * nxk + xk)

    def at_x(xx):
        return (y, z * nxk + xx * 2 + k)

    right_x = lax.rem(x + 1, nx)
    left_x = lax.rem(x + nx - 1, nx)
    far_x = lax.rem(x + 2, nx)

    def at_y(yy):
        return (yy, chip)

    sibling = (y, z * nxk + x * 2 + (1 - k))

    def copy(src, dst, ssem, rsem, dev):
        return pltpu.make_async_remote_copy(
            src_ref=src, dst_ref=dst, send_sem=ssem, recv_sem=rsem,
            device_id=dev, device_id_type=MESH,
        )

    load_x = pltpu.make_async_copy(x_hbm, x_ref, s_in.at[0])
    load_r = pltpu.make_async_copy(r_hbm, r_ref, s_in.at[1])
    load_err = pltpu.make_async_copy(err_hbm, err_ref, s_in.at[2])
    load_gh = pltpu.make_async_copy(gh_hbm, ghp.at[pl.ds(0, POS)], s_in.at[3])
    load_w = pltpu.make_async_copy(w_hbm, w_ref, s_in.at[4])
    load_k = pltpu.make_async_copy(k_hbm, k_ref, s_in.at[5])
    for load in (load_x, load_r, load_err, load_gh, load_w, load_k):
        load.start()

    barrier = pltpu.get_barrier_semaphore()

    def greet(dev):
        pl.semaphore_signal(barrier, inc=1, device_id=dev, device_id_type=MESH)

    loop(1, nz, lambda s: greet(at_z(zpeer(s))))
    loop(1, nx, lambda s: greet(at_x(lax.rem(x + s, nx))))
    greet(sibling)
    loop(1, ny, lambda s: greet(at_y(lax.rem(y + s, ny))))

    pl.semaphore_wait(barrier, (nz - 1) + (nx - 1) + (ny - 1) + 1)

    in_gh = copy(gh_hbm, ghs.at[pl.ds(0, POS)], s_in2.at[0], r_in2.at[0], sibling)
    in_r = copy(r_hbm, rs, s_in2.at[1], r_in2.at[1], sibling)
    in_w = copy(w_hbm, ws, s_in2.at[2], r_in2.at[2], sibling)
    for one in (in_r, in_gh, in_w):
        one.start()

    x2[...] = jnp.zeros((3, LX, OWN), F32)
    load_x.wait()
    for i in range(SIDE):
        image_row = x_ref[i].astype(F32)
        x2[0, SIDE * i : SIDE * (i + 1), :] = image_row
        late = i >= SIDE // 2
        at = POS + SIDE * (i % (SIDE // 2))
        x2[2 if late else 1, at : at + SIDE, :] = image_row
    out_row = lax.broadcasted_iota(jnp.int32, (16, OWN), 0)
    channel = lax.broadcasted_iota(jnp.int32, (16, OWN), 1)
    picks = (
        channel == out_row,
        (channel == out_row + 16) & (out_row < 8),
        (channel == out_row + 8) & (out_row >= 8),
    )
    packed = None
    for j in range(3):
        term = dot(picks[j].astype(F32).astype(BF16), x2[j].astype(BF16), NT)
        packed = term if packed is None else packed + term
    xz[z] = packed.astype(BF16)

    def xz_copy(s):
        return copy(xz.at[z], xz.at[z], s_xz.at[s], r_xz.at[s], at_z(zpeer(s)))

    loop(1, nz, lambda s: xz_copy(s).start())

    load_r.wait()
    load_err.wait()
    rh, rl = split2(r_ref[...])
    four = jnp.concatenate(
        [jnp.concatenate([rh, rh], axis=1), jnp.concatenate([rl, rl], axis=1)], axis=0
    )
    for q in range(nxk):
        eh, el = split2(err_ref[:, q].reshape(ch, 128))
        rows = jnp.concatenate([eh, el], axis=1)
        if ch < 256:
            rows = jnp.concatenate([rows, jnp.zeros((256 - ch, 256), BF16)], axis=0)
        e = dot(four, rows, NT)
        e = e[0:32] + e[32:64]
        for rg in range(4):
            for part in range(2):
                eg[q // 2, q % 2, 2 * rg + part] = e[8 * rg : 8 * rg + 8, 128 * part : 128 * part + 128]

    es_copy = copy(eg.at[:, 1 - k], es, s_es.at[0], r_es.at[0], sibling)
    es_copy.start()

    ghp[POS:, :] = jnp.zeros((LP - POS, 128), BF16)
    ghs[POS:, :] = jnp.zeros((LP - POS, 128), BF16)

    load_gh.wait()
    in_gh.wait_recv()
    in_r.wait_recv()
    sh, sl = split2(rs[...])
    both = jnp.concatenate([ghp[...], ghs[...]], axis=1)
    g = dot(
        jnp.concatenate([rh, sh, rl, sl], axis=1), jnp.concatenate([both, both], axis=1), NT
    )
    for rg in range(4):
        for j in range(5):
            gg[rg // 2, (rg % 2) * 5 + j] = g[8 * rg : 8 * rg + 8, 128 * j : 128 * j + 128]

    es_copy.wait_recv()

    def chip_sum(xx):
        cs[xx, 0, 0:8] = eg[xx, k] + es[xx]
        cs[xx, 0, 8:18] = gg[k]

    loop(0, nx, chip_sum)
    cs[x, 1] = cs[x, 0]

    def cs_copy(s):
        xx = lax.rem(x + s, nx)
        return copy(cs.at[xx, 0], cs.at[x, 1], s_cs.at[s], r_cs.at[s], at_x(xx))

    loop(1, nx, lambda s: cs_copy(s).start())

    load_w.wait()
    in_w.wait_recv()
    wf[:, :, :, :, 0:128] = w_ref[...].astype(F32).reshape(nz, nx, 2, OWN, 128)
    wf[:, :, :, :, 128:256] = ws[...].astype(F32).reshape(nz, nx, 2, OWN, 128)

    def grad_rows(xx):
        rows = wf[:, xx, k].reshape(ch, 256).astype(BF16)
        return dot(rows, jnp.concatenate([ghp[...], ghs[...]], axis=1), NT)

    gb[0] = grad_rows(far_x).astype(BF16)
    far_right = copy(
        gb.at[0, pl.ds(0, half)], rh1.at[0], s_gx.at[0], r_gx.at[0], at_x(right_x)
    )
    far_left = copy(
        gb.at[0, pl.ds(half, half)], rh1.at[1], s_gx.at[1], r_gx.at[1], at_x(left_x)
    )
    far_right.start()
    far_left.start()
    gr[0] = grad_rows(right_x)
    gr[1] = grad_rows(left_x)
    g32[...] = grad_rows(x)

    loop(1, nx, lambda s: cs_copy(s).wait_recv())
    total = cs[0, 1]
    for q in range(1, nx):
        total = total + cs[q, 1]
    st[...] = total[0:8]
    gt[k] = total[8:18]
    gt_copy = copy(gt.at[k], gt.at[k], s_gt.at[0], r_gt.at[0], sibling)
    gt_copy.start()

    load_k.wait()
    for a in range(7):
        kflat[8 * a : 8 * a + 7, :] = k_ref[a]
        kflat[8 * a + 7 : 8 * a + 8, :] = jnp.zeros((1, channels), F32)
    kflat[56:64, :] = jnp.zeros((8, channels), F32)
    row = lax.broadcasted_iota(jnp.int32, (OWN, channels), 0)
    lane = lax.broadcasted_iota(jnp.int32, (OWN, channels), 1)
    apart = lane - row - xk * OWN
    pick = jnp.concatenate([(apart == zz * nxk * OWN).astype(F32) for zz in range(nz)], axis=0)
    three = jnp.concatenate(split3(kflat[...]), axis=0)
    taps3 = dot(pick.astype(BF16), three, NT)
    kt[...] = taps3[:, 0:64] + taps3[:, 64:128] + taps3[:, 128:192]
    pos = lax.broadcasted_iota(jnp.int32, (8, LP), 1)
    col = lax.rem(pos, SIDE) + lax.broadcasted_iota(jnp.int32, (8, LP), 0) - 3
    mk[...] = ((col >= 0) & (col < SIDE) & (pos < POS)).astype(F32)
    xp[:, 0:128] = jnp.zeros((ch, 128), F32)
    xp[:, 128 + LP :] = jnp.zeros((ch, LX - 128 - LP), F32)

    loop(1, nz, lambda s: xz_copy(s).wait_recv())
    lane_x = lax.broadcasted_iota(jnp.int32, (16, LX), 1)
    for zz in range(nz):
        v = xz[zz].astype(F32)
        xp[OWN * zz : OWN * zz + 16, 128 : 128 + LP] = jnp.where(lane_x < POS, v, 0.0)[:, 0:LP]
        early = pltpu.roll(v[0:8], LX - POS, 1)
        late = pltpu.roll(v[8:16], LX - POS // 2, 1)
        last = jnp.where(
            lane_x[0:8] < POS // 2, early, jnp.where(lane_x[0:8] < POS, late, 0.0)
        )
        xp[OWN * zz + 16 : OWN * zz + 24, 128 : 128 + LP] = last[:, 0:LP]

    def conv_rows(t):
        rows = pl.ds(pl.multiple_of(t * 8, 8), 8)
        v = xp[rows, :]
        taps = kt[rows, :]
        moved = [pltpu.roll(v, LX - (96 + SIDE * (a - 3)), 1)[:, 0:LP] for a in range(7)]
        for a in range(7):
            xs[a, rows, :] = moved[a]
        out = None
        for b in range(7):
            part = None
            for a in range(7):
                term = taps[:, 8 * a + b : 8 * a + b + 1] * moved[a]
                part = term if a == 0 else part + term
            part = pltpu.roll(part, LP - (32 + b - 3), 1) * mk[b : b + 1, :]
            out = part if b == 0 else out + part
        conv32[rows, :] = out

    loop(0, ch // 8, conv_rows, 2)
    cvf[x, k] = conv32[...].astype(BF16)

    mine = cvf.at[x, k]
    cx_copies = [
        copy(mine, mine, s_cx.at[0], r_cx.at[0], at_x(right_x)),
        copy(mine, mine, s_cx.at[1], r_cx.at[1], at_x(left_x)),
    ]
    for s in range(2):
        cx_copies[s].start()

    sources = (x, left_x, right_x, far_x)

    def cc_copy(s):
        block = cvf.at[sources[s], k]
        return copy(block, block, s_cc.at[s], r_cc.at[s], sibling)

    cc_copy(0).start()

    gt_copy.wait_recv()
    groups = []
    for rg in range(4):
        groups.append(
            jnp.concatenate([gt[rg // 2, (rg % 2) * 5 + j] for j in range(5)], axis=1)
        )
    gsplit = jnp.concatenate(split2(jnp.concatenate(groups, axis=0)), axis=0)
    conv_pad = cvf[x, k]
    if ch < 256:
        conv_pad = jnp.concatenate([conv_pad, jnp.zeros((256 - ch, LP), BF16)], axis=0)
    conv_left = dot(gsplit, conv_pad, NT)
    conv_left = conv_left[0:32] + conv_left[32:64]
    for rg in range(4):
        for part in range(2):
            st[2 * rg + part] += conv_left[8 * rg : 8 * rg + 8, 128 * part : 128 * part + 128]

    def rz_copy(s):
        zz = zpeer(s)
        return copy(st.at[pl.ds(zz * tpz, tpz)], rz.at[z], s_rz.at[s], r_rz.at[s], at_z(zz))

    loop(1, nz, lambda s: rz_copy(s).start())
    rz[z] = st[pl.ds(z * tpz, tpz)]

    far_right.wait_recv()
    gb[1, 0:half, :] = (gr[0, 0:half, :] + rh1[0].astype(F32)).astype(BF16)
    gb[1, half:, :] = gr[0, half:, :].astype(BF16)
    near_right = copy(gb.at[1], rh2.at[0], s_gx.at[2], r_gx.at[2], at_x(right_x))
    near_right.start()
    far_left.wait_recv()
    gb[2, 0:half, :] = gr[1, 0:half, :].astype(BF16)
    gb[2, half:, :] = (gr[1, half:, :] + rh1[1].astype(F32)).astype(BF16)
    near_left = copy(gb.at[2], rh2.at[1], s_gx.at[3], r_gx.at[3], at_x(left_x))
    near_left.start()

    loop(1, nz, lambda s: rz_copy(s).wait_recv())
    total = rz[0]
    for q in range(1, nz):
        total = total + rz[q]
    ys[y] = total

    def ys_copy(s):
        return copy(ys.at[y], ys.at[y], s_ys.at[s], r_ys.at[s], at_y(lax.rem(y + s, ny)))

    loop(1, ny, lambda s: ys_copy(s).start())

    def local_grad(xx, kk):
        q = xx * 2 + kk
        part = dot(cvf[xx, kk], ghp[...], NN) + err_ref[:, q].reshape(ch, 128)
        cor[:, q] = part.reshape(nz, OWN, 128)
        chl[q, 0:ch, :] = jnp.concatenate(split2(part), axis=1)

    if ch < 256:
        chl[:, ch:, :] = jnp.zeros((nxk, 256 - ch, 256), BF16)
    loop(1, ny, lambda s: ys_copy(s).wait_recv())
    total = ys[0]
    for q in range(1, ny):
        total = total + ys[q]
    ll[k, z, x] = total

    def lx_copy(s):
        own = ll.at[k, z, x]
        return copy(own, own, s_lx.at[s], r_lx.at[s], at_x(lax.rem(x + s, nx)))

    loop(1, nx, lambda s: lx_copy(s).start())

    local_grad(x, k)
    def lx_wait(s):
        got = ll.at[k, z, lax.rem(x - s + nx, nx)]
        copy(got, got, s_lx.at[s], r_lx.at[s], at_x(lax.rem(x + s, nx))).wait_recv()

    loop(1, nx, lx_wait)

    def lz_copy(s):
        own = ll.at[k, z]
        return copy(own, own, s_lz.at[s], r_lz.at[s], at_z(zpeer(s)))

    loop(1, nz, lambda s: lz_copy(s).start())
    cx_copies[0].wait_recv()
    part0 = cvf.at[left_x, k, pl.ds(0, half)]
    cx_copies.append(copy(part0, part0, s_cx.at[2], r_cx.at[2], at_x(right_x)))
    cx_copies[2].start()
    cc_copy(1).start()
    cx_copies[1].wait_recv()
    part1 = cvf.at[right_x, k, pl.ds(half, half)]
    cx_copies.append(copy(part1, part1, s_cx.at[3], r_cx.at[3], at_x(left_x)))
    cx_copies[3].start()
    cc_copy(2).start()
    local_grad(left_x, k)
    local_grad(right_x, k)

    for s in range(3):
        cc_copy(s).wait_recv()
        local_grad(sources[s], 1 - k)

    def lz_wait(s):
        got = ll.at[k, lax.rem(z - s + nz, nz)]
        copy(got, got, s_lz.at[s], r_lz.at[s], at_z(zpeer(s))).wait_recv()

    loop(1, nz, lz_wait)
    lk_copy = copy(ll.at[k], ll.at[k], s_lk.at[0], r_lk.at[0], sibling)
    lk_copy.start()

    near_right.wait_recv()
    near_left.wait_recv()
    g32[...] += rh2[0].astype(F32) + rh2[1].astype(F32)
    lane128 = lax.broadcasted_iota(jnp.int32, (8, 128), 1)

    def kernel_terms(t):
        rows = pl.ds(pl.multiple_of(t * 8, 8), 8)
        gt = g32[rows, :]
        out = jnp.zeros((8, 128), F32)
        for b in range(7):
            gm = pltpu.roll(gt * mk[b : b + 1, :], 32 + b - 3, 1)
            for a in range(7):
                one = jnp.sum(gm * xs[a, rows, :], axis=1, keepdims=True)
                out = jnp.where(lane128 == 7 * a + b, one, out)
        kgt[t // 3, pl.ds(pl.multiple_of(lax.rem(t, 3) * 8, 8), 8), :] = out

    loop(0, ch // 8, kernel_terms, 2)

    def rk_copy(s):
        zz = zpeer(s)
        return copy(kgt.at[zz], rk.at[z], s_rk.at[s], r_rk.at[s], at_z(zz))

    loop(1, nz, lambda s: rk_copy(s).start())
    rk[z] = kgt[z]


    cx_copies[2].wait_recv()
    cx_copies[3].wait_recv()
    cc_copy(3).start()
    local_grad(far_x, k)
    cc_copy(3).wait_recv()
    local_grad(far_x, 1 - k)
    cor_store = pltpu.make_async_copy(cor, cor_out, s_in.at[6])
    cor_store.start()
    lk_copy.wait_recv()

    def left_of(q):
        rows = []
        for rg in range(4):
            tiles = [ll[q % 2, t // tpz, q // 2, t % tpz] for t in (2 * rg, 2 * rg + 1)]
            rows.append(jnp.concatenate(tiles, axis=1))
        return jnp.concatenate(rows, axis=0)

    lefts = [left_of(q) for q in range(nxk)]
    right = None
    for q in range(nxk):
        term = dot(jnp.concatenate(split2(lefts[q]), axis=0), chl[q], NN)
        right = term if q == 0 else right + term
    right = right[0:32] + right[32:64]
    rp[y] = right[:, 0:128] + right[:, 128:256]

    def rp_copy(s):
        return copy(rp.at[y], rp.at[y], s_rp.at[s], r_rp.at[s], at_y(lax.rem(y + s, ny)))

    loop(1, ny, lambda s: rp_copy(s).start())

    wide3 = split3(jnp.concatenate(lefts, axis=1))
    stack3 = jnp.concatenate(wide3, axis=0)
    gram = None
    for part in wide3:
        term = dot(stack3, part, NT)
        term = term[0:32] + term[32:64] + term[64:96]
        gram = term if gram is None else gram + term
    for q in range(nxk):
        lsn[:, q] = lefts[q].T[0:ch].reshape(nz, OWN, RANK)
    natural = lsn[...].reshape(channels, RANK).T
    nh, nm, nl = split3(natural)
    ls4[...] = jnp.concatenate([nh, nm, nh, nm], axis=0).T
    ls4_store = pltpu.make_async_copy(ls4, ls4_out, s_in.at[7])
    ls4_store.start()

    row_id = lax.broadcasted_iota(jnp.int32, (RANK, RANK), 0)
    lane_id = lax.broadcasted_iota(jnp.int32, (RANK, RANK), 1)
    same = row_id == lane_id
    aug = jnp.concatenate([gram, same.astype(F32)], axis=1)
    row_col = lax.broadcasted_iota(jnp.int32, (RANK, 2 * RANK), 0)

    def full(v):
        return jnp.broadcast_to(v, (RANK, 2 * RANK))

    for i in range(0, RANK, 2):
        c0 = full(aug[:, i : i + 1])
        c1 = full(aug[:, i + 1 : i + 2])
        r0 = full(aug[i : i + 1, :])
        r1 = full(aug[i + 1 : i + 2, :])
        p00 = full(c0[i : i + 1, :])
        p01 = full(c1[i : i + 1, :])
        p11 = full(c1[i + 1 : i + 2, :])
        inv = 1.0 / (p00 * p11 - p01 * p01)
        u0 = (p11 * c0 - p01 * c1) * inv
        u1 = (p00 * c1 - p01 * c0) * inv
        u0 = jnp.where(row_col > i + 1, u0, jnp.where(row_col == i + 1, p01 / p00, 0.0))
        u1 = jnp.where(row_col > i + 1, u1, 0.0)
        aug = aug - u0 * r0 - u1 * r1
    diag = jnp.sum(jnp.where(same, aug[:, 0:RANK], 0.0), axis=1, keepdims=True)
    scale = lax.rsqrt(diag)
    scale = scale * (1.5 - 0.5 * diag * scale * scale)
    linv = aug[:, RANK:] * scale
    ih, im, il = split3(linv)
    left[...] = dot(
        jnp.concatenate([ih, ih, ih, im, im, il], axis=1),
        jnp.concatenate([nh, nm, nl, nh, nm, nh], axis=0),
        NN,
    )
    left_store = pltpu.make_async_copy(left, left_out, s_in.at[8])
    left_store.start()

    loop(1, nz, lambda s: rk_copy(s).wait_recv())
    total = rk[0]
    for q in range(1, nz):
        total = total + rk[q]
    yk[y] = total

    def yk_copy(s):
        return copy(yk.at[y], yk.at[y], s_yk.at[s], r_yk.at[s], at_y(lax.rem(y + s, ny)))

    loop(1, ny, lambda s: yk_copy(s).start())

    loop(1, ny, lambda s: rp_copy(s).wait_recv())
    total = rp[0]
    for q in range(1, ny):
        total = total + rp[q]
    fright = dot(linv, total, NN, HIGH)
    right_out[...] = fright
    wh, wl = split2(dot(linv.T, fright, NN, HIGH) * (1.0 / workers))
    w_out[...] = jnp.concatenate([wh, wh, wl, wl], axis=0)

    loop(1, ny, lambda s: yk_copy(s).wait_recv())
    total = yk[0]
    for q in range(1, ny):
        total = total + yk[q]
    total = total.T
    for a in range(7):
        kg_out[a] = total[7 * a : 7 * a + 7]

    for one in (cor_store, ls4_store, left_store):
        one.wait()
    loop(1, nz, lambda s: xz_copy(s).wait_send())
    es_copy.wait_send()
    for one in (in_r, in_gh, in_w):
        one.wait_send()
    loop(1, nx, lambda s: cs_copy(s).wait_send())
    gt_copy.wait_send()
    loop(1, nz, lambda s: rz_copy(s).wait_send())
    loop(1, ny, lambda s: ys_copy(s).wait_send())
    loop(1, nx, lambda s: lx_copy(s).wait_send())
    loop(1, nz, lambda s: lz_copy(s).wait_send())
    lk_copy.wait_send()
    loop(1, ny, lambda s: rp_copy(s).wait_send())
    loop(1, nz, lambda s: rk_copy(s).wait_send())
    loop(1, ny, lambda s: yk_copy(s).wait_send())
    for s in range(4):
        cx_copies[s].wait_send()
        cc_copy(s).wait_send()
    for one in (far_right, far_left, near_right, near_left):
        one.wait_send()


def finish(kg_ref, left_ref, right_ref, w_ref, ls_ref, cor_ref, kg_out, left_out, right_out, err_out):
    kg_out[...] = kg_ref[...]
    left_out[...] = left_ref[...]
    right_out[...] = right_ref[...]
    approx = dot(ls_ref[...], w_ref[...], NN)
    err_out[...] = cor_ref[...] - approx.reshape(cor_ref.shape)


def on_device(ny, nz, nx, block_input, depth_kernel, w_expand, grad_hidden, error_old, right_init):
    nxk = 2 * nx
    ch = OWN * nz
    channels = nz * nxk * OWN
    tpz = 8 // nz
    hid = right_init.shape[0]
    vmem = pltpu.VMEM
    scratch = [
        vmem((SIDE, SIDE, OWN), BF16),
        vmem((7, 7, channels), F32),
        vmem((channels, 128), BF16),
        vmem((nz, nxk, OWN, 128), F32),
        vmem((RANK, 128), F32),
        vmem((LP, 128), BF16),
        vmem((LP, 128), BF16),
        vmem((channels, 128), BF16),
        vmem((RANK, 128), F32),
        vmem((nz, nx, 2, OWN, 256), F32),
        vmem((3, LX, OWN), F32),
        vmem((nz, 16, LX), BF16),
        vmem((ch, LX), F32),
        vmem((7, ch, LP), F32),
        vmem((8, LP), F32),
        vmem((64, channels), F32),
        vmem((ch, 64), F32),
        vmem((ch, LP), F32),
        vmem((nx, 2, ch, LP), BF16),
        vmem((2, ch, LP), F32),
        vmem((3, ch, LP), BF16),
        vmem((2, ch // 2, LP), BF16),
        vmem((2, ch, LP), BF16),
        vmem((ch, LP), F32),
        vmem((nx, 2, 8, 8, 128), F32),
        vmem((2, 10, 8, 128), F32),
        vmem((nx, 8, 8, 128), F32),
        vmem((nx, 2, 18, 8, 128), F32),
        vmem((2, 10, 8, 128), F32),
        vmem((8, 8, 128), F32),
        vmem((nz, tpz, 8, 128), F32),
        vmem((ny, tpz, 8, 128), F32),
        vmem((2, nz, nx, tpz, 8, 128), F32),
        vmem((nxk, 256, 256), BF16),
        vmem((ny, RANK, 128), F32),
        vmem((nz, OWN, 128), F32),
        vmem((nz, OWN, 128), F32),
        vmem((ny, OWN, 128), F32),
        vmem((nz, nxk, OWN, RANK), F32),
        vmem((channels, 4 * RANK), BF16),
        vmem((nz, nxk, OWN, 128), F32),
        vmem((RANK, channels), F32),
    ]
    sems = [pltpu.SemaphoreType.DMA((9,))]
    for count in (nz, 2, nx, 1, nz, ny, nx, nz, 1, ny, nz, ny, 4, 4, 4, 4):
        sems += [pltpu.SemaphoreType.DMA((count,))] * 2
    spec = pl.BlockSpec(memory_space=pltpu.VMEM)
    far = pl.BlockSpec(memory_space=pl.ANY)
    cor_shape = jax.ShapeDtypeStruct((nz, nxk, OWN, 128), F32)
    mids = (
        jax.ShapeDtypeStruct((7, 7, OWN), F32),
        jax.ShapeDtypeStruct((RANK, channels), F32),
        jax.ShapeDtypeStruct((RANK, 128), F32),
        jax.ShapeDtypeStruct((4 * RANK, 128), BF16),
        jax.ShapeDtypeStruct((channels, 4 * RANK), BF16),
        cor_shape,
    )
    parts = pl.pallas_call(
        functools.partial(kernel, ny, nz, nx),
        out_shape=mids,
        in_specs=[pl.BlockSpec(memory_space=pl.ANY)] * 6,
        out_specs=(spec, far, spec, spec, far, far),
        scratch_shapes=scratch + sems,
        compiler_params=pltpu.CompilerParams(
            collective_id=0, has_side_effects=True, vmem_limit_bytes=60 * 1024 * 1024
        ),
        cost_estimate=pl.CostEstimate(
            flops=600_000_000, bytes_accessed=4_000_000, transcendentals=0
        ),
    )(
        block_input.reshape(SIDE, SIDE, OWN),
        depth_kernel,
        w_expand,
        grad_hidden.reshape(POS, 128),
        error_old.reshape(nz, nxk, OWN, 128),
        right_init.T,
    )
    steps = min(4, nz)

    def whole(shape):
        return pl.BlockSpec(shape, lambda i: (0,) * len(shape))

    rows = pl.BlockSpec((nz // steps, nxk, OWN, 128), lambda i: (i, 0, 0, 0))
    small = [whole((7, 7, OWN)), whole((RANK, channels)), whole((RANK, 128))]
    kg, left, right, err = pl.pallas_call(
        finish,
        grid=(steps,),
        out_shape=mids[0:3] + (cor_shape,),
        in_specs=small
        + [
            whole((4 * RANK, 128)),
            pl.BlockSpec((channels // steps, 4 * RANK), lambda i: (i, 0)),
            rows,
        ],
        out_specs=tuple(small) + (rows,),
        compiler_params=pltpu.CompilerParams(vmem_limit_bytes=60 * 1024 * 1024),
        cost_estimate=pl.CostEstimate(
            flops=60_000_000, bytes_accessed=2_500_000, transcendentals=0
        ),
    )(*parts)
    return (
        kg,
        left.T,
        right.T,
        err.reshape(1, channels, 128),
    )


def solution(mesh, nx=NX):
    ny = mesh.shape["outer"]
    nz = mesh.shape["chip"] // (2 * nx)
    placed = (
        P("outer", None, None, "chip"),
        P(),
        P(None, "chip"),
        P("outer", None, None, "chip"),
        P("outer", None, "chip"),
        P("chip", None),
    )
    return jax.shard_map(
        functools.partial(on_device, ny, nz, nx),
        mesh=mesh,
        in_specs=placed,
        out_specs=(P(None, None, "chip"), P(), P("chip", None), P("outer", None, "chip")),
        check_vma=False,
    )
```

```python
import functools

import jax
import jax.numpy as jnp
from jax import lax
from jax.experimental import pallas as pl
from jax.experimental.pallas import tpu as pltpu
from jax.sharding import PartitionSpec as P

F32 = jnp.float32
BF16 = jnp.bfloat16
HIGH = lax.Precision.HIGHEST
MESH = pl.DeviceIdType.MESH

NX = 4
SIDE = 24
POS = SIDE * SIDE
LP = 640
LX = 896
OWN = 24
RANK = 32


def dot(a, b, dims, precision=None):
    return lax.dot_general(a, b, (dims, ((), ())), precision=precision, preferred_element_type=F32)


NN = ((1,), (0,))
NT = ((1,), (1,))
TN = ((0,), (0,))


def loop(lo, hi, body, unroll=1):
    def step(i, carry):
        body(i)
        return carry

    lax.fori_loop(lo, hi, step, 0, unroll=unroll)


def split2(v):
    hi = v.astype(BF16)
    return hi, (v - hi.astype(F32)).astype(BF16)


def split3(v):
    hi = v.astype(BF16)
    rest = v - hi.astype(F32)
    mid = rest.astype(BF16)
    return hi, mid, (rest - mid.astype(F32)).astype(BF16)


def kernel(
    ny, nz, nx,
    x_hbm, k_hbm, w_hbm, gh_hbm, err_hbm, r_hbm,
    kg_out, left_out, right_out, w_out, ls4_out, cor_out,
    x_ref, k_ref, w_ref, err_ref, r_ref,
    ghp, ghs, ws, rs, wf, x2, xo, conv24, cz, xz, xp, mk, kflat, kt, conv32, cvf, gr, gb, rh1, rh2, g32,
    eg, gg, es, cs, gt, st, rz, ys, ll, chl, rp, kgt, rk, yk, lsn, ls4, cor, left,
    s_in,
    s_cz, r_cz, s_xz, r_xz, s_es, r_es, s_cs, r_cs, s_gt, r_gt, s_rz, r_rz, s_ys, r_ys, s_lx, r_lx, s_lz, r_lz,
    s_lk, r_lk, s_rp, r_rp, s_rk, r_rk, s_yk, r_yk, s_in2, r_in2, s_gx, r_gx, s_cx, r_cx, s_cc, r_cc,
):
    nxk = 2 * nx
    ch = OWN * nz
    channels = ch * nxk
    tpz = 8 // nz
    half = ch // 2
    workers = ny
    y = lax.axis_index("outer")
    chip = lax.axis_index("chip")
    z = chip // nxk
    xk = lax.rem(chip, nxk)
    x = xk // 2
    k = lax.rem(xk, 2)

    def zpeer(s):
        return lax.rem(z + s, nz)

    def at_z(zz):
        return (y, zz * nxk + xk)

    def at_x(xx):
        return (y, z * nxk + xx * 2 + k)

    right_x = lax.rem(x + 1, nx)
    left_x = lax.rem(x + nx - 1, nx)
    far_x = lax.rem(x + 2, nx)

    def at_y(yy):
        return (yy, chip)

    sibling = (y, z * nxk + x * 2 + (1 - k))

    def copy(src, dst, ssem, rsem, dev):
        return pltpu.make_async_remote_copy(
            src_ref=src, dst_ref=dst, send_sem=ssem, recv_sem=rsem,
            device_id=dev, device_id_type=MESH,
        )

    load_x = pltpu.make_async_copy(x_hbm, x_ref, s_in.at[0])
    load_r = pltpu.make_async_copy(r_hbm, r_ref, s_in.at[1])
    load_err = pltpu.make_async_copy(err_hbm, err_ref, s_in.at[2])
    load_gh = pltpu.make_async_copy(gh_hbm, ghp.at[pl.ds(0, POS)], s_in.at[3])
    load_w = pltpu.make_async_copy(w_hbm, w_ref, s_in.at[4])
    load_k = pltpu.make_async_copy(k_hbm, k_ref, s_in.at[5])
    for load in (load_x, load_r, load_err, load_gh, load_w, load_k):
        load.start()

    barrier = pltpu.get_barrier_semaphore()

    def greet(dev):
        pl.semaphore_signal(barrier, inc=1, device_id=dev, device_id_type=MESH)

    loop(1, nz, lambda s: greet(at_z(zpeer(s))))
    loop(1, nx, lambda s: greet(at_x(lax.rem(x + s, nx))))
    greet(sibling)
    loop(1, ny, lambda s: greet(at_y(lax.rem(y + s, ny))))

    pl.semaphore_wait(barrier, (nz - 1) + (nx - 1) + (ny - 1) + 1)

    in_gh = copy(gh_hbm, ghs.at[pl.ds(0, POS)], s_in2.at[0], r_in2.at[0], sibling)
    in_r = copy(r_hbm, rs, s_in2.at[1], r_in2.at[1], sibling)
    in_w = copy(w_hbm, ws, s_in2.at[2], r_in2.at[2], sibling)
    for one in (in_r, in_gh, in_w):
        one.start()

    x2[POS:, :] = jnp.zeros((LP - POS, OWN), F32)
    load_x.wait()
    for i in range(SIDE):
        x2[SIDE * i : SIDE * (i + 1), :] = x_ref[i].astype(F32)
    eye = (
        lax.broadcasted_iota(jnp.int32, (32, OWN), 0)
        == lax.broadcasted_iota(jnp.int32, (32, OWN), 1)
    )
    own = dot(eye.astype(F32).astype(BF16), x2[...].astype(BF16), NT)[0:OWN]
    xo[:, 0:128] = jnp.zeros((OWN, 128), F32)
    xo[:, 128 : 128 + LP] = own
    xo[:, 128 + LP :] = jnp.zeros((OWN, LX - 128 - LP), F32)
    load_k.wait()
    for a in range(7):
        kflat[8 * a : 8 * a + 7, :] = k_ref[a]
        kflat[8 * a + 7 : 8 * a + 8, :] = jnp.zeros((1, channels), F32)
    kflat[56:64, :] = jnp.zeros((8, channels), F32)
    row = lax.broadcasted_iota(jnp.int32, (OWN, channels), 0)
    lane = lax.broadcasted_iota(jnp.int32, (OWN, channels), 1)
    pick = (lane - row == chip * OWN).astype(F32).astype(BF16)
    three = jnp.concatenate(split3(kflat[...]), axis=0)
    taps3 = dot(pick, three, NT)
    kt[...] = taps3[:, 0:64] + taps3[:, 64:128] + taps3[:, 128:192]
    pos = lax.broadcasted_iota(jnp.int32, (8, LP), 1)
    col = lax.rem(pos, SIDE) + lax.broadcasted_iota(jnp.int32, (8, LP), 0) - 3
    mk[...] = ((col >= 0) & (col < SIDE) & (pos < POS)).astype(F32)

    def shifted(v):
        return [pltpu.roll(v, LX - (96 + SIDE * (a - 3)), 1)[:, 0:LP] for a in range(7)]

    for t in range(OWN // 8):
        rows = slice(8 * t, 8 * t + 8)
        taps = kt[rows, :]
        moved = shifted(xo[rows, :])
        out = None
        for b in range(7):
            part = None
            for a in range(7):
                term = taps[:, 8 * a + b : 8 * a + b + 1] * moved[a]
                part = term if a == 0 else part + term
            part = pltpu.roll(part, LP - (32 + b - 3), 1) * mk[b : b + 1, :]
            out = part if b == 0 else out + part
        conv24[rows, :] = out

    lane_x = lax.broadcasted_iota(jnp.int32, (16, LX), 1)

    def pack(v):
        wide = jnp.concatenate([v, jnp.zeros((OWN, LX - LP), F32)], axis=1)
        last = wide[16:24]
        early = jnp.where(lane_x[0:8] < POS // 2, last, 0.0)
        late = jnp.where(lane_x[0:8] < POS // 2, 0.0, last)
        tail = jnp.concatenate(
            [pltpu.roll(early, POS, 1), pltpu.roll(late, POS // 2, 1)], axis=0
        )
        return (wide[0:16] + tail).astype(BF16)

    def unpack(v):
        v = v.astype(F32)
        early = pltpu.roll(v[0:8], LX - POS, 1)
        late = pltpu.roll(v[8:16], LX - POS // 2, 1)
        last = jnp.where(
            lane_x[0:8] < POS // 2, early, jnp.where(lane_x[0:8] < POS, late, 0.0)
        )
        return jnp.where(lane_x < POS, v, 0.0)[:, 0:LP], last[:, 0:LP]

    cz[z] = pack(conv24[...])

    def cz_copy(s):
        return copy(cz.at[z], cz.at[z], s_cz.at[s], r_cz.at[s], at_z(zpeer(s)))

    loop(1, nz, lambda s: cz_copy(s).start())
    xz[z] = pack(own)

    def xz_copy(s):
        return copy(xz.at[z], xz.at[z], s_xz.at[s], r_xz.at[s], at_z(zpeer(s)))

    loop(1, nz, lambda s: xz_copy(s).start())

    load_r.wait()
    load_err.wait()
    rh, rl = split2(r_ref[...])
    four = jnp.concatenate(
        [jnp.concatenate([rh, rh], axis=1), jnp.concatenate([rl, rl], axis=1)], axis=0
    )
    for q in range(nxk):
        eh, el = split2(err_ref[:, q].reshape(ch, 128))
        rows = jnp.concatenate([eh, el], axis=1)
        if ch < 256:
            rows = jnp.concatenate([rows, jnp.zeros((256 - ch, 256), BF16)], axis=0)
        e = dot(four, rows, NT)
        e = e[0:32] + e[32:64]
        for rg in range(4):
            for part in range(2):
                eg[q // 2, q % 2, 2 * rg + part] = e[8 * rg : 8 * rg + 8, 128 * part : 128 * part + 128]

    es_copy = copy(eg.at[:, 1 - k], es, s_es.at[0], r_es.at[0], sibling)
    es_copy.start()

    ghp[POS:, :] = jnp.zeros((LP - POS, 128), BF16)
    ghs[POS:, :] = jnp.zeros((LP - POS, 128), BF16)

    load_gh.wait()
    in_gh.wait_recv()
    in_r.wait_recv()
    sh, sl = split2(rs[...])
    both = jnp.concatenate([ghp[...], ghs[...]], axis=1)
    g = dot(
        jnp.concatenate([rh, sh, rl, sl], axis=1), jnp.concatenate([both, both], axis=1), NT
    )
    for rg in range(4):
        for j in range(5):
            gg[rg // 2, (rg % 2) * 5 + j] = g[8 * rg : 8 * rg + 8, 128 * j : 128 * j + 128]

    es_copy.wait_recv()

    def chip_sum(xx):
        cs[xx, 0, 0:8] = eg[xx, k] + es[xx]
        cs[xx, 0, 8:18] = gg[k]

    loop(0, nx, chip_sum)
    cs[x, 1] = cs[x, 0]

    def cs_copy(s):
        xx = lax.rem(x + s, nx)
        return copy(cs.at[xx, 0], cs.at[x, 1], s_cs.at[s], r_cs.at[s], at_x(xx))

    loop(1, nx, lambda s: cs_copy(s).start())

    load_w.wait()
    in_w.wait_recv()
    wf[:, :, :, :, 0:128] = w_ref[...].astype(F32).reshape(nz, nx, 2, OWN, 128)
    wf[:, :, :, :, 128:256] = ws[...].astype(F32).reshape(nz, nx, 2, OWN, 128)

    def grad_rows(xx):
        rows = wf[:, xx, k].reshape(ch, 256).astype(BF16)
        return dot(rows, jnp.concatenate([ghp[...], ghs[...]], axis=1), NT)

    gb[0] = grad_rows(far_x).astype(BF16)
    far_right = copy(
        gb.at[0, pl.ds(0, half)], rh1.at[0], s_gx.at[0], r_gx.at[0], at_x(right_x)
    )
    far_left = copy(
        gb.at[0, pl.ds(half, half)], rh1.at[1], s_gx.at[1], r_gx.at[1], at_x(left_x)
    )
    far_right.start()
    far_left.start()
    gr[0] = grad_rows(right_x)
    gr[1] = grad_rows(left_x)
    g32[...] = grad_rows(x)

    loop(1, nx, lambda s: cs_copy(s).wait_recv())
    total = cs[0, 1]
    for q in range(1, nx):
        total = total + cs[q, 1]
    st[...] = total[0:8]
    gt[k] = total[8:18]
    gt_copy = copy(gt.at[k], gt.at[k], s_gt.at[0], r_gt.at[0], sibling)
    gt_copy.start()

    loop(1, nz, lambda s: cz_copy(s).wait_recv())
    for zz in range(nz):
        first, last = unpack(cz[zz])
        conv32[OWN * zz : OWN * zz + 16, :] = first
        conv32[OWN * zz + 16 : OWN * zz + 24, :] = last
    cvf[x, k] = conv32[...].astype(BF16)

    mine = cvf.at[x, k]
    cx_copies = [
        copy(mine, mine, s_cx.at[0], r_cx.at[0], at_x(right_x)),
        copy(mine, mine, s_cx.at[1], r_cx.at[1], at_x(left_x)),
    ]
    for s in range(2):
        cx_copies[s].start()

    sources = (x, left_x, right_x, far_x)

    def cc_copy(s):
        block = cvf.at[sources[s], k]
        return copy(block, block, s_cc.at[s], r_cc.at[s], sibling)

    cc_copy(0).start()

    gt_copy.wait_recv()
    groups = []
    for rg in range(4):
        groups.append(
            jnp.concatenate([gt[rg // 2, (rg % 2) * 5 + j] for j in range(5)], axis=1)
        )
    gsplit = jnp.concatenate(split2(jnp.concatenate(groups, axis=0)), axis=0)
    conv_pad = cvf[x, k]
    if ch < 256:
        conv_pad = jnp.concatenate([conv_pad, jnp.zeros((256 - ch, LP), BF16)], axis=0)
    conv_left = dot(gsplit, conv_pad, NT)
    conv_left = conv_left[0:32] + conv_left[32:64]
    for rg in range(4):
        for part in range(2):
            st[2 * rg + part] += conv_left[8 * rg : 8 * rg + 8, 128 * part : 128 * part + 128]

    def rz_copy(s):
        zz = zpeer(s)
        return copy(st.at[pl.ds(zz * tpz, tpz)], rz.at[z], s_rz.at[s], r_rz.at[s], at_z(zz))

    loop(1, nz, lambda s: rz_copy(s).start())
    rz[z] = st[pl.ds(z * tpz, tpz)]

    far_right.wait_recv()
    gb[1, 0:half, :] = (gr[0, 0:half, :] + rh1[0].astype(F32)).astype(BF16)
    gb[1, half:, :] = gr[0, half:, :].astype(BF16)
    near_right = copy(gb.at[1], rh2.at[0], s_gx.at[2], r_gx.at[2], at_x(right_x))
    near_right.start()
    far_left.wait_recv()
    gb[2, 0:half, :] = gr[1, 0:half, :].astype(BF16)
    gb[2, half:, :] = (gr[1, half:, :] + rh1[1].astype(F32)).astype(BF16)
    near_left = copy(gb.at[2], rh2.at[1], s_gx.at[3], r_gx.at[3], at_x(left_x))
    near_left.start()

    loop(1, nz, lambda s: rz_copy(s).wait_recv())
    total = rz[0]
    for q in range(1, nz):
        total = total + rz[q]
    ys[y] = total

    def ys_copy(s):
        return copy(ys.at[y], ys.at[y], s_ys.at[s], r_ys.at[s], at_y(lax.rem(y + s, ny)))

    loop(1, ny, lambda s: ys_copy(s).start())

    def local_grad(xx, kk):
        q = xx * 2 + kk
        part = dot(cvf[xx, kk], ghp[...], NN) + err_ref[:, q].reshape(ch, 128)
        cor[:, q] = part.reshape(nz, OWN, 128)
        chl[q, 0:ch, :] = jnp.concatenate(split2(part), axis=1)

    if ch < 256:
        chl[:, ch:, :] = jnp.zeros((nxk, 256 - ch, 256), BF16)
    loop(1, ny, lambda s: ys_copy(s).wait_recv())
    total = ys[0]
    for q in range(1, ny):
        total = total + ys[q]
    ll[k, z, x] = total

    def lx_copy(s):
        own = ll.at[k, z, x]
        return copy(own, own, s_lx.at[s], r_lx.at[s], at_x(lax.rem(x + s, nx)))

    loop(1, nx, lambda s: lx_copy(s).start())

    local_grad(x, k)
    def lx_wait(s):
        got = ll.at[k, z, lax.rem(x - s + nx, nx)]
        copy(got, got, s_lx.at[s], r_lx.at[s], at_x(lax.rem(x + s, nx))).wait_recv()

    loop(1, nx, lx_wait)

    def lz_copy(s):
        own = ll.at[k, z]
        return copy(own, own, s_lz.at[s], r_lz.at[s], at_z(zpeer(s)))

    loop(1, nz, lambda s: lz_copy(s).start())
    cx_copies[0].wait_recv()
    part0 = cvf.at[left_x, k, pl.ds(0, half)]
    cx_copies.append(copy(part0, part0, s_cx.at[2], r_cx.at[2], at_x(right_x)))
    cx_copies[2].start()
    cc_copy(1).start()
    cx_copies[1].wait_recv()
    part1 = cvf.at[right_x, k, pl.ds(half, half)]
    cx_copies.append(copy(part1, part1, s_cx.at[3], r_cx.at[3], at_x(left_x)))
    cx_copies[3].start()
    cc_copy(2).start()
    local_grad(left_x, k)
    local_grad(right_x, k)

    for s in range(3):
        cc_copy(s).wait_recv()
        local_grad(sources[s], 1 - k)

    def lz_wait(s):
        got = ll.at[k, lax.rem(z - s + nz, nz)]
        copy(got, got, s_lz.at[s], r_lz.at[s], at_z(zpeer(s))).wait_recv()

    loop(1, nz, lz_wait)
    lk_copy = copy(ll.at[k], ll.at[k], s_lk.at[0], r_lk.at[0], sibling)
    lk_copy.start()

    cx_copies[2].wait_recv()
    cx_copies[3].wait_recv()
    cc_copy(3).start()
    local_grad(far_x, k)

    loop(1, nz, lambda s: xz_copy(s).wait_recv())
    xp[:, 0:128] = jnp.zeros((ch, 128), F32)
    xp[:, 128 + LP :] = jnp.zeros((ch, LX - 128 - LP), F32)
    for zz in range(nz):
        first, last = unpack(xz[zz])
        xp[OWN * zz : OWN * zz + 16, 128 : 128 + LP] = first
        xp[OWN * zz + 16 : OWN * zz + 24, 128 : 128 + LP] = last
    near_right.wait_recv()
    near_left.wait_recv()
    g32[...] += rh2[0].astype(F32) + rh2[1].astype(F32)
    pair_row = lax.broadcasted_iota(jnp.int32, (OWN, 7 * OWN), 0)
    pair_lane = lax.broadcasted_iota(jnp.int32, (OWN, 7 * OWN), 1)
    diagonal = lax.rem(pair_lane, OWN) == pair_row
    tap_row = lax.broadcasted_iota(jnp.int32, (8, 7 * OWN), 0)

    def kernel_terms(zz):
        rows = pl.ds(pl.multiple_of(zz * OWN, 8), OWN)
        maps = jnp.concatenate(shifted(xp[rows, :]), axis=0).astype(BF16)
        gt = g32[rows, :]
        moved = [pltpu.roll(gt * mk[b : b + 1, :], 32 + b - 3, 1) for b in range(7)]
        hi, lo = split2(jnp.concatenate(moved, axis=0))
        pairs = dot(hi, maps, NT) + dot(lo, maps, NT)
        out = jnp.zeros((8, 7 * OWN), F32)
        for b in range(7):
            block = jnp.where(diagonal, pairs[OWN * b : OWN * (b + 1)], 0.0)
            one = jnp.sum(block, axis=0, keepdims=True)
            out = jnp.where(tap_row == b, one, out)
        kgt[zz] = jnp.concatenate([out, jnp.zeros((8, 256 - 7 * OWN), F32)], axis=1)

    loop(0, nz, kernel_terms, 2)

    def rk_copy(s):
        zz = zpeer(s)
        return copy(kgt.at[zz], rk.at[z], s_rk.at[s], r_rk.at[s], at_z(zz))

    loop(1, nz, lambda s: rk_copy(s).start())
    rk[z] = kgt[z]


    lk_copy.wait_recv()

    def left_of(q):
        rows = []
        for rg in range(4):
            tiles = [ll[q % 2, t // tpz, q // 2, t % tpz] for t in (2 * rg, 2 * rg + 1)]
            rows.append(jnp.concatenate(tiles, axis=1))
        return jnp.concatenate(rows, axis=0)

    lefts = [left_of(q) for q in range(nxk)]
    wide3 = split3(jnp.concatenate(lefts, axis=1))
    stack3 = jnp.concatenate(wide3, axis=0)
    gram = None
    for part in wide3:
        term = dot(stack3, part, NT)
        term = term[0:32] + term[32:64] + term[64:96]
        gram = term if gram is None else gram + term
    for q in range(nxk):
        lsn[:, q] = lefts[q].T[0:ch].reshape(nz, OWN, RANK)
    natural = lsn[...].reshape(channels, RANK).T
    nh, nm, nl = split3(natural)
    ls4[...] = jnp.concatenate([nh, nm, nh, nm], axis=0).T
    ls4_store = pltpu.make_async_copy(ls4, ls4_out, s_in.at[7])
    ls4_store.start()

    cc_copy(3).wait_recv()
    local_grad(far_x, 1 - k)
    cor_store = pltpu.make_async_copy(cor, cor_out, s_in.at[6])
    cor_store.start()

    right = None
    for q in range(nxk):
        term = dot(jnp.concatenate(split2(lefts[q]), axis=0), chl[q], NN)
        right = term if q == 0 else right + term
    right = right[0:32] + right[32:64]
    rp[y] = right[:, 0:128] + right[:, 128:256]

    def rp_copy(s):
        return copy(rp.at[y], rp.at[y], s_rp.at[s], r_rp.at[s], at_y(lax.rem(y + s, ny)))

    loop(1, ny, lambda s: rp_copy(s).start())

    row_id = lax.broadcasted_iota(jnp.int32, (RANK, RANK), 0)
    lane_id = lax.broadcasted_iota(jnp.int32, (RANK, RANK), 1)
    same = row_id == lane_id
    aug = jnp.concatenate([gram, same.astype(F32)], axis=1)
    row_col = lax.broadcasted_iota(jnp.int32, (RANK, 2 * RANK), 0)

    def full(v):
        return jnp.broadcast_to(v, (RANK, 2 * RANK))

    for i in range(0, RANK, 2):
        c0 = full(aug[:, i : i + 1])
        c1 = full(aug[:, i + 1 : i + 2])
        r0 = full(aug[i : i + 1, :])
        r1 = full(aug[i + 1 : i + 2, :])
        p00 = full(c0[i : i + 1, :])
        p01 = full(c1[i : i + 1, :])
        p11 = full(c1[i + 1 : i + 2, :])
        inv = 1.0 / (p00 * p11 - p01 * p01)
        u0 = (p11 * c0 - p01 * c1) * inv
        u1 = (p00 * c1 - p01 * c0) * inv
        u0 = jnp.where(row_col > i + 1, u0, jnp.where(row_col == i + 1, p01 / p00, 0.0))
        u1 = jnp.where(row_col > i + 1, u1, 0.0)
        aug = aug - u0 * r0 - u1 * r1
    diag = jnp.sum(jnp.where(same, aug[:, 0:RANK], 0.0), axis=1, keepdims=True)
    scale = lax.rsqrt(diag)
    scale = scale * (1.5 - 0.5 * diag * scale * scale)
    linv = aug[:, RANK:] * scale
    ih, im, il = split3(linv)
    left[...] = dot(
        jnp.concatenate([ih, ih, ih, im, im, il], axis=1),
        jnp.concatenate([nh, nm, nl, nh, nm, nh], axis=0),
        NN,
    )
    left_store = pltpu.make_async_copy(left, left_out, s_in.at[8])
    left_store.start()

    loop(1, nz, lambda s: rk_copy(s).wait_recv())
    total = rk[0]
    for q in range(1, nz):
        total = total + rk[q]
    yk[y] = total

    def yk_copy(s):
        return copy(yk.at[y], yk.at[y], s_yk.at[s], r_yk.at[s], at_y(lax.rem(y + s, ny)))

    loop(1, ny, lambda s: yk_copy(s).start())

    loop(1, ny, lambda s: rp_copy(s).wait_recv())
    total = rp[0]
    for q in range(1, ny):
        total = total + rp[q]
    fright = dot(linv, total, NN, HIGH)
    right_out[...] = fright
    wh, wl = split2(dot(linv.T, fright, NN, HIGH) * (1.0 / workers))
    w_out[...] = jnp.concatenate([wh, wh, wl, wl], axis=0)

    loop(1, ny, lambda s: yk_copy(s).wait_recv())
    total = yk[0]
    for q in range(1, ny):
        total = total + yk[q]
    for a in range(7):
        kg_out[a] = total[0:7, OWN * a : OWN * (a + 1)]

    for one in (cor_store, ls4_store, left_store):
        one.wait()
    loop(1, nz, lambda s: cz_copy(s).wait_send())
    loop(1, nz, lambda s: xz_copy(s).wait_send())
    es_copy.wait_send()
    for one in (in_r, in_gh, in_w):
        one.wait_send()
    loop(1, nx, lambda s: cs_copy(s).wait_send())
    gt_copy.wait_send()
    loop(1, nz, lambda s: rz_copy(s).wait_send())
    loop(1, ny, lambda s: ys_copy(s).wait_send())
    loop(1, nx, lambda s: lx_copy(s).wait_send())
    loop(1, nz, lambda s: lz_copy(s).wait_send())
    lk_copy.wait_send()
    loop(1, ny, lambda s: rp_copy(s).wait_send())
    loop(1, nz, lambda s: rk_copy(s).wait_send())
    loop(1, ny, lambda s: yk_copy(s).wait_send())
    for s in range(4):
        cx_copies[s].wait_send()
        cc_copy(s).wait_send()
    for one in (far_right, far_left, near_right, near_left):
        one.wait_send()


def finish(kg_ref, left_ref, right_ref, w_ref, ls_ref, cor_ref, kg_out, left_out, right_out, err_out):
    kg_out[...] = kg_ref[...]
    left_out[...] = left_ref[...]
    right_out[...] = right_ref[...]
    approx = dot(ls_ref[...], w_ref[...], NN)
    err_out[...] = cor_ref[...] - approx.reshape(cor_ref.shape)


def on_device(ny, nz, nx, block_input, depth_kernel, w_expand, grad_hidden, error_old, right_init):
    nxk = 2 * nx
    ch = OWN * nz
    channels = nz * nxk * OWN
    tpz = 8 // nz
    hid = right_init.shape[0]
    vmem = pltpu.VMEM
    scratch = [
        vmem((SIDE, SIDE, OWN), BF16),
        vmem((7, 7, channels), F32),
        vmem((channels, 128), BF16),
        vmem((nz, nxk, OWN, 128), F32),
        vmem((RANK, 128), F32),
        vmem((LP, 128), BF16),
        vmem((LP, 128), BF16),
        vmem((channels, 128), BF16),
        vmem((RANK, 128), F32),
        vmem((nz, nx, 2, OWN, 256), F32),
        vmem((LP, OWN), F32),
        vmem((OWN, LX), F32),
        vmem((OWN, LP), F32),
        vmem((nz, 16, LX), BF16),
        vmem((nz, 16, LX), BF16),
        vmem((ch, LX), F32),
        vmem((8, LP), F32),
        vmem((64, channels), F32),
        vmem((OWN, 64), F32),
        vmem((ch, LP), F32),
        vmem((nx, 2, ch, LP), BF16),
        vmem((2, ch, LP), F32),
        vmem((3, ch, LP), BF16),
        vmem((2, ch // 2, LP), BF16),
        vmem((2, ch, LP), BF16),
        vmem((ch, LP), F32),
        vmem((nx, 2, 8, 8, 128), F32),
        vmem((2, 10, 8, 128), F32),
        vmem((nx, 8, 8, 128), F32),
        vmem((nx, 2, 18, 8, 128), F32),
        vmem((2, 10, 8, 128), F32),
        vmem((8, 8, 128), F32),
        vmem((nz, tpz, 8, 128), F32),
        vmem((ny, tpz, 8, 128), F32),
        vmem((2, nz, nx, tpz, 8, 128), F32),
        vmem((nxk, 256, 256), BF16),
        vmem((ny, RANK, 128), F32),
        vmem((nz, 8, 256), F32),
        vmem((nz, 8, 256), F32),
        vmem((ny, 8, 256), F32),
        vmem((nz, nxk, OWN, RANK), F32),
        vmem((channels, 4 * RANK), BF16),
        vmem((nz, nxk, OWN, 128), F32),
        vmem((RANK, channels), F32),
    ]
    sems = [pltpu.SemaphoreType.DMA((9,))]
    for count in (nz, nz, 2, nx, 1, nz, ny, nx, nz, 1, ny, nz, ny, 4, 4, 4, 4):
        sems += [pltpu.SemaphoreType.DMA((count,))] * 2
    spec = pl.BlockSpec(memory_space=pltpu.VMEM)
    far = pl.BlockSpec(memory_space=pl.ANY)
    cor_shape = jax.ShapeDtypeStruct((nz, nxk, OWN, 128), F32)
    mids = (
        jax.ShapeDtypeStruct((7, 7, OWN), F32),
        jax.ShapeDtypeStruct((RANK, channels), F32),
        jax.ShapeDtypeStruct((RANK, 128), F32),
        jax.ShapeDtypeStruct((4 * RANK, 128), BF16),
        jax.ShapeDtypeStruct((channels, 4 * RANK), BF16),
        cor_shape,
    )
    parts = pl.pallas_call(
        functools.partial(kernel, ny, nz, nx),
        out_shape=mids,
        in_specs=[pl.BlockSpec(memory_space=pl.ANY)] * 6,
        out_specs=(spec, far, spec, spec, far, far),
        scratch_shapes=scratch + sems,
        compiler_params=pltpu.CompilerParams(
            collective_id=0, has_side_effects=True, vmem_limit_bytes=60 * 1024 * 1024
        ),
        cost_estimate=pl.CostEstimate(
            flops=600_000_000, bytes_accessed=4_000_000, transcendentals=0
        ),
    )(
        block_input.reshape(SIDE, SIDE, OWN),
        depth_kernel,
        w_expand,
        grad_hidden.reshape(POS, 128),
        error_old.reshape(nz, nxk, OWN, 128),
        right_init.T,
    )
    kg, left, right, err = pl.pallas_call(
        finish,
        out_shape=mids[0:3] + (cor_shape,),
        in_specs=[spec] * 6,
        out_specs=(spec,) * 4,
        compiler_params=pltpu.CompilerParams(vmem_limit_bytes=60 * 1024 * 1024),
        cost_estimate=pl.CostEstimate(
            flops=60_000_000, bytes_accessed=2_500_000, transcendentals=0
        ),
    )(*parts)
    return (
        kg,
        left.T,
        right.T,
        err.reshape(1, channels, 128),
    )


def solution(mesh, nx=NX):
    ny = mesh.shape["outer"]
    nz = mesh.shape["chip"] // (2 * nx)
    placed = (
        P("outer", None, None, "chip"),
        P(),
        P(None, "chip"),
        P("outer", None, None, "chip"),
        P("outer", None, "chip"),
        P("chip", None),
    )
    return jax.shard_map(
        functools.partial(on_device, ny, nz, nx),
        mesh=mesh,
        in_specs=placed,
        out_specs=(P(None, None, "chip"), P(), P("chip", None), P("outer", None, "chip")),
        check_vma=False,
    )
```

```python
import functools

import jax
import jax.numpy as jnp
from jax import lax
from jax.experimental import pallas as pl
from jax.experimental.pallas import tpu as pltpu
from jax.sharding import PartitionSpec as P

F32 = jnp.float32
BF16 = jnp.bfloat16
HIGH = lax.Precision.HIGHEST
MESH = pl.DeviceIdType.MESH

NX = 4
SIDE = 24
POS = SIDE * SIDE
LP = 640
LX = 896
OWN = 24
RANK = 32


def dot(a, b, dims, precision=None):
    return lax.dot_general(a, b, (dims, ((), ())), precision=precision, preferred_element_type=F32)


NN = ((1,), (0,))
NT = ((1,), (1,))
TN = ((0,), (0,))


def loop(lo, hi, body, unroll=1):
    def step(i, carry):
        body(i)
        return carry

    lax.fori_loop(lo, hi, step, 0, unroll=unroll)


def split2(v):
    hi = v.astype(BF16)
    return hi, (v - hi.astype(F32)).astype(BF16)


def split3(v):
    hi = v.astype(BF16)
    rest = v - hi.astype(F32)
    mid = rest.astype(BF16)
    return hi, mid, (rest - mid.astype(F32)).astype(BF16)


def kernel(
    ny, nz, nx,
    x_hbm, k_hbm, w_hbm, gh_hbm, err_hbm, r_hbm,
    kg_out, left_out, right_out, w_out, ls4_out, cor_out,
    x_ref, k_ref, w_ref, err_ref, r_ref,
    ghp, ghs, ws, rs, wf, x2, xo, conv24, cz, xz, xp, mk, kflat, kt, conv32, cvf, gr, gb, rh1, rh2, g32,
    eg, gg, es, cs, gt, st, rz, ys, ll, chl, rp, kgt, rk, yk, lsn, ls4, cor, left,
    s_in,
    s_cz, r_cz, s_xz, r_xz, s_es, r_es, s_cs, r_cs, s_gt, r_gt, s_rz, r_rz, s_ys, r_ys, s_lx, r_lx, s_lz, r_lz,
    s_lk, r_lk, s_rp, r_rp, s_rk, r_rk, s_yk, r_yk, s_in2, r_in2, s_gx, r_gx, s_cx, r_cx, s_cc, r_cc,
):
    nxk = 2 * nx
    ch = OWN * nz
    channels = ch * nxk
    tpz = 8 // nz
    half = ch // 2
    workers = ny
    y = lax.axis_index("outer")
    chip = lax.axis_index("chip")
    z = chip // nxk
    xk = lax.rem(chip, nxk)
    x = xk // 2
    k = lax.rem(xk, 2)

    def zpeer(s):
        return lax.rem(z + s, nz)

    def at_z(zz):
        return (y, zz * nxk + xk)

    def at_x(xx):
        return (y, z * nxk + xx * 2 + k)

    right_x = lax.rem(x + 1, nx)
    left_x = lax.rem(x + nx - 1, nx)
    far_x = lax.rem(x + 2, nx)

    def at_y(yy):
        return (yy, chip)

    sibling = (y, z * nxk + x * 2 + (1 - k))

    def copy(src, dst, ssem, rsem, dev):
        return pltpu.make_async_remote_copy(
            src_ref=src, dst_ref=dst, send_sem=ssem, recv_sem=rsem,
            device_id=dev, device_id_type=MESH,
        )

    load_x = pltpu.make_async_copy(x_hbm, x_ref, s_in.at[0])
    load_r = pltpu.make_async_copy(r_hbm, r_ref, s_in.at[1])
    load_err = pltpu.make_async_copy(err_hbm, err_ref, s_in.at[2])
    load_gh = pltpu.make_async_copy(gh_hbm, ghp.at[pl.ds(0, POS)], s_in.at[3])
    load_w = pltpu.make_async_copy(w_hbm, w_ref, s_in.at[4])
    load_k = pltpu.make_async_copy(k_hbm, k_ref, s_in.at[5])
    for load in (load_x, load_r, load_err, load_gh, load_w, load_k):
        load.start()

    barrier = pltpu.get_barrier_semaphore()

    def greet(dev):
        pl.semaphore_signal(barrier, inc=1, device_id=dev, device_id_type=MESH)

    loop(1, nz, lambda s: greet(at_z(zpeer(s))))
    loop(1, nx, lambda s: greet(at_x(lax.rem(x + s, nx))))
    greet(sibling)
    loop(1, ny, lambda s: greet(at_y(lax.rem(y + s, ny))))

    pl.semaphore_wait(barrier, (nz - 1) + (nx - 1) + (ny - 1) + 1)

    in_gh = copy(gh_hbm, ghs.at[pl.ds(0, POS)], s_in2.at[0], r_in2.at[0], sibling)
    in_r = copy(r_hbm, rs, s_in2.at[1], r_in2.at[1], sibling)
    in_w = copy(w_hbm, ws, s_in2.at[2], r_in2.at[2], sibling)
    for one in (in_r, in_gh, in_w):
        one.start()

    x2[POS:, :] = jnp.zeros((LP - POS, OWN), F32)
    load_x.wait()
    for i in range(SIDE):
        x2[SIDE * i : SIDE * (i + 1), :] = x_ref[i].astype(F32)
    eye = (
        lax.broadcasted_iota(jnp.int32, (32, OWN), 0)
        == lax.broadcasted_iota(jnp.int32, (32, OWN), 1)
    )
    own = dot(eye.astype(F32).astype(BF16), x2[...].astype(BF16), NT)[0:OWN]
    xo[:, 0:128] = jnp.zeros((OWN, 128), F32)
    xo[:, 128 : 128 + LP] = own
    xo[:, 128 + LP :] = jnp.zeros((OWN, LX - 128 - LP), F32)
    load_k.wait()
    for a in range(7):
        kflat[8 * a : 8 * a + 7, :] = k_ref[a]
        kflat[8 * a + 7 : 8 * a + 8, :] = jnp.zeros((1, channels), F32)
    kflat[56:64, :] = jnp.zeros((8, channels), F32)
    row = lax.broadcasted_iota(jnp.int32, (OWN, channels), 0)
    lane = lax.broadcasted_iota(jnp.int32, (OWN, channels), 1)
    pick = (lane - row == chip * OWN).astype(F32).astype(BF16)
    three = jnp.concatenate(split3(kflat[...]), axis=0)
    taps3 = dot(pick, three, NT)
    kt[...] = taps3[:, 0:64] + taps3[:, 64:128] + taps3[:, 128:192]
    pos = lax.broadcasted_iota(jnp.int32, (8, LP), 1)
    col = lax.rem(pos, SIDE) + lax.broadcasted_iota(jnp.int32, (8, LP), 0) - 3
    mk[...] = ((col >= 0) & (col < SIDE) & (pos < POS)).astype(F32)

    def shifted(v):
        return [pltpu.roll(v, LX - (96 + SIDE * (a - 3)), 1)[:, 0:LP] for a in range(7)]

    for t in range(OWN // 8):
        rows = slice(8 * t, 8 * t + 8)
        taps = kt[rows, :]
        moved = shifted(xo[rows, :])
        out = None
        for b in range(7):
            part = None
            for a in range(7):
                term = taps[:, 8 * a + b : 8 * a + b + 1] * moved[a]
                part = term if a == 0 else part + term
            part = pltpu.roll(part, LP - (32 + b - 3), 1) * mk[b : b + 1, :]
            out = part if b == 0 else out + part
        conv24[rows, :] = out

    lane_x = lax.broadcasted_iota(jnp.int32, (16, LX), 1)

    def pack(v):
        wide = jnp.concatenate([v, jnp.zeros((OWN, LX - LP), F32)], axis=1)
        last = wide[16:24]
        early = jnp.where(lane_x[0:8] < POS // 2, last, 0.0)
        late = jnp.where(lane_x[0:8] < POS // 2, 0.0, last)
        tail = jnp.concatenate(
            [pltpu.roll(early, POS, 1), pltpu.roll(late, POS // 2, 1)], axis=0
        )
        return (wide[0:16] + tail).astype(BF16)

    def unpack(v):
        v = v.astype(F32)
        early = pltpu.roll(v[0:8], LX - POS, 1)
        late = pltpu.roll(v[8:16], LX - POS // 2, 1)
        last = jnp.where(
            lane_x[0:8] < POS // 2, early, jnp.where(lane_x[0:8] < POS, late, 0.0)
        )
        return jnp.where(lane_x < POS, v, 0.0)[:, 0:LP], last[:, 0:LP]

    cz[z] = pack(conv24[...])

    def cz_copy(s):
        return copy(cz.at[z], cz.at[z], s_cz.at[s], r_cz.at[s], at_z(zpeer(s)))

    loop(1, nz, lambda s: cz_copy(s).start())
    xz[z] = pack(own)

    def xz_copy(s):
        return copy(xz.at[z], xz.at[z], s_xz.at[s], r_xz.at[s], at_z(zpeer(s)))


    load_r.wait()
    load_err.wait()
    rh, rl = split2(r_ref[...])
    four = jnp.concatenate(
        [jnp.concatenate([rh, rh], axis=1), jnp.concatenate([rl, rl], axis=1)], axis=0
    )
    for q in range(nxk):
        eh, el = split2(err_ref[:, q].reshape(ch, 128))
        rows = jnp.concatenate([eh, el], axis=1)
        if ch < 256:
            rows = jnp.concatenate([rows, jnp.zeros((256 - ch, 256), BF16)], axis=0)
        e = dot(four, rows, NT)
        e = e[0:32] + e[32:64]
        for rg in range(4):
            for part in range(2):
                eg[q // 2, q % 2, 2 * rg + part] = e[8 * rg : 8 * rg + 8, 128 * part : 128 * part + 128]

    es_copy = copy(eg.at[:, 1 - k], es, s_es.at[0], r_es.at[0], sibling)
    es_copy.start()

    ghp[POS:, :] = jnp.zeros((LP - POS, 128), BF16)
    ghs[POS:, :] = jnp.zeros((LP - POS, 128), BF16)

    load_gh.wait()
    in_gh.wait_recv()
    in_r.wait_recv()
    sh, sl = split2(rs[...])
    both = jnp.concatenate([ghp[...], ghs[...]], axis=1)
    g = dot(
        jnp.concatenate([rh, sh, rl, sl], axis=1), jnp.concatenate([both, both], axis=1), NT
    )
    for rg in range(4):
        for j in range(5):
            gg[rg // 2, (rg % 2) * 5 + j] = g[8 * rg : 8 * rg + 8, 128 * j : 128 * j + 128]

    es_copy.wait_recv()

    def chip_sum(xx):
        cs[xx, 0, 0:8] = eg[xx, k] + es[xx]
        cs[xx, 0, 8:18] = gg[k]

    loop(0, nx, chip_sum)
    cs[x, 1] = cs[x, 0]

    def cs_copy(s):
        xx = lax.rem(x + s, nx)
        return copy(cs.at[xx, 0], cs.at[x, 1], s_cs.at[s], r_cs.at[s], at_x(xx))

    loop(1, nx, lambda s: cs_copy(s).start())

    load_w.wait()
    in_w.wait_recv()
    wf[:, :, :, :, 0:128] = w_ref[...].astype(F32).reshape(nz, nx, 2, OWN, 128)
    wf[:, :, :, :, 128:256] = ws[...].astype(F32).reshape(nz, nx, 2, OWN, 128)

    def grad_rows(xx):
        rows = wf[:, xx, k].reshape(ch, 256).astype(BF16)
        return dot(rows, jnp.concatenate([ghp[...], ghs[...]], axis=1), NT)

    gb[0] = grad_rows(far_x).astype(BF16)
    far_right = copy(
        gb.at[0, pl.ds(0, half)], rh1.at[0], s_gx.at[0], r_gx.at[0], at_x(right_x)
    )
    far_left = copy(
        gb.at[0, pl.ds(half, half)], rh1.at[1], s_gx.at[1], r_gx.at[1], at_x(left_x)
    )
    far_right.start()
    far_left.start()
    gr[0] = grad_rows(right_x)
    gr[1] = grad_rows(left_x)
    g32[...] = grad_rows(x)

    loop(1, nx, lambda s: cs_copy(s).wait_recv())
    total = cs[0, 1]
    for q in range(1, nx):
        total = total + cs[q, 1]
    st[...] = total[0:8]
    gt[k] = total[8:18]
    gt_copy = copy(gt.at[k], gt.at[k], s_gt.at[0], r_gt.at[0], sibling)
    gt_copy.start()

    loop(1, nz, lambda s: cz_copy(s).wait_recv())
    for zz in range(nz):
        first, last = unpack(cz[zz])
        conv32[OWN * zz : OWN * zz + 16, :] = first
        conv32[OWN * zz + 16 : OWN * zz + 24, :] = last
    cvf[x, k] = conv32[...].astype(BF16)

    gt_copy.wait_recv()
    groups = []
    for rg in range(4):
        groups.append(
            jnp.concatenate([gt[rg // 2, (rg % 2) * 5 + j] for j in range(5)], axis=1)
        )
    gsplit = jnp.concatenate(split2(jnp.concatenate(groups, axis=0)), axis=0)
    conv_pad = cvf[x, k]
    if ch < 256:
        conv_pad = jnp.concatenate([conv_pad, jnp.zeros((256 - ch, LP), BF16)], axis=0)
    conv_left = dot(gsplit, conv_pad, NT)
    conv_left = conv_left[0:32] + conv_left[32:64]
    for rg in range(4):
        for part in range(2):
            st[2 * rg + part] += conv_left[8 * rg : 8 * rg + 8, 128 * part : 128 * part + 128]

    def rz_copy(s):
        zz = zpeer(s)
        return copy(st.at[pl.ds(zz * tpz, tpz)], rz.at[z], s_rz.at[s], r_rz.at[s], at_z(zz))

    loop(1, nz, lambda s: rz_copy(s).start())
    rz[z] = st[pl.ds(z * tpz, tpz)]
    loop(1, nz, lambda s: xz_copy(s).start())

    far_right.wait_recv()
    gb[1, 0:half, :] = (gr[0, 0:half, :] + rh1[0].astype(F32)).astype(BF16)
    gb[1, half:, :] = gr[0, half:, :].astype(BF16)
    near_right = copy(gb.at[1], rh2.at[0], s_gx.at[2], r_gx.at[2], at_x(right_x))
    near_right.start()
    far_left.wait_recv()
    gb[2, 0:half, :] = gr[1, 0:half, :].astype(BF16)
    gb[2, half:, :] = (gr[1, half:, :] + rh1[1].astype(F32)).astype(BF16)
    near_left = copy(gb.at[2], rh2.at[1], s_gx.at[3], r_gx.at[3], at_x(left_x))
    near_left.start()

    mine = cvf.at[x, k]
    cx_copies = [
        copy(mine, mine, s_cx.at[0], r_cx.at[0], at_x(right_x)),
        copy(mine, mine, s_cx.at[1], r_cx.at[1], at_x(left_x)),
    ]
    for s in range(2):
        cx_copies[s].start()

    sources = (x, left_x, right_x, far_x)

    def cc_copy(s):
        block = cvf.at[sources[s], k]
        return copy(block, block, s_cc.at[s], r_cc.at[s], sibling)

    cc_copy(0).start()

    loop(1, nz, lambda s: rz_copy(s).wait_recv())
    total = rz[0]
    for q in range(1, nz):
        total = total + rz[q]
    ys[y] = total

    def ys_copy(s):
        return copy(ys.at[y], ys.at[y], s_ys.at[s], r_ys.at[s], at_y(lax.rem(y + s, ny)))

    loop(1, ny, lambda s: ys_copy(s).start())

    def local_grad(xx, kk):
        q = xx * 2 + kk
        part = dot(cvf[xx, kk], ghp[...], NN) + err_ref[:, q].reshape(ch, 128)
        cor[:, q] = part.reshape(nz, OWN, 128)
        chl[q, 0:ch, :] = jnp.concatenate(split2(part), axis=1)

    if ch < 256:
        chl[:, ch:, :] = jnp.zeros((nxk, 256 - ch, 256), BF16)
    loop(1, ny, lambda s: ys_copy(s).wait_recv())
    total = ys[0]
    for q in range(1, ny):
        total = total + ys[q]
    ll[k, z, x] = total

    def lx_copy(s):
        own = ll.at[k, z, x]
        return copy(own, own, s_lx.at[s], r_lx.at[s], at_x(lax.rem(x + s, nx)))

    loop(1, nx, lambda s: lx_copy(s).start())

    local_grad(x, k)

    loop(1, nz, lambda s: xz_copy(s).wait_recv())
    xp[:, 0:128] = jnp.zeros((ch, 128), F32)
    xp[:, 128 + LP :] = jnp.zeros((ch, LX - 128 - LP), F32)
    for zz in range(nz):
        first, last = unpack(xz[zz])
        xp[OWN * zz : OWN * zz + 16, 128 : 128 + LP] = first
        xp[OWN * zz + 16 : OWN * zz + 24, 128 : 128 + LP] = last
    near_right.wait_recv()
    near_left.wait_recv()
    g32[...] += rh2[0].astype(F32) + rh2[1].astype(F32)
    pair_row = lax.broadcasted_iota(jnp.int32, (OWN, 7 * OWN), 0)
    pair_lane = lax.broadcasted_iota(jnp.int32, (OWN, 7 * OWN), 1)
    diagonal = lax.rem(pair_lane, OWN) == pair_row
    tap_row = lax.broadcasted_iota(jnp.int32, (8, 7 * OWN), 0)

    def kernel_terms(zz):
        rows = pl.ds(pl.multiple_of(zz * OWN, 8), OWN)
        maps = jnp.concatenate(shifted(xp[rows, :]), axis=0).astype(BF16)
        gt = g32[rows, :]
        moved = [pltpu.roll(gt * mk[b : b + 1, :], 32 + b - 3, 1) for b in range(7)]
        hi, lo = split2(jnp.concatenate(moved, axis=0))
        pairs = dot(hi, maps, NT) + dot(lo, maps, NT)
        out = jnp.zeros((8, 7 * OWN), F32)
        for b in range(7):
            block = jnp.where(diagonal, pairs[OWN * b : OWN * (b + 1)], 0.0)
            one = jnp.sum(block, axis=0, keepdims=True)
            out = jnp.where(tap_row == b, one, out)
        kgt[zz] = jnp.concatenate([out, jnp.zeros((8, 256 - 7 * OWN), F32)], axis=1)

    loop(0, nz, kernel_terms, 2)

    def rk_copy(s):
        zz = zpeer(s)
        return copy(kgt.at[zz], rk.at[z], s_rk.at[s], r_rk.at[s], at_z(zz))

    loop(1, nz, lambda s: rk_copy(s).start())
    rk[z] = kgt[z]

    def lx_wait(s):
        got = ll.at[k, z, lax.rem(x - s + nx, nx)]
        copy(got, got, s_lx.at[s], r_lx.at[s], at_x(lax.rem(x + s, nx))).wait_recv()

    loop(1, nx, lx_wait)

    def lz_copy(s):
        own = ll.at[k, z]
        return copy(own, own, s_lz.at[s], r_lz.at[s], at_z(zpeer(s)))

    loop(1, nz, lambda s: lz_copy(s).start())

    cx_copies[0].wait_recv()
    part0 = cvf.at[left_x, k, pl.ds(0, half)]
    cx_copies.append(copy(part0, part0, s_cx.at[2], r_cx.at[2], at_x(right_x)))
    cx_copies[2].start()
    cc_copy(1).start()
    cx_copies[1].wait_recv()
    part1 = cvf.at[right_x, k, pl.ds(half, half)]
    cx_copies.append(copy(part1, part1, s_cx.at[3], r_cx.at[3], at_x(left_x)))
    cx_copies[3].start()
    cc_copy(2).start()
    local_grad(left_x, k)
    local_grad(right_x, k)

    for s in range(3):
        cc_copy(s).wait_recv()
        local_grad(sources[s], 1 - k)

    loop(1, nz, lambda s: rk_copy(s).wait_recv())
    total = rk[0]
    for q in range(1, nz):
        total = total + rk[q]
    yk[y] = total

    def yk_copy(s):
        return copy(yk.at[y], yk.at[y], s_yk.at[s], r_yk.at[s], at_y(lax.rem(y + s, ny)))

    loop(1, ny, lambda s: yk_copy(s).start())

    def lz_wait(s):
        got = ll.at[k, lax.rem(z - s + nz, nz)]
        copy(got, got, s_lz.at[s], r_lz.at[s], at_z(zpeer(s))).wait_recv()

    loop(1, nz, lz_wait)
    lk_copy = copy(ll.at[k], ll.at[k], s_lk.at[0], r_lk.at[0], sibling)
    lk_copy.start()

    cx_copies[2].wait_recv()
    cx_copies[3].wait_recv()
    cc_copy(3).start()
    local_grad(far_x, k)

    lk_copy.wait_recv()

    def left_of(q):
        rows = []
        for rg in range(4):
            tiles = [ll[q % 2, t // tpz, q // 2, t % tpz] for t in (2 * rg, 2 * rg + 1)]
            rows.append(jnp.concatenate(tiles, axis=1))
        return jnp.concatenate(rows, axis=0)

    lefts = [left_of(q) for q in range(nxk)]
    wide3 = split3(jnp.concatenate(lefts, axis=1))
    stack3 = jnp.concatenate(wide3, axis=0)
    gram = None
    for part in wide3:
        term = dot(stack3, part, NT)
        term = term[0:32] + term[32:64] + term[64:96]
        gram = term if gram is None else gram + term
    for q in range(nxk):
        lsn[:, q] = lefts[q].T[0:ch].reshape(nz, OWN, RANK)
    natural = lsn[...].reshape(channels, RANK).T
    nh, nm, nl = split3(natural)
    ls4[...] = jnp.concatenate([nh, nm, nh, nm], axis=0).T
    ls4_store = pltpu.make_async_copy(ls4, ls4_out, s_in.at[7])
    ls4_store.start()

    cc_copy(3).wait_recv()
    local_grad(far_x, 1 - k)
    cor_store = pltpu.make_async_copy(cor, cor_out, s_in.at[6])
    cor_store.start()

    right = None
    for q in range(nxk):
        term = dot(jnp.concatenate(split2(lefts[q]), axis=0), chl[q], NN)
        right = term if q == 0 else right + term
    right = right[0:32] + right[32:64]
    rp[y] = right[:, 0:128] + right[:, 128:256]

    def rp_copy(s):
        return copy(rp.at[y], rp.at[y], s_rp.at[s], r_rp.at[s], at_y(lax.rem(y + s, ny)))

    loop(1, ny, lambda s: rp_copy(s).start())

    row_id = lax.broadcasted_iota(jnp.int32, (RANK, RANK), 0)
    lane_id = lax.broadcasted_iota(jnp.int32, (RANK, RANK), 1)
    same = row_id == lane_id
    aug = jnp.concatenate([gram, same.astype(F32)], axis=1)
    row_col = lax.broadcasted_iota(jnp.int32, (RANK, 2 * RANK), 0)

    def full(v):
        return jnp.broadcast_to(v, (RANK, 2 * RANK))

    for i in range(0, RANK, 2):
        c0 = full(aug[:, i : i + 1])
        c1 = full(aug[:, i + 1 : i + 2])
        r0 = full(aug[i : i + 1, :])
        r1 = full(aug[i + 1 : i + 2, :])
        p00 = full(c0[i : i + 1, :])
        p01 = full(c1[i : i + 1, :])
        p11 = full(c1[i + 1 : i + 2, :])
        inv = 1.0 / (p00 * p11 - p01 * p01)
        u0 = (p11 * c0 - p01 * c1) * inv
        u1 = (p00 * c1 - p01 * c0) * inv
        u0 = jnp.where(row_col > i + 1, u0, jnp.where(row_col == i + 1, p01 / p00, 0.0))
        u1 = jnp.where(row_col > i + 1, u1, 0.0)
        aug = aug - u0 * r0 - u1 * r1
    diag = jnp.sum(jnp.where(same, aug[:, 0:RANK], 0.0), axis=1, keepdims=True)
    scale = lax.rsqrt(diag)
    scale = scale * (1.5 - 0.5 * diag * scale * scale)
    linv = aug[:, RANK:] * scale
    ih, im, il = split3(linv)
    left[...] = dot(
        jnp.concatenate([ih, ih, ih, im, im, il], axis=1),
        jnp.concatenate([nh, nm, nl, nh, nm, nh], axis=0),
        NN,
    )
    left_store = pltpu.make_async_copy(left, left_out, s_in.at[8])
    left_store.start()

    loop(1, ny, lambda s: rp_copy(s).wait_recv())
    total = rp[0]
    for q in range(1, ny):
        total = total + rp[q]
    fright = dot(linv, total, NN, HIGH)
    right_out[...] = fright
    wh, wl = split2(dot(linv.T, fright, NN, HIGH) * (1.0 / workers))
    w_out[...] = jnp.concatenate([wh, wh, wl, wl], axis=0)

    loop(1, ny, lambda s: yk_copy(s).wait_recv())
    total = yk[0]
    for q in range(1, ny):
        total = total + yk[q]
    for a in range(7):
        kg_out[a] = total[0:7, OWN * a : OWN * (a + 1)]

    for one in (cor_store, ls4_store, left_store):
        one.wait()
    loop(1, nz, lambda s: cz_copy(s).wait_send())
    loop(1, nz, lambda s: xz_copy(s).wait_send())
    es_copy.wait_send()
    for one in (in_r, in_gh, in_w):
        one.wait_send()
    loop(1, nx, lambda s: cs_copy(s).wait_send())
    gt_copy.wait_send()
    loop(1, nz, lambda s: rz_copy(s).wait_send())
    loop(1, ny, lambda s: ys_copy(s).wait_send())
    loop(1, nx, lambda s: lx_copy(s).wait_send())
    loop(1, nz, lambda s: lz_copy(s).wait_send())
    lk_copy.wait_send()
    loop(1, ny, lambda s: rp_copy(s).wait_send())
    loop(1, nz, lambda s: rk_copy(s).wait_send())
    loop(1, ny, lambda s: yk_copy(s).wait_send())
    for s in range(4):
        cx_copies[s].wait_send()
        cc_copy(s).wait_send()
    for one in (far_right, far_left, near_right, near_left):
        one.wait_send()


def finish(kg_ref, left_ref, right_ref, w_ref, ls_ref, cor_ref, kg_out, left_out, right_out, err_out):
    kg_out[...] = kg_ref[...]
    left_out[...] = left_ref[...]
    right_out[...] = right_ref[...]
    approx = dot(ls_ref[...], w_ref[...], NN)
    err_out[...] = cor_ref[...] - approx.reshape(cor_ref.shape)


def on_device(ny, nz, nx, block_input, depth_kernel, w_expand, grad_hidden, error_old, right_init):
    nxk = 2 * nx
    ch = OWN * nz
    channels = nz * nxk * OWN
    tpz = 8 // nz
    hid = right_init.shape[0]
    vmem = pltpu.VMEM
    scratch = [
        vmem((SIDE, SIDE, OWN), BF16),
        vmem((7, 7, channels), F32),
        vmem((channels, 128), BF16),
        vmem((nz, nxk, OWN, 128), F32),
        vmem((RANK, 128), F32),
        vmem((LP, 128), BF16),
        vmem((LP, 128), BF16),
        vmem((channels, 128), BF16),
        vmem((RANK, 128), F32),
        vmem((nz, nx, 2, OWN, 256), F32),
        vmem((LP, OWN), F32),
        vmem((OWN, LX), F32),
        vmem((OWN, LP), F32),
        vmem((nz, 16, LX), BF16),
        vmem((nz, 16, LX), BF16),
        vmem((ch, LX), F32),
        vmem((8, LP), F32),
        vmem((64, channels), F32),
        vmem((OWN, 64), F32),
        vmem((ch, LP), F32),
        vmem((nx, 2, ch, LP), BF16),
        vmem((2, ch, LP), F32),
        vmem((3, ch, LP), BF16),
        vmem((2, ch // 2, LP), BF16),
        vmem((2, ch, LP), BF16),
        vmem((ch, LP), F32),
        vmem((nx, 2, 8, 8, 128), F32),
        vmem((2, 10, 8, 128), F32),
        vmem((nx, 8, 8, 128), F32),
        vmem((nx, 2, 18, 8, 128), F32),
        vmem((2, 10, 8, 128), F32),
        vmem((8, 8, 128), F32),
        vmem((nz, tpz, 8, 128), F32),
        vmem((ny, tpz, 8, 128), F32),
        vmem((2, nz, nx, tpz, 8, 128), F32),
        vmem((nxk, 256, 256), BF16),
        vmem((ny, RANK, 128), F32),
        vmem((nz, 8, 256), F32),
        vmem((nz, 8, 256), F32),
        vmem((ny, 8, 256), F32),
        vmem((nz, nxk, OWN, RANK), F32),
        vmem((channels, 4 * RANK), BF16),
        vmem((nz, nxk, OWN, 128), F32),
        vmem((RANK, channels), F32),
    ]
    sems = [pltpu.SemaphoreType.DMA((9,))]
    for count in (nz, nz, 2, nx, 1, nz, ny, nx, nz, 1, ny, nz, ny, 4, 4, 4, 4):
        sems += [pltpu.SemaphoreType.DMA((count,))] * 2
    spec = pl.BlockSpec(memory_space=pltpu.VMEM)
    far = pl.BlockSpec(memory_space=pl.ANY)
    cor_shape = jax.ShapeDtypeStruct((nz, nxk, OWN, 128), F32)
    mids = (
        jax.ShapeDtypeStruct((7, 7, OWN), F32),
        jax.ShapeDtypeStruct((RANK, channels), F32),
        jax.ShapeDtypeStruct((RANK, 128), F32),
        jax.ShapeDtypeStruct((4 * RANK, 128), BF16),
        jax.ShapeDtypeStruct((channels, 4 * RANK), BF16),
        cor_shape,
    )
    parts = pl.pallas_call(
        functools.partial(kernel, ny, nz, nx),
        out_shape=mids,
        in_specs=[pl.BlockSpec(memory_space=pl.ANY)] * 6,
        out_specs=(spec, far, spec, spec, far, far),
        scratch_shapes=scratch + sems,
        compiler_params=pltpu.CompilerParams(
            collective_id=0, has_side_effects=True, vmem_limit_bytes=60 * 1024 * 1024
        ),
        cost_estimate=pl.CostEstimate(
            flops=600_000_000, bytes_accessed=4_000_000, transcendentals=0
        ),
    )(
        block_input.reshape(SIDE, SIDE, OWN),
        depth_kernel,
        w_expand,
        grad_hidden.reshape(POS, 128),
        error_old.reshape(nz, nxk, OWN, 128),
        right_init.T,
    )
    kg, left, right, err = pl.pallas_call(
        finish,
        out_shape=mids[0:3] + (cor_shape,),
        in_specs=[spec] * 6,
        out_specs=(spec,) * 4,
        compiler_params=pltpu.CompilerParams(vmem_limit_bytes=60 * 1024 * 1024),
        cost_estimate=pl.CostEstimate(
            flops=60_000_000, bytes_accessed=2_500_000, transcendentals=0
        ),
    )(*parts)
    return (
        kg,
        left.T,
        right.T,
        err.reshape(1, channels, 128),
    )


def solution(mesh, nx=NX):
    ny = mesh.shape["outer"]
    nz = mesh.shape["chip"] // (2 * nx)
    placed = (
        P("outer", None, None, "chip"),
        P(),
        P(None, "chip"),
        P("outer", None, None, "chip"),
        P("outer", None, "chip"),
        P("chip", None),
    )
    return jax.shard_map(
        functools.partial(on_device, ny, nz, nx),
        mesh=mesh,
        in_specs=placed,
        out_specs=(P(None, None, "chip"), P(), P("chip", None), P("outer", None, "chip")),
        check_vma=False,
    )
```

```python
import functools

import jax
import jax.numpy as jnp
from jax import lax
from jax.experimental import pallas as pl
from jax.experimental.pallas import tpu as pltpu
from jax.sharding import PartitionSpec as P

F32 = jnp.float32
BF16 = jnp.bfloat16
HIGH = lax.Precision.HIGHEST
MESH = pl.DeviceIdType.MESH

NX = 4
SIDE = 24
POS = SIDE * SIDE
LP = 640
LX = 896
OWN = 24
RANK = 32


def dot(a, b, dims, precision=None):
    return lax.dot_general(a, b, (dims, ((), ())), precision=precision, preferred_element_type=F32)


NN = ((1,), (0,))
NT = ((1,), (1,))
TN = ((0,), (0,))


def loop(lo, hi, body, unroll=1):
    def step(i, carry):
        body(i)
        return carry

    lax.fori_loop(lo, hi, step, 0, unroll=unroll)


def split2(v):
    hi = v.astype(BF16)
    return hi, (v - hi.astype(F32)).astype(BF16)


def split3(v):
    hi = v.astype(BF16)
    rest = v - hi.astype(F32)
    mid = rest.astype(BF16)
    return hi, mid, (rest - mid.astype(F32)).astype(BF16)


def kernel(
    ny, nz, nx,
    x_hbm, k_hbm, w_hbm, gh_hbm, err_hbm, r_hbm,
    kg_out, left_out, right_out, w_out, ls4_out, cor_out,
    x_ref, k_ref, w_ref, err_ref, r_ref,
    ghp, ghs, ws, rs, wf, x2, xo, conv24, cz, xz, xp, mk, kflat, kt, conv32, cvf, gr, gb, rh1, rh2, g32,
    eg, gg, es, cs, gt, st, rz, ys, ll, chl, rp, kgt, rk, yk, lsn, ls4, cor, left,
    s_in,
    s_cz, r_cz, s_xz, r_xz, s_es, r_es, s_cs, r_cs, s_gt, r_gt, s_rz, r_rz, s_ys, r_ys, s_lx, r_lx, s_lz, r_lz,
    s_lk, r_lk, s_rp, r_rp, s_rk, r_rk, s_yk, r_yk, s_in2, r_in2, s_gx, r_gx, s_cx, r_cx, s_cc, r_cc,
):
    nxk = 2 * nx
    ch = OWN * nz
    channels = ch * nxk
    tpz = 8 // nz
    half = ch // 2
    workers = ny
    y = lax.axis_index("outer")
    chip = lax.axis_index("chip")
    z = chip // nxk
    xk = lax.rem(chip, nxk)
    x = xk // 2
    k = lax.rem(xk, 2)

    def zpeer(s):
        return lax.rem(z + s, nz)

    def at_z(zz):
        return (y, zz * nxk + xk)

    def at_x(xx):
        return (y, z * nxk + xx * 2 + k)

    right_x = lax.rem(x + 1, nx)
    left_x = lax.rem(x + nx - 1, nx)
    far_x = lax.rem(x + 2, nx)

    def at_y(yy):
        return (yy, chip)

    sibling = (y, z * nxk + x * 2 + (1 - k))

    def copy(src, dst, ssem, rsem, dev):
        return pltpu.make_async_remote_copy(
            src_ref=src, dst_ref=dst, send_sem=ssem, recv_sem=rsem,
            device_id=dev, device_id_type=MESH,
        )

    load_x = pltpu.make_async_copy(x_hbm, x_ref, s_in.at[0])
    load_r = pltpu.make_async_copy(r_hbm, r_ref, s_in.at[1])
    load_err = pltpu.make_async_copy(err_hbm, err_ref, s_in.at[2])
    load_gh = pltpu.make_async_copy(gh_hbm, ghp.at[pl.ds(0, POS)], s_in.at[3])
    load_w = pltpu.make_async_copy(w_hbm, w_ref, s_in.at[4])
    load_k = pltpu.make_async_copy(k_hbm, k_ref, s_in.at[5])
    for load in (load_x, load_r, load_err, load_gh, load_w, load_k):
        load.start()

    barrier = pltpu.get_barrier_semaphore()

    def greet(dev):
        pl.semaphore_signal(barrier, inc=1, device_id=dev, device_id_type=MESH)

    loop(1, nz, lambda s: greet(at_z(zpeer(s))))
    loop(1, nx, lambda s: greet(at_x(lax.rem(x + s, nx))))
    greet(sibling)
    loop(1, ny, lambda s: greet(at_y(lax.rem(y + s, ny))))

    x2[POS:, :] = jnp.zeros((LP - POS, OWN), F32)
    load_x.wait()
    for i in range(SIDE):
        x2[SIDE * i : SIDE * (i + 1), :] = x_ref[i].astype(F32)
    eye = (
        lax.broadcasted_iota(jnp.int32, (32, OWN), 0)
        == lax.broadcasted_iota(jnp.int32, (32, OWN), 1)
    )
    own = dot(eye.astype(F32).astype(BF16), x2[...].astype(BF16), NT)[0:OWN]
    xo[:, 0:128] = jnp.zeros((OWN, 128), F32)
    xo[:, 128 : 128 + LP] = own
    xo[:, 128 + LP :] = jnp.zeros((OWN, LX - 128 - LP), F32)
    load_k.wait()
    for a in range(7):
        kflat[8 * a : 8 * a + 7, :] = k_ref[a]
        kflat[8 * a + 7 : 8 * a + 8, :] = jnp.zeros((1, channels), F32)
    kflat[56:64, :] = jnp.zeros((8, channels), F32)
    row = lax.broadcasted_iota(jnp.int32, (OWN, channels), 0)
    lane = lax.broadcasted_iota(jnp.int32, (OWN, channels), 1)
    pick = (lane - row == chip * OWN).astype(F32).astype(BF16)
    three = jnp.concatenate(split3(kflat[...]), axis=0)
    taps3 = dot(pick, three, NT)
    kt[...] = taps3[:, 0:64] + taps3[:, 64:128] + taps3[:, 128:192]
    pos = lax.broadcasted_iota(jnp.int32, (8, LP), 1)
    col = lax.rem(pos, SIDE) + lax.broadcasted_iota(jnp.int32, (8, LP), 0) - 3
    mk[...] = ((col >= 0) & (col < SIDE) & (pos < POS)).astype(F32)

    def shifted(v):
        return [pltpu.roll(v, LX - (96 + SIDE * (a - 3)), 1)[:, 0:LP] for a in range(7)]

    for t in range(OWN // 8):
        rows = slice(8 * t, 8 * t + 8)
        taps = kt[rows, :]
        moved = shifted(xo[rows, :])
        out = None
        for b in range(7):
            part = None
            for a in range(7):
                term = taps[:, 8 * a + b : 8 * a + b + 1] * moved[a]
                part = term if a == 0 else part + term
            part = pltpu.roll(part, LP - (32 + b - 3), 1) * mk[b : b + 1, :]
            out = part if b == 0 else out + part
        conv24[rows, :] = out

    lane_x = lax.broadcasted_iota(jnp.int32, (16, LX), 1)

    def pack(v):
        wide = jnp.concatenate([v, jnp.zeros((OWN, LX - LP), F32)], axis=1)
        last = wide[16:24]
        early = jnp.where(lane_x[0:8] < POS // 2, last, 0.0)
        late = jnp.where(lane_x[0:8] < POS // 2, 0.0, last)
        tail = jnp.concatenate(
            [pltpu.roll(early, POS, 1), pltpu.roll(late, POS // 2, 1)], axis=0
        )
        return (wide[0:16] + tail).astype(BF16)

    def unpack(v):
        v = v.astype(F32)
        early = pltpu.roll(v[0:8], LX - POS, 1)
        late = pltpu.roll(v[8:16], LX - POS // 2, 1)
        last = jnp.where(
            lane_x[0:8] < POS // 2, early, jnp.where(lane_x[0:8] < POS, late, 0.0)
        )
        return jnp.where(lane_x < POS, v, 0.0)[:, 0:LP], last[:, 0:LP]

    cz[z] = pack(conv24[...])

    def cz_copy(s):
        return copy(cz.at[z], cz.at[z], s_cz.at[s], r_cz.at[s], at_z(zpeer(s)))

    xz[z] = pack(own)

    pl.semaphore_wait(barrier, (nz - 1) + (nx - 1) + (ny - 1) + 1)

    loop(1, nz, lambda s: cz_copy(s).start())

    in_gh = copy(gh_hbm, ghs.at[pl.ds(0, POS)], s_in2.at[0], r_in2.at[0], sibling)
    in_r = copy(r_hbm, rs, s_in2.at[1], r_in2.at[1], sibling)
    in_w = copy(w_hbm, ws, s_in2.at[2], r_in2.at[2], sibling)
    for one in (in_r, in_gh, in_w):
        one.start()


    def xz_copy(s):
        return copy(xz.at[z], xz.at[z], s_xz.at[s], r_xz.at[s], at_z(zpeer(s)))


    load_r.wait()
    load_err.wait()
    rh, rl = split2(r_ref[...])
    four = jnp.concatenate(
        [jnp.concatenate([rh, rh], axis=1), jnp.concatenate([rl, rl], axis=1)], axis=0
    )
    for q in range(nxk):
        eh, el = split2(err_ref[:, q].reshape(ch, 128))
        rows = jnp.concatenate([eh, el], axis=1)
        if ch < 256:
            rows = jnp.concatenate([rows, jnp.zeros((256 - ch, 256), BF16)], axis=0)
        e = dot(four, rows, NT)
        e = e[0:32] + e[32:64]
        for rg in range(4):
            for part in range(2):
                eg[q // 2, q % 2, 2 * rg + part] = e[8 * rg : 8 * rg + 8, 128 * part : 128 * part + 128]

    es_copy = copy(eg.at[:, 1 - k], es, s_es.at[0], r_es.at[0], sibling)
    es_copy.start()

    ghp[POS:, :] = jnp.zeros((LP - POS, 128), BF16)
    ghs[POS:, :] = jnp.zeros((LP - POS, 128), BF16)

    load_gh.wait()
    in_gh.wait_recv()
    in_r.wait_recv()
    sh, sl = split2(rs[...])
    both = jnp.concatenate([ghp[...], ghs[...]], axis=1)
    g = dot(
        jnp.concatenate([rh, sh, rl, sl], axis=1), jnp.concatenate([both, both], axis=1), NT
    )
    for rg in range(4):
        for j in range(5):
            gg[rg // 2, (rg % 2) * 5 + j] = g[8 * rg : 8 * rg + 8, 128 * j : 128 * j + 128]

    es_copy.wait_recv()

    def chip_sum(xx):
        cs[xx, 0, 0:8] = eg[xx, k] + es[xx]
        cs[xx, 0, 8:18] = gg[k]

    loop(0, nx, chip_sum)
    cs[x, 1] = cs[x, 0]

    def cs_copy(s):
        xx = lax.rem(x + s, nx)
        return copy(cs.at[xx, 0], cs.at[x, 1], s_cs.at[s], r_cs.at[s], at_x(xx))

    loop(1, nx, lambda s: cs_copy(s).start())

    load_w.wait()
    in_w.wait_recv()
    wf[:, :, :, :, 0:128] = w_ref[...].astype(F32).reshape(nz, nx, 2, OWN, 128)
    wf[:, :, :, :, 128:256] = ws[...].astype(F32).reshape(nz, nx, 2, OWN, 128)

    def grad_rows(xx):
        rows = wf[:, xx, k].reshape(ch, 256).astype(BF16)
        return dot(rows, jnp.concatenate([ghp[...], ghs[...]], axis=1), NT)

    gb[0] = grad_rows(far_x).astype(BF16)
    far_right = copy(
        gb.at[0, pl.ds(0, half)], rh1.at[0], s_gx.at[0], r_gx.at[0], at_x(right_x)
    )
    far_left = copy(
        gb.at[0, pl.ds(half, half)], rh1.at[1], s_gx.at[1], r_gx.at[1], at_x(left_x)
    )
    far_right.start()
    far_left.start()
    gr[0] = grad_rows(right_x)
    gr[1] = grad_rows(left_x)
    g32[...] = grad_rows(x)

    loop(1, nx, lambda s: cs_copy(s).wait_recv())
    total = cs[0, 1]
    for q in range(1, nx):
        total = total + cs[q, 1]
    st[...] = total[0:8]
    gt[k] = total[8:18]
    gt_copy = copy(gt.at[k], gt.at[k], s_gt.at[0], r_gt.at[0], sibling)
    gt_copy.start()

    loop(1, nz, lambda s: cz_copy(s).wait_recv())
    for zz in range(nz):
        first, last = unpack(cz[zz])
        conv32[OWN * zz : OWN * zz + 16, :] = first
        conv32[OWN * zz + 16 : OWN * zz + 24, :] = last
    cvf[x, k] = conv32[...].astype(BF16)

    gt_copy.wait_recv()
    groups = []
    for rg in range(4):
        groups.append(
            jnp.concatenate([gt[rg // 2, (rg % 2) * 5 + j] for j in range(5)], axis=1)
        )
    gsplit = jnp.concatenate(split2(jnp.concatenate(groups, axis=0)), axis=0)
    conv_pad = cvf[x, k]
    if ch < 256:
        conv_pad = jnp.concatenate([conv_pad, jnp.zeros((256 - ch, LP), BF16)], axis=0)
    conv_left = dot(gsplit, conv_pad, NT)
    conv_left = conv_left[0:32] + conv_left[32:64]
    for rg in range(4):
        for part in range(2):
            st[2 * rg + part] += conv_left[8 * rg : 8 * rg + 8, 128 * part : 128 * part + 128]

    def rz_copy(s):
        zz = zpeer(s)
        return copy(st.at[pl.ds(zz * tpz, tpz)], rz.at[z], s_rz.at[s], r_rz.at[s], at_z(zz))

    loop(1, nz, lambda s: rz_copy(s).start())
    rz[z] = st[pl.ds(z * tpz, tpz)]
    loop(1, nz, lambda s: xz_copy(s).start())

    far_right.wait_recv()
    gb[1, 0:half, :] = (gr[0, 0:half, :] + rh1[0].astype(F32)).astype(BF16)
    gb[1, half:, :] = gr[0, half:, :].astype(BF16)
    near_right = copy(gb.at[1], rh2.at[0], s_gx.at[2], r_gx.at[2], at_x(right_x))
    near_right.start()
    far_left.wait_recv()
    gb[2, 0:half, :] = gr[1, 0:half, :].astype(BF16)
    gb[2, half:, :] = (gr[1, half:, :] + rh1[1].astype(F32)).astype(BF16)
    near_left = copy(gb.at[2], rh2.at[1], s_gx.at[3], r_gx.at[3], at_x(left_x))
    near_left.start()

    mine = cvf.at[x, k]
    cx_copies = [
        copy(mine, mine, s_cx.at[0], r_cx.at[0], at_x(right_x)),
        copy(mine, mine, s_cx.at[1], r_cx.at[1], at_x(left_x)),
    ]
    for s in range(2):
        cx_copies[s].start()

    sources = (x, left_x, right_x, far_x)

    def cc_copy(s):
        block = cvf.at[sources[s], k]
        return copy(block, block, s_cc.at[s], r_cc.at[s], sibling)

    cc_copy(0).start()

    loop(1, nz, lambda s: rz_copy(s).wait_recv())
    total = rz[0]
    for q in range(1, nz):
        total = total + rz[q]
    ys[y] = total

    def ys_copy(s):
        return copy(ys.at[y], ys.at[y], s_ys.at[s], r_ys.at[s], at_y(lax.rem(y + s, ny)))

    loop(1, ny, lambda s: ys_copy(s).start())

    def local_grad(xx, kk):
        q = xx * 2 + kk
        part = dot(cvf[xx, kk], ghp[...], NN) + err_ref[:, q].reshape(ch, 128)
        cor[:, q] = part.reshape(nz, OWN, 128)
        chl[q, 0:ch, :] = jnp.concatenate(split2(part), axis=1)

    if ch < 256:
        chl[:, ch:, :] = jnp.zeros((nxk, 256 - ch, 256), BF16)
    loop(1, ny, lambda s: ys_copy(s).wait_recv())
    total = ys[0]
    for q in range(1, ny):
        total = total + ys[q]
    ll[k, z, x] = total

    def lx_copy(s):
        own = ll.at[k, z, x]
        return copy(own, own, s_lx.at[s], r_lx.at[s], at_x(lax.rem(x + s, nx)))

    loop(1, nx, lambda s: lx_copy(s).start())

    local_grad(x, k)

    loop(1, nz, lambda s: xz_copy(s).wait_recv())
    xp[:, 0:128] = jnp.zeros((ch, 128), F32)
    xp[:, 128 + LP :] = jnp.zeros((ch, LX - 128 - LP), F32)
    for zz in range(nz):
        first, last = unpack(xz[zz])
        xp[OWN * zz : OWN * zz + 16, 128 : 128 + LP] = first
        xp[OWN * zz + 16 : OWN * zz + 24, 128 : 128 + LP] = last
    near_right.wait_recv()
    near_left.wait_recv()
    g32[...] += rh2[0].astype(F32) + rh2[1].astype(F32)
    pair_row = lax.broadcasted_iota(jnp.int32, (OWN, 7 * OWN), 0)
    pair_lane = lax.broadcasted_iota(jnp.int32, (OWN, 7 * OWN), 1)
    diagonal = lax.rem(pair_lane, OWN) == pair_row
    tap_row = lax.broadcasted_iota(jnp.int32, (8, 7 * OWN), 0)

    def kernel_terms(zz):
        rows = pl.ds(pl.multiple_of(zz * OWN, 8), OWN)
        maps = jnp.concatenate(shifted(xp[rows, :]), axis=0).astype(BF16)
        gt = g32[rows, :]
        moved = [pltpu.roll(gt * mk[b : b + 1, :], 32 + b - 3, 1) for b in range(7)]
        hi, lo = split2(jnp.concatenate(moved, axis=0))
        pairs = dot(hi, maps, NT) + dot(lo, maps, NT)
        out = jnp.zeros((8, 7 * OWN), F32)
        for b in range(7):
            block = jnp.where(diagonal, pairs[OWN * b : OWN * (b + 1)], 0.0)
            one = jnp.sum(block, axis=0, keepdims=True)
            out = jnp.where(tap_row == b, one, out)
        kgt[zz] = jnp.concatenate([out, jnp.zeros((8, 256 - 7 * OWN), F32)], axis=1)

    loop(0, nz, kernel_terms, 2)

    def rk_copy(s):
        zz = zpeer(s)
        return copy(kgt.at[zz], rk.at[z], s_rk.at[s], r_rk.at[s], at_z(zz))

    loop(1, nz, lambda s: rk_copy(s).start())
    rk[z] = kgt[z]

    def lx_wait(s):
        got = ll.at[k, z, lax.rem(x - s + nx, nx)]
        copy(got, got, s_lx.at[s], r_lx.at[s], at_x(lax.rem(x + s, nx))).wait_recv()

    loop(1, nx, lx_wait)

    def lz_copy(s):
        own = ll.at[k, z]
        return copy(own, own, s_lz.at[s], r_lz.at[s], at_z(zpeer(s)))

    loop(1, nz, lambda s: lz_copy(s).start())

    cx_copies[0].wait_recv()
    part0 = cvf.at[left_x, k, pl.ds(0, half)]
    cx_copies.append(copy(part0, part0, s_cx.at[2], r_cx.at[2], at_x(right_x)))
    cx_copies[2].start()
    cc_copy(1).start()
    cx_copies[1].wait_recv()
    part1 = cvf.at[right_x, k, pl.ds(half, half)]
    cx_copies.append(copy(part1, part1, s_cx.at[3], r_cx.at[3], at_x(left_x)))
    cx_copies[3].start()
    cc_copy(2).start()
    local_grad(left_x, k)
    local_grad(right_x, k)

    for s in range(3):
        cc_copy(s).wait_recv()
        local_grad(sources[s], 1 - k)

    loop(1, nz, lambda s: rk_copy(s).wait_recv())
    total = rk[0]
    for q in range(1, nz):
        total = total + rk[q]
    yk[y] = total

    def yk_copy(s):
        return copy(yk.at[y], yk.at[y], s_yk.at[s], r_yk.at[s], at_y(lax.rem(y + s, ny)))

    loop(1, ny, lambda s: yk_copy(s).start())

    def lz_wait(s):
        got = ll.at[k, lax.rem(z - s + nz, nz)]
        copy(got, got, s_lz.at[s], r_lz.at[s], at_z(zpeer(s))).wait_recv()

    loop(1, nz, lz_wait)
    lk_copy = copy(ll.at[k], ll.at[k], s_lk.at[0], r_lk.at[0], sibling)
    lk_copy.start()

    cx_copies[2].wait_recv()
    cx_copies[3].wait_recv()
    cc_copy(3).start()
    local_grad(far_x, k)

    lk_copy.wait_recv()

    def left_of(q):
        rows = []
        for rg in range(4):
            tiles = [ll[q % 2, t // tpz, q // 2, t % tpz] for t in (2 * rg, 2 * rg + 1)]
            rows.append(jnp.concatenate(tiles, axis=1))
        return jnp.concatenate(rows, axis=0)

    lefts = [left_of(q) for q in range(nxk)]
    wide3 = split3(jnp.concatenate(lefts, axis=1))
    stack3 = jnp.concatenate(wide3, axis=0)
    gram = None
    for part in wide3:
        term = dot(stack3, part, NT)
        term = term[0:32] + term[32:64] + term[64:96]
        gram = term if gram is None else gram + term
    for q in range(nxk):
        lsn[:, q] = lefts[q].T[0:ch].reshape(nz, OWN, RANK)
    natural = lsn[...].reshape(channels, RANK).T
    nh, nm, nl = split3(natural)
    ls4[...] = jnp.concatenate([nh, nm, nh, nm], axis=0).T
    ls4_store = pltpu.make_async_copy(ls4, ls4_out, s_in.at[7])
    ls4_store.start()

    cc_copy(3).wait_recv()
    local_grad(far_x, 1 - k)
    cor_store = pltpu.make_async_copy(cor, cor_out, s_in.at[6])
    cor_store.start()

    right = None
    for q in range(nxk):
        term = dot(jnp.concatenate(split2(lefts[q]), axis=0), chl[q], NN)
        right = term if q == 0 else right + term
    right = right[0:32] + right[32:64]
    rp[y] = right[:, 0:128] + right[:, 128:256]

    def rp_copy(s):
        return copy(rp.at[y], rp.at[y], s_rp.at[s], r_rp.at[s], at_y(lax.rem(y + s, ny)))

    loop(1, ny, lambda s: rp_copy(s).start())

    row_id = lax.broadcasted_iota(jnp.int32, (RANK, RANK), 0)
    lane_id = lax.broadcasted_iota(jnp.int32, (RANK, RANK), 1)
    same = row_id == lane_id
    aug = jnp.concatenate([gram, same.astype(F32)], axis=1)
    row_col = lax.broadcasted_iota(jnp.int32, (RANK, 2 * RANK), 0)

    def full(v):
        return jnp.broadcast_to(v, (RANK, 2 * RANK))

    for i in range(0, RANK, 2):
        c0 = full(aug[:, i : i + 1])
        c1 = full(aug[:, i + 1 : i + 2])
        r0 = full(aug[i : i + 1, :])
        r1 = full(aug[i + 1 : i + 2, :])
        p00 = full(c0[i : i + 1, :])
        p01 = full(c1[i : i + 1, :])
        p11 = full(c1[i + 1 : i + 2, :])
        inv = 1.0 / (p00 * p11 - p01 * p01)
        u0 = (p11 * c0 - p01 * c1) * inv
        u1 = (p00 * c1 - p01 * c0) * inv
        u0 = jnp.where(row_col > i + 1, u0, jnp.where(row_col == i + 1, p01 / p00, 0.0))
        u1 = jnp.where(row_col > i + 1, u1, 0.0)
        aug = aug - u0 * r0 - u1 * r1
    diag = jnp.sum(jnp.where(same, aug[:, 0:RANK], 0.0), axis=1, keepdims=True)
    scale = lax.rsqrt(diag)
    scale = scale * (1.5 - 0.5 * diag * scale * scale)
    linv = aug[:, RANK:] * scale
    ih, im, il = split3(linv)
    left[...] = dot(
        jnp.concatenate([ih, ih, ih, im, im, il], axis=1),
        jnp.concatenate([nh, nm, nl, nh, nm, nh], axis=0),
        NN,
    )
    left_store = pltpu.make_async_copy(left, left_out, s_in.at[8])
    left_store.start()

    inverse = dot(linv.T, linv, NN, HIGH) * (1.0 / workers)
    ah, am, al = split3(jnp.concatenate([linv, inverse], axis=0))
    final_left = jnp.concatenate([ah, ah, ah, am, am, al], axis=1)

    loop(1, ny, lambda s: rp_copy(s).wait_recv())
    total = rp[0]
    for q in range(1, ny):
        total = total + rp[q]
    th, tm, tl = split3(total)
    solved = dot(final_left, jnp.concatenate([th, tm, tl, th, tm, th], axis=0), NN)
    right_out[...] = solved[0:RANK]
    wh, wl = split2(solved[RANK:])
    w_out[...] = jnp.concatenate([wh, wh, wl, wl], axis=0)

    loop(1, ny, lambda s: yk_copy(s).wait_recv())
    total = yk[0]
    for q in range(1, ny):
        total = total + yk[q]
    for a in range(7):
        kg_out[a] = total[0:7, OWN * a : OWN * (a + 1)]

    for one in (cor_store, ls4_store, left_store):
        one.wait()
    loop(1, nz, lambda s: cz_copy(s).wait_send())
    loop(1, nz, lambda s: xz_copy(s).wait_send())
    es_copy.wait_send()
    for one in (in_r, in_gh, in_w):
        one.wait_send()
    loop(1, nx, lambda s: cs_copy(s).wait_send())
    gt_copy.wait_send()
    loop(1, nz, lambda s: rz_copy(s).wait_send())
    loop(1, ny, lambda s: ys_copy(s).wait_send())
    loop(1, nx, lambda s: lx_copy(s).wait_send())
    loop(1, nz, lambda s: lz_copy(s).wait_send())
    lk_copy.wait_send()
    loop(1, ny, lambda s: rp_copy(s).wait_send())
    loop(1, nz, lambda s: rk_copy(s).wait_send())
    loop(1, ny, lambda s: yk_copy(s).wait_send())
    for s in range(4):
        cx_copies[s].wait_send()
        cc_copy(s).wait_send()
    for one in (far_right, far_left, near_right, near_left):
        one.wait_send()


def finish(kg_ref, left_ref, right_ref, w_ref, ls_ref, cor_ref, kg_out, left_out, right_out, err_out):
    kg_out[...] = kg_ref[...]
    left_out[...] = left_ref[...]
    right_out[...] = right_ref[...]
    approx = dot(ls_ref[...], w_ref[...], NN)
    err_out[...] = cor_ref[...] - approx.reshape(cor_ref.shape)


def on_device(ny, nz, nx, block_input, depth_kernel, w_expand, grad_hidden, error_old, right_init):
    nxk = 2 * nx
    ch = OWN * nz
    channels = nz * nxk * OWN
    tpz = 8 // nz
    hid = right_init.shape[0]
    vmem = pltpu.VMEM
    scratch = [
        vmem((SIDE, SIDE, OWN), BF16),
        vmem((7, 7, channels), F32),
        vmem((channels, 128), BF16),
        vmem((nz, nxk, OWN, 128), F32),
        vmem((RANK, 128), F32),
        vmem((LP, 128), BF16),
        vmem((LP, 128), BF16),
        vmem((channels, 128), BF16),
        vmem((RANK, 128), F32),
        vmem((nz, nx, 2, OWN, 256), F32),
        vmem((LP, OWN), F32),
        vmem((OWN, LX), F32),
        vmem((OWN, LP), F32),
        vmem((nz, 16, LX), BF16),
        vmem((nz, 16, LX), BF16),
        vmem((ch, LX), F32),
        vmem((8, LP), F32),
        vmem((64, channels), F32),
        vmem((OWN, 64), F32),
        vmem((ch, LP), F32),
        vmem((nx, 2, ch, LP), BF16),
        vmem((2, ch, LP), F32),
        vmem((3, ch, LP), BF16),
        vmem((2, ch // 2, LP), BF16),
        vmem((2, ch, LP), BF16),
        vmem((ch, LP), F32),
        vmem((nx, 2, 8, 8, 128), F32),
        vmem((2, 10, 8, 128), F32),
        vmem((nx, 8, 8, 128), F32),
        vmem((nx, 2, 18, 8, 128), F32),
        vmem((2, 10, 8, 128), F32),
        vmem((8, 8, 128), F32),
        vmem((nz, tpz, 8, 128), F32),
        vmem((ny, tpz, 8, 128), F32),
        vmem((2, nz, nx, tpz, 8, 128), F32),
        vmem((nxk, 256, 256), BF16),
        vmem((ny, RANK, 128), F32),
        vmem((nz, 8, 256), F32),
        vmem((nz, 8, 256), F32),
        vmem((ny, 8, 256), F32),
        vmem((nz, nxk, OWN, RANK), F32),
        vmem((channels, 4 * RANK), BF16),
        vmem((nz, nxk, OWN, 128), F32),
        vmem((RANK, channels), F32),
    ]
    sems = [pltpu.SemaphoreType.DMA((9,))]
    for count in (nz, nz, 2, nx, 1, nz, ny, nx, nz, 1, ny, nz, ny, 4, 4, 4, 4):
        sems += [pltpu.SemaphoreType.DMA((count,))] * 2
    spec = pl.BlockSpec(memory_space=pltpu.VMEM)
    far = pl.BlockSpec(memory_space=pl.ANY)
    cor_shape = jax.ShapeDtypeStruct((nz, nxk, OWN, 128), F32)
    mids = (
        jax.ShapeDtypeStruct((7, 7, OWN), F32),
        jax.ShapeDtypeStruct((RANK, channels), F32),
        jax.ShapeDtypeStruct((RANK, 128), F32),
        jax.ShapeDtypeStruct((4 * RANK, 128), BF16),
        jax.ShapeDtypeStruct((channels, 4 * RANK), BF16),
        cor_shape,
    )
    parts = pl.pallas_call(
        functools.partial(kernel, ny, nz, nx),
        out_shape=mids,
        in_specs=[pl.BlockSpec(memory_space=pl.ANY)] * 6,
        out_specs=(spec, far, spec, spec, far, far),
        scratch_shapes=scratch + sems,
        compiler_params=pltpu.CompilerParams(
            collective_id=0, has_side_effects=True, vmem_limit_bytes=60 * 1024 * 1024
        ),
        cost_estimate=pl.CostEstimate(
            flops=600_000_000, bytes_accessed=4_000_000, transcendentals=0
        ),
    )(
        block_input.reshape(SIDE, SIDE, OWN),
        depth_kernel,
        w_expand,
        grad_hidden.reshape(POS, 128),
        error_old.reshape(nz, nxk, OWN, 128),
        right_init.T,
    )
    kg, left, right, err = pl.pallas_call(
        finish,
        out_shape=mids[0:3] + (cor_shape,),
        in_specs=[spec] * 6,
        out_specs=(spec,) * 4,
        compiler_params=pltpu.CompilerParams(vmem_limit_bytes=60 * 1024 * 1024),
        cost_estimate=pl.CostEstimate(
            flops=60_000_000, bytes_accessed=2_500_000, transcendentals=0
        ),
    )(*parts)
    return (
        kg,
        left.T,
        right.T,
        err.reshape(1, channels, 128),
    )


def solution(mesh, nx=NX):
    ny = mesh.shape["outer"]
    nz = mesh.shape["chip"] // (2 * nx)
    placed = (
        P("outer", None, None, "chip"),
        P(),
        P(None, "chip"),
        P("outer", None, None, "chip"),
        P("outer", None, "chip"),
        P("chip", None),
    )
    return jax.shard_map(
        functools.partial(on_device, ny, nz, nx),
        mesh=mesh,
        in_specs=placed,
        out_specs=(P(None, None, "chip"), P(), P("chip", None), P("outer", None, "chip")),
        check_vma=False,
    )
```

```python
import functools

import jax
import jax.numpy as jnp
from jax import lax
from jax.experimental import pallas as pl
from jax.experimental.pallas import tpu as pltpu
from jax.sharding import PartitionSpec as P

F32 = jnp.float32
BF16 = jnp.bfloat16
HIGH = lax.Precision.HIGHEST
MESH = pl.DeviceIdType.MESH

NX = 4
SIDE = 24
POS = SIDE * SIDE
LP = 640
LX = 896
OWN = 24
RANK = 32


def dot(a, b, dims, precision=None):
    return lax.dot_general(a, b, (dims, ((), ())), precision=precision, preferred_element_type=F32)


NN = ((1,), (0,))
NT = ((1,), (1,))
TN = ((0,), (0,))


def loop(lo, hi, body, unroll=1):
    def step(i, carry):
        body(i)
        return carry

    lax.fori_loop(lo, hi, step, 0, unroll=unroll)


def split2(v):
    hi = v.astype(BF16)
    return hi, (v - hi.astype(F32)).astype(BF16)


def split3(v):
    hi = v.astype(BF16)
    rest = v - hi.astype(F32)
    mid = rest.astype(BF16)
    return hi, mid, (rest - mid.astype(F32)).astype(BF16)


def kernel(
    ny, nz, nx,
    x_hbm, k_hbm, w_hbm, gh_hbm, err_hbm, r_hbm,
    kg_out, left_out, right_out, w_out, ls4_out, cor_out,
    x_ref, k_ref, w_ref, err_ref, r_ref,
    ghp, ghs, ght, ws, rs, wf, x2, xo, conv24, cz, xz, xp, mk, kflat, kt, cvf, gr, gb, rh1, rh2, g32,
    eg, gg, es, cs, gt, st, rz, ys, ll, chl, rp, kgt, rk, yk, lsn, ls4, cor, left,
    s_in,
    s_cz, r_cz, s_xz, r_xz, s_es, r_es, s_cs, r_cs, s_gt, r_gt, s_rz, r_rz, s_ys, r_ys, s_lx, r_lx, s_lz, r_lz,
    s_lk, r_lk, s_rp, r_rp, s_rk, r_rk, s_yk, r_yk, s_in2, r_in2, s_gx, r_gx, s_cx, r_cx, s_cc, r_cc,
):
    nxk = 2 * nx
    ch = OWN * nz
    channels = ch * nxk
    tpz = 8 // nz
    half = ch // 2
    top = 16 * nz
    workers = ny
    y = lax.axis_index("outer")
    chip = lax.axis_index("chip")
    z = chip // nxk
    xk = lax.rem(chip, nxk)
    x = xk // 2
    k = lax.rem(xk, 2)

    def zpeer(s):
        return lax.rem(z + s, nz)

    def at_z(zz):
        return (y, zz * nxk + xk)

    def at_x(xx):
        return (y, z * nxk + xx * 2 + k)

    right_x = lax.rem(x + 1, nx)
    left_x = lax.rem(x + nx - 1, nx)
    far_x = lax.rem(x + 2, nx)

    def at_y(yy):
        return (yy, chip)

    sibling = (y, z * nxk + x * 2 + (1 - k))

    def copy(src, dst, ssem, rsem, dev):
        return pltpu.make_async_remote_copy(
            src_ref=src, dst_ref=dst, send_sem=ssem, recv_sem=rsem,
            device_id=dev, device_id_type=MESH,
        )

    def slots(v):
        return jnp.concatenate(
            [v[:, 0:16].reshape(top, v.shape[2]), v[:, 16:24].reshape(ch - top, v.shape[2])], axis=0
        )

    def natural_rows(v):
        return jnp.concatenate(
            [v[0:top].reshape(nz, 16, v.shape[1]), v[top:ch].reshape(nz, 8, v.shape[1])], axis=1
        )

    load_x = pltpu.make_async_copy(x_hbm, x_ref, s_in.at[0])
    load_r = pltpu.make_async_copy(r_hbm, r_ref, s_in.at[1])
    load_err = pltpu.make_async_copy(err_hbm, err_ref, s_in.at[2])
    load_gh = pltpu.make_async_copy(gh_hbm, ghp.at[pl.ds(0, POS)], s_in.at[3])
    load_w = pltpu.make_async_copy(w_hbm, w_ref, s_in.at[4])
    load_k = pltpu.make_async_copy(k_hbm, k_ref, s_in.at[5])
    for load in (load_x, load_r, load_err, load_gh, load_w, load_k):
        load.start()

    barrier = pltpu.get_barrier_semaphore()

    def greet(dev):
        pl.semaphore_signal(barrier, inc=1, device_id=dev, device_id_type=MESH)

    loop(1, nz, lambda s: greet(at_z(zpeer(s))))
    loop(1, nx, lambda s: greet(at_x(lax.rem(x + s, nx))))
    greet(sibling)
    loop(1, ny, lambda s: greet(at_y(lax.rem(y + s, ny))))

    x2[POS:, :] = jnp.zeros((LP - POS, OWN), F32)
    load_x.wait()
    for i in range(SIDE):
        x2[SIDE * i : SIDE * (i + 1), :] = x_ref[i].astype(F32)
    eye = (
        lax.broadcasted_iota(jnp.int32, (32, OWN), 0)
        == lax.broadcasted_iota(jnp.int32, (32, OWN), 1)
    )
    own = dot(eye.astype(F32).astype(BF16), x2[...].astype(BF16), NT)[0:OWN]
    xo[:, 0:128] = jnp.zeros((OWN, 128), F32)
    xo[:, 128 : 128 + LP] = own
    xo[:, 128 + LP :] = jnp.zeros((OWN, LX - 128 - LP), F32)
    load_k.wait()
    for a in range(7):
        kflat[8 * a : 8 * a + 7, :] = k_ref[a]
        kflat[8 * a + 7 : 8 * a + 8, :] = jnp.zeros((1, channels), F32)
    kflat[56:64, :] = jnp.zeros((8, channels), F32)
    row = lax.broadcasted_iota(jnp.int32, (OWN, channels), 0)
    lane = lax.broadcasted_iota(jnp.int32, (OWN, channels), 1)
    pick = (lane - row == chip * OWN).astype(F32).astype(BF16)
    three = jnp.concatenate(split3(kflat[...]), axis=0)
    taps3 = dot(pick, three, NT)
    kt[...] = taps3[:, 0:64] + taps3[:, 64:128] + taps3[:, 128:192]
    pos = lax.broadcasted_iota(jnp.int32, (8, LP), 1)
    col = lax.rem(pos, SIDE) + lax.broadcasted_iota(jnp.int32, (8, LP), 0) - 3
    mk[...] = ((col >= 0) & (col < SIDE) & (pos < POS)).astype(F32)

    def shifted(v):
        return [pltpu.roll(v, LX - (96 + SIDE * (a - 3)), 1)[:, 0:LP] for a in range(7)]

    for t in range(OWN // 8):
        rows = slice(8 * t, 8 * t + 8)
        taps = kt[rows, :]
        moved = shifted(xo[rows, :])
        out = None
        for b in range(7):
            part = None
            for a in range(7):
                term = taps[:, 8 * a + b : 8 * a + b + 1] * moved[a]
                part = term if a == 0 else part + term
            part = pltpu.roll(part, LP - (32 + b - 3), 1) * mk[b : b + 1, :]
            out = part if b == 0 else out + part
        conv24[rows, :] = out

    lane_x = lax.broadcasted_iota(jnp.int32, (16, LX), 1)

    def pack(v):
        wide = jnp.concatenate([v, jnp.zeros((OWN, LX - LP), F32)], axis=1)
        last = wide[16:24]
        early = jnp.where(lane_x[0:8] < POS // 2, last, 0.0)
        late = jnp.where(lane_x[0:8] < POS // 2, 0.0, last)
        tail = jnp.concatenate(
            [pltpu.roll(early, POS, 1), pltpu.roll(late, POS // 2, 1)], axis=0
        )
        return (wide[0:16] + tail).astype(BF16)

    def unpack(v):
        v = v.astype(F32)
        early = pltpu.roll(v[0:8], LX - POS, 1)
        late = pltpu.roll(v[8:16], LX - POS // 2, 1)
        last = jnp.where(
            lane_x[0:8] < POS // 2, early, jnp.where(lane_x[0:8] < POS, late, 0.0)
        )
        return jnp.where(lane_x < POS, v, 0.0)[:, 0:LP], last[:, 0:LP]

    cz[z] = pack(conv24[...])

    def cz_copy(s):
        return copy(cz.at[z], cz.at[z], s_cz.at[s], r_cz.at[s], at_z(zpeer(s)))

    xz[z] = pack(own)

    pl.semaphore_wait(barrier, (nz - 1) + (nx - 1) + (ny - 1) + 1)

    loop(1, nz, lambda s: cz_copy(s).start())

    in_gh = copy(gh_hbm, ghs.at[pl.ds(0, POS)], s_in2.at[0], r_in2.at[0], sibling)
    in_r = copy(r_hbm, rs, s_in2.at[1], r_in2.at[1], sibling)
    in_w = copy(w_hbm, ws, s_in2.at[2], r_in2.at[2], sibling)
    for one in (in_r, in_gh, in_w):
        one.start()


    def xz_copy(s):
        return copy(xz.at[z], xz.at[z], s_xz.at[s], r_xz.at[s], at_z(zpeer(s)))


    load_r.wait()
    load_err.wait()
    rh, rl = split2(r_ref[...])
    four = jnp.concatenate(
        [jnp.concatenate([rh, rh], axis=1), jnp.concatenate([rl, rl], axis=1)], axis=0
    )
    for q in range(nxk):
        eh, el = split2(slots(err_ref[:, q]))
        rows = jnp.concatenate([eh, el], axis=1)
        if ch < 256:
            rows = jnp.concatenate([rows, jnp.zeros((256 - ch, 256), BF16)], axis=0)
        e = dot(four, rows, NT)
        e = e[0:32] + e[32:64]
        for rg in range(4):
            for part in range(2):
                eg[q // 2, q % 2, 2 * rg + part] = e[8 * rg : 8 * rg + 8, 128 * part : 128 * part + 128]

    es_copy = copy(eg.at[:, 1 - k], es, s_es.at[0], r_es.at[0], sibling)
    es_copy.start()

    ghp[POS:, :] = jnp.zeros((LP - POS, 128), BF16)
    ghs[POS:, :] = jnp.zeros((LP - POS, 128), BF16)

    load_gh.wait()
    halves_of = jnp.concatenate([ghp[0 : POS // 2, :], ghp[POS // 2 : POS, :]], axis=1)
    ght[...] = jnp.concatenate(
        [
            jnp.zeros((64, 256), BF16),
            halves_of,
            jnp.zeros((LX - 512 - 64 - POS // 2, 256), BF16),
        ],
        axis=0,
    )
    in_gh.wait_recv()
    in_r.wait_recv()
    sh, sl = split2(rs[...])
    both = jnp.concatenate([ghp[...], ghs[...]], axis=1)
    g = dot(
        jnp.concatenate([rh, sh, rl, sl], axis=1), jnp.concatenate([both, both], axis=1), NT
    )
    for rg in range(4):
        for j in range(5):
            gg[rg // 2, (rg % 2) * 5 + j] = g[8 * rg : 8 * rg + 8, 128 * j : 128 * j + 128]

    es_copy.wait_recv()

    def chip_sum(xx):
        cs[xx, 0, 0:8] = eg[xx, k] + es[xx]
        cs[xx, 0, 8:18] = gg[k]

    loop(0, nx, chip_sum)
    cs[x, 1] = cs[x, 0]

    def cs_copy(s):
        xx = lax.rem(x + s, nx)
        return copy(cs.at[xx, 0], cs.at[x, 1], s_cs.at[s], r_cs.at[s], at_x(xx))

    loop(1, nx, lambda s: cs_copy(s).start())

    load_w.wait()
    in_w.wait_recv()
    wf[:, :, :, :, 0:128] = w_ref[...].astype(F32).reshape(nz, nx, 2, OWN, 128)
    wf[:, :, :, :, 128:256] = ws[...].astype(F32).reshape(nz, nx, 2, OWN, 128)

    def grad_rows(xx):
        rows = wf[:, xx, k].reshape(ch, 256).astype(BF16)
        return dot(rows, jnp.concatenate([ghp[...], ghs[...]], axis=1), NT)

    gb[0] = grad_rows(far_x).astype(BF16)
    far_right = copy(
        gb.at[0, pl.ds(0, half)], rh1.at[0], s_gx.at[0], r_gx.at[0], at_x(right_x)
    )
    far_left = copy(
        gb.at[0, pl.ds(half, half)], rh1.at[1], s_gx.at[1], r_gx.at[1], at_x(left_x)
    )
    far_right.start()
    far_left.start()
    gr[0] = grad_rows(right_x)
    gr[1] = grad_rows(left_x)
    g32[...] = grad_rows(x)

    loop(1, nx, lambda s: cs_copy(s).wait_recv())
    total = cs[0, 1]
    for q in range(1, nx):
        total = total + cs[q, 1]
    st[...] = total[0:8]
    gt[k] = total[8:18]
    gt_copy = copy(gt.at[k], gt.at[k], s_gt.at[0], r_gt.at[0], sibling)
    gt_copy.start()

    loop(1, nz, lambda s: cz_copy(s).wait_recv())
    cvf[x, k] = cz[...]

    gt_copy.wait_recv()
    groups = []
    for rg in range(4):
        groups.append(
            jnp.concatenate([gt[rg // 2, (rg % 2) * 5 + j] for j in range(5)], axis=1)
        )
    gfull = jnp.concatenate(groups, axis=0)
    lane_g = lax.broadcasted_iota(jnp.int32, (32, LP), 1)
    inside = (lane_g >= 64) & (lane_g < 64 + POS // 2)
    glow = jnp.where(inside, pltpu.roll(gfull, 64, 1), 0.0)[:, 0 : LX - 512]
    ghigh = jnp.where(inside, pltpu.roll(gfull, LP + 64 - POS // 2, 1), 0.0)[:, 0 : LX - 512]
    packed = cz[...]
    halves = packed[:, :, 512:].astype(F32)
    conv_top = dot(
        jnp.concatenate(split2(gfull), axis=0), packed[:, :, 0:LP].reshape(top, LP), NT
    )
    conv_last = None
    for part, rows in ((glow, halves[:, 0:8]), (ghigh, halves[:, 8:16])):
        rows = rows.reshape(ch - top, LX - 512).astype(BF16)
        term = dot(jnp.concatenate(split2(part), axis=0), rows, NT)
        conv_last = term if conv_last is None else conv_last + term
    conv_left = jnp.concatenate(
        [
            conv_top[0:32] + conv_top[32:64],
            conv_last[0:32] + conv_last[32:64],
            jnp.zeros((32, 256 - ch), F32),
        ],
        axis=1,
    )
    for rg in range(4):
        for part in range(2):
            st[2 * rg + part] += conv_left[8 * rg : 8 * rg + 8, 128 * part : 128 * part + 128]

    def rz_copy(s):
        zz = zpeer(s)
        return copy(st.at[pl.ds(zz * tpz, tpz)], rz.at[z], s_rz.at[s], r_rz.at[s], at_z(zz))

    loop(1, nz, lambda s: rz_copy(s).start())
    rz[z] = st[pl.ds(z * tpz, tpz)]
    loop(1, nz, lambda s: xz_copy(s).start())

    far_right.wait_recv()
    gb[1, 0:half, :] = (gr[0, 0:half, :] + rh1[0].astype(F32)).astype(BF16)
    gb[1, half:, :] = gr[0, half:, :].astype(BF16)
    near_right = copy(gb.at[1], rh2.at[0], s_gx.at[2], r_gx.at[2], at_x(right_x))
    near_right.start()
    far_left.wait_recv()
    gb[2, 0:half, :] = gr[1, 0:half, :].astype(BF16)
    gb[2, half:, :] = (gr[1, half:, :] + rh1[1].astype(F32)).astype(BF16)
    near_left = copy(gb.at[2], rh2.at[1], s_gx.at[3], r_gx.at[3], at_x(left_x))
    near_left.start()

    mine = cvf.at[x, k]
    cx_copies = [
        copy(mine, mine, s_cx.at[0], r_cx.at[0], at_x(right_x)),
        copy(mine, mine, s_cx.at[1], r_cx.at[1], at_x(left_x)),
    ]
    for s in range(2):
        cx_copies[s].start()

    sources = (x, left_x, right_x, far_x)

    def cc_copy(s):
        block = cvf.at[sources[s], k]
        return copy(block, block, s_cc.at[s], r_cc.at[s], sibling)

    cc_copy(0).start()

    loop(1, nz, lambda s: rz_copy(s).wait_recv())
    total = rz[0]
    for q in range(1, nz):
        total = total + rz[q]
    ys[y] = total

    def ys_copy(s):
        return copy(ys.at[y], ys.at[y], s_ys.at[s], r_ys.at[s], at_y(lax.rem(y + s, ny)))

    loop(1, ny, lambda s: ys_copy(s).start())

    def local_grad(xx, kk):
        q = xx * 2 + kk
        packed = cvf[xx, kk].reshape(top, LX)
        first = dot(packed[:, 0:LP], ghp[...], NN)
        both = dot(packed[:, 512:], ght[...], NN).reshape(nz, 16, 256)
        last = both[:, 0:8, 0:128] + both[:, 8:16, 128:256]
        part = jnp.concatenate([first, last.reshape(ch - top, 128)], axis=0) + slots(err_ref[:, q])
        cor[:, q] = natural_rows(part)
        chl[q, 0:ch, :] = jnp.concatenate(split2(part), axis=1)

    if ch < 256:
        chl[:, ch:, :] = jnp.zeros((nxk, 256 - ch, 256), BF16)
    loop(1, ny, lambda s: ys_copy(s).wait_recv())
    total = ys[0]
    for q in range(1, ny):
        total = total + ys[q]
    ll[k, z, x] = total

    def lx_copy(s):
        own = ll.at[k, z, x]
        return copy(own, own, s_lx.at[s], r_lx.at[s], at_x(lax.rem(x + s, nx)))

    loop(1, nx, lambda s: lx_copy(s).start())

    local_grad(x, k)

    loop(1, nz, lambda s: xz_copy(s).wait_recv())
    xp[:, 0:128] = jnp.zeros((ch, 128), F32)
    xp[:, 128 + LP :] = jnp.zeros((ch, LX - 128 - LP), F32)
    for zz in range(nz):
        first, last = unpack(xz[zz])
        xp[OWN * zz : OWN * zz + 16, 128 : 128 + LP] = first
        xp[OWN * zz + 16 : OWN * zz + 24, 128 : 128 + LP] = last
    near_right.wait_recv()
    near_left.wait_recv()
    g32[...] += rh2[0].astype(F32) + rh2[1].astype(F32)
    pair_row = lax.broadcasted_iota(jnp.int32, (OWN, 7 * OWN), 0)
    pair_lane = lax.broadcasted_iota(jnp.int32, (OWN, 7 * OWN), 1)
    diagonal = lax.rem(pair_lane, OWN) == pair_row
    tap_row = lax.broadcasted_iota(jnp.int32, (8, 7 * OWN), 0)

    def kernel_terms(zz):
        rows = pl.ds(pl.multiple_of(zz * OWN, 8), OWN)
        maps = jnp.concatenate(shifted(xp[rows, :]), axis=0).astype(BF16)
        gt = g32[rows, :]
        moved = [pltpu.roll(gt * mk[b : b + 1, :], 32 + b - 3, 1) for b in range(7)]
        hi, lo = split2(jnp.concatenate(moved, axis=0))
        pairs = dot(hi, maps, NT) + dot(lo, maps, NT)
        out = jnp.zeros((8, 7 * OWN), F32)
        for b in range(7):
            block = jnp.where(diagonal, pairs[OWN * b : OWN * (b + 1)], 0.0)
            one = jnp.sum(block, axis=0, keepdims=True)
            out = jnp.where(tap_row == b, one, out)
        kgt[zz] = jnp.concatenate([out, jnp.zeros((8, 256 - 7 * OWN), F32)], axis=1)

    loop(0, nz, kernel_terms, 2)

    def rk_copy(s):
        zz = zpeer(s)
        return copy(kgt.at[zz], rk.at[z], s_rk.at[s], r_rk.at[s], at_z(zz))

    loop(1, nz, lambda s: rk_copy(s).start())
    rk[z] = kgt[z]

    def lx_wait(s):
        got = ll.at[k, z, lax.rem(x - s + nx, nx)]
        copy(got, got, s_lx.at[s], r_lx.at[s], at_x(lax.rem(x + s, nx))).wait_recv()

    loop(1, nx, lx_wait)

    def lz_copy(s):
        own = ll.at[k, z]
        return copy(own, own, s_lz.at[s], r_lz.at[s], at_z(zpeer(s)))

    loop(1, nz, lambda s: lz_copy(s).start())

    cx_copies[0].wait_recv()
    part0 = cvf.at[left_x, k, pl.ds(0, nz // 2)]
    cx_copies.append(copy(part0, part0, s_cx.at[2], r_cx.at[2], at_x(right_x)))
    cx_copies[2].start()
    cc_copy(1).start()
    cx_copies[1].wait_recv()
    part1 = cvf.at[right_x, k, pl.ds(nz // 2, nz // 2)]
    cx_copies.append(copy(part1, part1, s_cx.at[3], r_cx.at[3], at_x(left_x)))
    cx_copies[3].start()
    cc_copy(2).start()
    local_grad(left_x, k)
    local_grad(right_x, k)

    for s in range(3):
        cc_copy(s).wait_recv()
        local_grad(sources[s], 1 - k)

    loop(1, nz, lambda s: rk_copy(s).wait_recv())
    total = rk[0]
    for q in range(1, nz):
        total = total + rk[q]
    yk[y] = total

    def yk_copy(s):
        return copy(yk.at[y], yk.at[y], s_yk.at[s], r_yk.at[s], at_y(lax.rem(y + s, ny)))

    loop(1, ny, lambda s: yk_copy(s).start())

    def lz_wait(s):
        got = ll.at[k, lax.rem(z - s + nz, nz)]
        copy(got, got, s_lz.at[s], r_lz.at[s], at_z(zpeer(s))).wait_recv()

    loop(1, nz, lz_wait)
    lk_copy = copy(ll.at[k], ll.at[k], s_lk.at[0], r_lk.at[0], sibling)
    lk_copy.start()

    cx_copies[2].wait_recv()
    cx_copies[3].wait_recv()
    cc_copy(3).start()
    local_grad(far_x, k)

    lk_copy.wait_recv()

    def left_of(q):
        rows = []
        for rg in range(4):
            tiles = [ll[q % 2, t // tpz, q // 2, t % tpz] for t in (2 * rg, 2 * rg + 1)]
            rows.append(jnp.concatenate(tiles, axis=1))
        return jnp.concatenate(rows, axis=0)

    lefts = [left_of(q) for q in range(nxk)]
    wide3 = split3(jnp.concatenate(lefts, axis=1))
    stack3 = jnp.concatenate(wide3, axis=0)
    gram = None
    for part in wide3:
        term = dot(stack3, part, NT)
        term = term[0:32] + term[32:64] + term[64:96]
        gram = term if gram is None else gram + term
    for q in range(nxk):
        lsn[:, q] = natural_rows(lefts[q].T)
    natural = lsn[...].reshape(channels, RANK).T
    nh, nm, nl = split3(natural)
    ls4[...] = jnp.concatenate([nh, nm, nh, nm], axis=0).T
    ls4_store = pltpu.make_async_copy(ls4, ls4_out, s_in.at[7])
    ls4_store.start()

    cc_copy(3).wait_recv()
    local_grad(far_x, 1 - k)
    cor_store = pltpu.make_async_copy(cor, cor_out, s_in.at[6])
    cor_store.start()

    right = None
    for q in range(nxk):
        term = dot(jnp.concatenate(split2(lefts[q]), axis=0), chl[q], NN)
        right = term if q == 0 else right + term
    right = right[0:32] + right[32:64]
    rp[y] = right[:, 0:128] + right[:, 128:256]

    def rp_copy(s):
        return copy(rp.at[y], rp.at[y], s_rp.at[s], r_rp.at[s], at_y(lax.rem(y + s, ny)))

    loop(1, ny, lambda s: rp_copy(s).start())

    row_id = lax.broadcasted_iota(jnp.int32, (RANK, RANK), 0)
    lane_id = lax.broadcasted_iota(jnp.int32, (RANK, RANK), 1)
    same = row_id == lane_id
    aug = jnp.concatenate([gram, same.astype(F32)], axis=1)
    row_col = lax.broadcasted_iota(jnp.int32, (RANK, 2 * RANK), 0)

    def full(v):
        return jnp.broadcast_to(v, (RANK, 2 * RANK))

    for i in range(0, RANK, 2):
        c0 = full(aug[:, i : i + 1])
        c1 = full(aug[:, i + 1 : i + 2])
        r0 = full(aug[i : i + 1, :])
        r1 = full(aug[i + 1 : i + 2, :])
        p00 = full(c0[i : i + 1, :])
        p01 = full(c1[i : i + 1, :])
        p11 = full(c1[i + 1 : i + 2, :])
        inv = 1.0 / (p00 * p11 - p01 * p01)
        u0 = (p11 * c0 - p01 * c1) * inv
        u1 = (p00 * c1 - p01 * c0) * inv
        u0 = jnp.where(row_col > i + 1, u0, jnp.where(row_col == i + 1, p01 / p00, 0.0))
        u1 = jnp.where(row_col > i + 1, u1, 0.0)
        aug = aug - u0 * r0 - u1 * r1
    diag = jnp.sum(jnp.where(same, aug[:, 0:RANK], 0.0), axis=1, keepdims=True)
    scale = lax.rsqrt(diag)
    scale = scale * (1.5 - 0.5 * diag * scale * scale)
    linv = aug[:, RANK:] * scale
    ih, im, il = split3(linv)
    left[...] = dot(
        jnp.concatenate([ih, ih, ih, im, im, il], axis=1),
        jnp.concatenate([nh, nm, nl, nh, nm, nh], axis=0),
        NN,
    )
    left_store = pltpu.make_async_copy(left, left_out, s_in.at[8])
    left_store.start()

    inverse = dot(linv.T, linv, NN, HIGH) * (1.0 / workers)
    ah, am, al = split3(jnp.concatenate([linv, inverse], axis=0))
    final_left = jnp.concatenate([ah, ah, ah, am, am, al], axis=1)

    loop(1, ny, lambda s: rp_copy(s).wait_recv())
    total = rp[0]
    for q in range(1, ny):
        total = total + rp[q]
    th, tm, tl = split3(total)
    solved = dot(final_left, jnp.concatenate([th, tm, tl, th, tm, th], axis=0), NN)
    right_out[...] = solved[0:RANK]
    wh, wl = split2(solved[RANK:])
    w_out[...] = jnp.concatenate([wh, wh, wl, wl], axis=0)

    loop(1, ny, lambda s: yk_copy(s).wait_recv())
    total = yk[0]
    for q in range(1, ny):
        total = total + yk[q]
    for a in range(7):
        kg_out[a] = total[0:7, OWN * a : OWN * (a + 1)]

    for one in (cor_store, ls4_store, left_store):
        one.wait()
    loop(1, nz, lambda s: cz_copy(s).wait_send())
    loop(1, nz, lambda s: xz_copy(s).wait_send())
    es_copy.wait_send()
    for one in (in_r, in_gh, in_w):
        one.wait_send()
    loop(1, nx, lambda s: cs_copy(s).wait_send())
    gt_copy.wait_send()
    loop(1, nz, lambda s: rz_copy(s).wait_send())
    loop(1, ny, lambda s: ys_copy(s).wait_send())
    loop(1, nx, lambda s: lx_copy(s).wait_send())
    loop(1, nz, lambda s: lz_copy(s).wait_send())
    lk_copy.wait_send()
    loop(1, ny, lambda s: rp_copy(s).wait_send())
    loop(1, nz, lambda s: rk_copy(s).wait_send())
    loop(1, ny, lambda s: yk_copy(s).wait_send())
    for s in range(4):
        cx_copies[s].wait_send()
        cc_copy(s).wait_send()
    for one in (far_right, far_left, near_right, near_left):
        one.wait_send()


def finish(
    kg_hbm, left_hbm, right_hbm, w_hbm, ls_hbm, cor_hbm, kg_out, left_out, right_out, err_out,
    w_ref, ls_ref, cor_ref, load_sems, store_sems, small_sems,
):
    count = load_sems.shape[0] - 1
    width = cor_ref.shape[0] // count
    rows = ls_ref.shape[0] // count
    small = [
        pltpu.make_async_copy(a, b, small_sems.at[i])
        for i, (a, b) in enumerate(((kg_hbm, kg_out), (left_hbm, left_out), (right_hbm, right_out)))
    ]
    w_load = pltpu.make_async_copy(w_hbm, w_ref, load_sems.at[count, 0])
    w_load.start()
    loads = []
    for i in range(count):
        at, lines = pl.ds(i * width, width), pl.ds(i * rows, rows)
        loads.append(
            (
                pltpu.make_async_copy(ls_hbm.at[lines], ls_ref.at[lines], load_sems.at[i, 0]),
                pltpu.make_async_copy(cor_hbm.at[at], cor_ref.at[at], load_sems.at[i, 1]),
            )
        )
        for one in loads[i]:
            one.start()
    for one in small:
        one.start()
    w_load.wait()
    stores = []
    for i in range(count):
        for one in loads[i]:
            one.wait()
        at, lines = slice(i * width, (i + 1) * width), slice(i * rows, (i + 1) * rows)
        approx = dot(ls_ref[lines, :], w_ref[...], NN)
        cor_ref[at] = cor_ref[at] - approx.reshape((width,) + cor_ref.shape[1:])
        part = pl.ds(i * width, width)
        stores.append(
            pltpu.make_async_copy(cor_ref.at[part], err_out.at[part], store_sems.at[i])
        )
        stores[i].start()
    for one in stores + small:
        one.wait()


def on_device(ny, nz, nx, block_input, depth_kernel, w_expand, grad_hidden, error_old, right_init):
    nxk = 2 * nx
    ch = OWN * nz
    channels = nz * nxk * OWN
    tpz = 8 // nz
    hid = right_init.shape[0]
    vmem = pltpu.VMEM
    scratch = [
        vmem((SIDE, SIDE, OWN), BF16),
        vmem((7, 7, channels), F32),
        vmem((channels, 128), BF16),
        vmem((nz, nxk, OWN, 128), F32),
        vmem((RANK, 128), F32),
        vmem((LP, 128), BF16),
        vmem((LP, 128), BF16),
        vmem((LX - 512, 256), BF16),
        vmem((channels, 128), BF16),
        vmem((RANK, 128), F32),
        vmem((nz, nx, 2, OWN, 256), F32),
        vmem((LP, OWN), F32),
        vmem((OWN, LX), F32),
        vmem((OWN, LP), F32),
        vmem((nz, 16, LX), BF16),
        vmem((nz, 16, LX), BF16),
        vmem((ch, LX), F32),
        vmem((8, LP), F32),
        vmem((64, channels), F32),
        vmem((OWN, 64), F32),
        vmem((nx, 2, nz, 16, LX), BF16),
        vmem((2, ch, LP), F32),
        vmem((3, ch, LP), BF16),
        vmem((2, ch // 2, LP), BF16),
        vmem((2, ch, LP), BF16),
        vmem((ch, LP), F32),
        vmem((nx, 2, 8, 8, 128), F32),
        vmem((2, 10, 8, 128), F32),
        vmem((nx, 8, 8, 128), F32),
        vmem((nx, 2, 18, 8, 128), F32),
        vmem((2, 10, 8, 128), F32),
        vmem((8, 8, 128), F32),
        vmem((nz, tpz, 8, 128), F32),
        vmem((ny, tpz, 8, 128), F32),
        vmem((2, nz, nx, tpz, 8, 128), F32),
        vmem((nxk, 256, 256), BF16),
        vmem((ny, RANK, 128), F32),
        vmem((nz, 8, 256), F32),
        vmem((nz, 8, 256), F32),
        vmem((ny, 8, 256), F32),
        vmem((nz, nxk, OWN, RANK), F32),
        vmem((channels, 4 * RANK), BF16),
        vmem((nz, nxk, OWN, 128), F32),
        vmem((RANK, channels), F32),
    ]
    sems = [pltpu.SemaphoreType.DMA((9,))]
    for count in (nz, nz, 2, nx, 1, nz, ny, nx, nz, 1, ny, nz, ny, 4, 4, 4, 4):
        sems += [pltpu.SemaphoreType.DMA((count,))] * 2
    spec = pl.BlockSpec(memory_space=pltpu.VMEM)
    far = pl.BlockSpec(memory_space=pl.ANY)
    cor_shape = jax.ShapeDtypeStruct((nz, nxk, OWN, 128), F32)
    mids = (
        jax.ShapeDtypeStruct((7, 7, OWN), F32),
        jax.ShapeDtypeStruct((RANK, channels), F32),
        jax.ShapeDtypeStruct((RANK, 128), F32),
        jax.ShapeDtypeStruct((4 * RANK, 128), BF16),
        jax.ShapeDtypeStruct((channels, 4 * RANK), BF16),
        cor_shape,
    )
    parts = pl.pallas_call(
        functools.partial(kernel, ny, nz, nx),
        out_shape=mids,
        in_specs=[pl.BlockSpec(memory_space=pl.ANY)] * 6,
        out_specs=(spec, far, spec, spec, far, far),
        scratch_shapes=scratch + sems,
        compiler_params=pltpu.CompilerParams(
            collective_id=0, has_side_effects=True, vmem_limit_bytes=60 * 1024 * 1024
        ),
        cost_estimate=pl.CostEstimate(
            flops=600_000_000, bytes_accessed=4_000_000, transcendentals=0
        ),
    )(
        block_input.reshape(SIDE, SIDE, OWN),
        depth_kernel,
        w_expand,
        grad_hidden.reshape(POS, 128),
        error_old.reshape(nz, nxk, OWN, 128),
        right_init.T,
    )
    steps = min(4, nz)
    kg, left, right, err = pl.pallas_call(
        finish,
        out_shape=mids[0:3] + (cor_shape,),
        in_specs=[far] * 6,
        out_specs=(far,) * 4,
        scratch_shapes=[
            vmem((4 * RANK, 128), BF16),
            vmem((channels, 4 * RANK), BF16),
            vmem((nz, nxk, OWN, 128), F32),
            pltpu.SemaphoreType.DMA((steps + 1, 2)),
            pltpu.SemaphoreType.DMA((steps,)),
            pltpu.SemaphoreType.DMA((3,)),
        ],
        compiler_params=pltpu.CompilerParams(vmem_limit_bytes=60 * 1024 * 1024),
        cost_estimate=pl.CostEstimate(
            flops=60_000_000, bytes_accessed=2_500_000, transcendentals=0
        ),
    )(*parts)
    return (
        kg,
        left.T,
        right.T,
        err.reshape(1, channels, 128),
    )


def solution(mesh, nx=NX):
    ny = mesh.shape["outer"]
    nz = mesh.shape["chip"] // (2 * nx)
    placed = (
        P("outer", None, None, "chip"),
        P(),
        P(None, "chip"),
        P("outer", None, None, "chip"),
        P("outer", None, "chip"),
        P("chip", None),
    )
    return jax.shard_map(
        functools.partial(on_device, ny, nz, nx),
        mesh=mesh,
        in_specs=placed,
        out_specs=(P(None, None, "chip"), P(), P("chip", None), P("outer", None, "chip")),
        check_vma=False,
    )
```

```python
import functools

import jax
import jax.numpy as jnp
from jax import lax
from jax.experimental import pallas as pl
from jax.experimental.pallas import tpu as pltpu
from jax.sharding import PartitionSpec as P

F32 = jnp.float32
BF16 = jnp.bfloat16
HIGH = lax.Precision.HIGHEST
MESH = pl.DeviceIdType.MESH

NX = 4
SIDE = 24
POS = SIDE * SIDE
LP = 640
LX = 896
OWN = 24
RANK = 32


def dot(a, b, dims, precision=None):
    return lax.dot_general(a, b, (dims, ((), ())), precision=precision, preferred_element_type=F32)


NN = ((1,), (0,))
NT = ((1,), (1,))
TN = ((0,), (0,))


def loop(lo, hi, body, unroll=1):
    def step(i, carry):
        body(i)
        return carry

    lax.fori_loop(lo, hi, step, 0, unroll=unroll)


def split2(v):
    hi = v.astype(BF16)
    return hi, (v - hi.astype(F32)).astype(BF16)


def split3(v):
    hi = v.astype(BF16)
    rest = v - hi.astype(F32)
    mid = rest.astype(BF16)
    return hi, mid, (rest - mid.astype(F32)).astype(BF16)


def kernel(
    ny, nz, nx,
    x_hbm, k_hbm, w_hbm, gh_hbm, err_hbm, r_hbm,
    kg_out, left_out, right_out, w_out, ls4_out, cor_out,
    x_ref, k_ref, w_ref, err_ref, r_ref,
    ghp, ghs, ght, ws, rs, wf, x2, xo, conv24, cz, xz, xp, mk, kflat, kt, cvf, gr, gb, rh1, rh2, g32,
    eg, gg, es, cs, gt, st, rz, ys, ll, chl, rp, kgt, rk, yk, lsn, ls4, cor, left,
    s_in,
    s_cz, r_cz, s_xz, r_xz, s_es, r_es, s_cs, r_cs, s_gt, r_gt, s_rz, r_rz, s_ys, r_ys, s_lx, r_lx, s_lz, r_lz,
    s_lk, r_lk, s_rp, r_rp, s_rk, r_rk, s_yk, r_yk, s_in2, r_in2, s_gx, r_gx, s_cx, r_cx, s_cc, r_cc,
):
    nxk = 2 * nx
    ch = OWN * nz
    channels = ch * nxk
    tpz = 8 // nz
    half = ch // 2
    top = 16 * nz
    workers = ny
    y = lax.axis_index("outer")
    chip = lax.axis_index("chip")
    z = chip // nxk
    xk = lax.rem(chip, nxk)
    x = xk // 2
    k = lax.rem(xk, 2)

    def zpeer(s):
        return lax.rem(z + s, nz)

    def at_z(zz):
        return (y, zz * nxk + xk)

    def at_x(xx):
        return (y, z * nxk + xx * 2 + k)

    right_x = lax.rem(x + 1, nx)
    left_x = lax.rem(x + nx - 1, nx)
    far_x = lax.rem(x + 2, nx)

    def at_y(yy):
        return (yy, chip)

    sibling = (y, z * nxk + x * 2 + (1 - k))

    def copy(src, dst, ssem, rsem, dev):
        return pltpu.make_async_remote_copy(
            src_ref=src, dst_ref=dst, send_sem=ssem, recv_sem=rsem,
            device_id=dev, device_id_type=MESH,
        )

    def slots(v):
        return jnp.concatenate(
            [v[:, 0:16].reshape(top, v.shape[2]), v[:, 16:24].reshape(ch - top, v.shape[2])], axis=0
        )

    def natural_rows(v):
        return jnp.concatenate(
            [v[0:top].reshape(nz, 16, v.shape[1]), v[top:ch].reshape(nz, 8, v.shape[1])], axis=1
        )

    load_x = pltpu.make_async_copy(x_hbm, x_ref, s_in.at[0])
    load_r = pltpu.make_async_copy(r_hbm, r_ref, s_in.at[1])
    load_err = pltpu.make_async_copy(err_hbm, err_ref, s_in.at[2])
    load_gh = pltpu.make_async_copy(gh_hbm, ghp.at[pl.ds(0, POS)], s_in.at[3])
    load_w = pltpu.make_async_copy(w_hbm, w_ref, s_in.at[4])
    load_k = pltpu.make_async_copy(k_hbm, k_ref, s_in.at[5])
    for load in (load_x, load_r, load_err, load_gh, load_w, load_k):
        load.start()

    barrier = pltpu.get_barrier_semaphore()

    def greet(dev):
        pl.semaphore_signal(barrier, inc=1, device_id=dev, device_id_type=MESH)

    loop(1, nz, lambda s: greet(at_z(zpeer(s))))
    loop(1, nx, lambda s: greet(at_x(lax.rem(x + s, nx))))
    greet(sibling)
    loop(1, ny, lambda s: greet(at_y(lax.rem(y + s, ny))))

    x2[POS:, :] = jnp.zeros((LP - POS, OWN), F32)
    load_x.wait()
    for i in range(SIDE):
        x2[SIDE * i : SIDE * (i + 1), :] = x_ref[i].astype(F32)
    eye = (
        lax.broadcasted_iota(jnp.int32, (32, OWN), 0)
        == lax.broadcasted_iota(jnp.int32, (32, OWN), 1)
    )
    own = dot(eye.astype(F32).astype(BF16), x2[...].astype(BF16), NT)[0:OWN]
    xo[:, 0:128] = jnp.zeros((OWN, 128), F32)
    xo[:, 128 : 128 + LP] = own
    xo[:, 128 + LP :] = jnp.zeros((OWN, LX - 128 - LP), F32)
    load_k.wait()
    for a in range(7):
        kflat[8 * a : 8 * a + 7, :] = k_ref[a]
        kflat[8 * a + 7 : 8 * a + 8, :] = jnp.zeros((1, channels), F32)
    kflat[56:64, :] = jnp.zeros((8, channels), F32)
    row = lax.broadcasted_iota(jnp.int32, (OWN, channels), 0)
    lane = lax.broadcasted_iota(jnp.int32, (OWN, channels), 1)
    pick = (lane - row == chip * OWN).astype(F32).astype(BF16)
    three = jnp.concatenate(split3(kflat[...]), axis=0)
    taps3 = dot(pick, three, NT)
    kt[...] = taps3[:, 0:64] + taps3[:, 64:128] + taps3[:, 128:192]
    pos = lax.broadcasted_iota(jnp.int32, (8, LP), 1)
    col = lax.rem(pos, SIDE) + lax.broadcasted_iota(jnp.int32, (8, LP), 0) - 3
    mk[...] = ((col >= 0) & (col < SIDE) & (pos < POS)).astype(F32)

    def shifted(v):
        return [pltpu.roll(v, LX - (96 + SIDE * (a - 3)), 1)[:, 0:LP] for a in range(7)]

    for t in range(OWN // 8):
        rows = slice(8 * t, 8 * t + 8)
        taps = kt[rows, :]
        moved = shifted(xo[rows, :])
        out = None
        for b in range(7):
            part = None
            for a in range(7):
                term = taps[:, 8 * a + b : 8 * a + b + 1] * moved[a]
                part = term if a == 0 else part + term
            part = pltpu.roll(part, LP - (32 + b - 3), 1) * mk[b : b + 1, :]
            out = part if b == 0 else out + part
        conv24[rows, :] = out

    lane_x = lax.broadcasted_iota(jnp.int32, (16, LX), 1)

    def pack(v):
        wide = jnp.concatenate([v, jnp.zeros((OWN, LX - LP), F32)], axis=1)
        last = wide[16:24]
        early = jnp.where(lane_x[0:8] < POS // 2, last, 0.0)
        late = jnp.where(lane_x[0:8] < POS // 2, 0.0, last)
        tail = jnp.concatenate(
            [pltpu.roll(early, POS, 1), pltpu.roll(late, POS // 2, 1)], axis=0
        )
        return (wide[0:16] + tail).astype(BF16)

    def unpack(v):
        v = v.astype(F32)
        early = pltpu.roll(v[0:8], LX - POS, 1)
        late = pltpu.roll(v[8:16], LX - POS // 2, 1)
        last = jnp.where(
            lane_x[0:8] < POS // 2, early, jnp.where(lane_x[0:8] < POS, late, 0.0)
        )
        return jnp.where(lane_x < POS, v, 0.0)[:, 0:LP], last[:, 0:LP]

    cz[z] = pack(conv24[...])

    def cz_copy(s):
        return copy(cz.at[z], cz.at[z], s_cz.at[s], r_cz.at[s], at_z(zpeer(s)))

    xz[z] = pack(own)

    pl.semaphore_wait(barrier, (nz - 1) + (nx - 1) + (ny - 1) + 1)

    loop(1, nz, lambda s: cz_copy(s).start())

    in_gh = copy(gh_hbm, ghs.at[pl.ds(0, POS)], s_in2.at[0], r_in2.at[0], sibling)
    in_r = copy(r_hbm, rs, s_in2.at[1], r_in2.at[1], sibling)
    in_w = copy(w_hbm, ws, s_in2.at[2], r_in2.at[2], sibling)
    for one in (in_r, in_gh, in_w):
        one.start()


    def xz_copy(s):
        return copy(xz.at[z], xz.at[z], s_xz.at[s], r_xz.at[s], at_z(zpeer(s)))


    load_r.wait()
    load_err.wait()
    rh, rl = split2(r_ref[...])
    four = jnp.concatenate(
        [jnp.concatenate([rh, rh], axis=1), jnp.concatenate([rl, rl], axis=1)], axis=0
    )
    for q in range(nxk):
        eh, el = split2(slots(err_ref[:, q]))
        rows = jnp.concatenate([eh, el], axis=1)
        if ch < 256:
            rows = jnp.concatenate([rows, jnp.zeros((256 - ch, 256), BF16)], axis=0)
        e = dot(four, rows, NT)
        e = e[0:32] + e[32:64]
        for rg in range(4):
            for part in range(2):
                eg[q // 2, q % 2, 2 * rg + part] = e[8 * rg : 8 * rg + 8, 128 * part : 128 * part + 128]

    es_copy = copy(eg.at[:, 1 - k], es, s_es.at[0], r_es.at[0], sibling)
    es_copy.start()

    ghp[POS:, :] = jnp.zeros((LP - POS, 128), BF16)
    ghs[POS:, :] = jnp.zeros((LP - POS, 128), BF16)

    load_gh.wait()
    halves_of = jnp.concatenate([ghp[0 : POS // 2, :], ghp[POS // 2 : POS, :]], axis=1)
    ght[...] = jnp.concatenate(
        [
            jnp.zeros((64, 256), BF16),
            halves_of,
            jnp.zeros((LX - 512 - 64 - POS // 2, 256), BF16),
        ],
        axis=0,
    )
    in_gh.wait_recv()
    in_r.wait_recv()
    sh, sl = split2(rs[...])
    both = jnp.concatenate([ghp[...], ghs[...]], axis=1)
    g = dot(
        jnp.concatenate([rh, sh, rl, sl], axis=1), jnp.concatenate([both, both], axis=1), NT
    )
    for rg in range(4):
        for j in range(5):
            gg[rg // 2, (rg % 2) * 5 + j] = g[8 * rg : 8 * rg + 8, 128 * j : 128 * j + 128]

    es_copy.wait_recv()

    def chip_sum(xx):
        cs[xx, 0, 0:8] = eg[xx, k] + es[xx]
        cs[xx, 0, 8:18] = gg[k]

    loop(0, nx, chip_sum)
    cs[x, 1] = cs[x, 0]

    def cs_copy(s):
        xx = lax.rem(x + s, nx)
        return copy(cs.at[xx, 0], cs.at[x, 1], s_cs.at[s], r_cs.at[s], at_x(xx))

    loop(1, nx, lambda s: cs_copy(s).start())

    load_w.wait()
    in_w.wait_recv()
    wf[:, :, :, :, 0:128] = w_ref[...].astype(F32).reshape(nz, nx, 2, OWN, 128)
    wf[:, :, :, :, 128:256] = ws[...].astype(F32).reshape(nz, nx, 2, OWN, 128)

    def grad_rows(xx):
        rows = wf[:, xx, k].reshape(ch, 256).astype(BF16)
        return dot(rows, jnp.concatenate([ghp[...], ghs[...]], axis=1), NT)

    gb[0] = grad_rows(far_x).astype(BF16)
    far_right = copy(
        gb.at[0, pl.ds(0, half)], rh1.at[0], s_gx.at[0], r_gx.at[0], at_x(right_x)
    )
    far_left = copy(
        gb.at[0, pl.ds(half, half)], rh1.at[1], s_gx.at[1], r_gx.at[1], at_x(left_x)
    )
    far_right.start()
    far_left.start()
    gr[0] = grad_rows(right_x)
    gr[1] = grad_rows(left_x)
    g32[...] = grad_rows(x)

    loop(1, nx, lambda s: cs_copy(s).wait_recv())
    total = cs[0, 1]
    for q in range(1, nx):
        total = total + cs[q, 1]
    st[...] = total[0:8]
    gt[k] = total[8:18]
    gt_copy = copy(gt.at[k], gt.at[k], s_gt.at[0], r_gt.at[0], sibling)
    gt_copy.start()

    loop(1, nz, lambda s: cz_copy(s).wait_recv())
    cvf[x, k] = cz[...]

    gt_copy.wait_recv()
    groups = []
    for rg in range(4):
        groups.append(
            jnp.concatenate([gt[rg // 2, (rg % 2) * 5 + j] for j in range(5)], axis=1)
        )
    gfull = jnp.concatenate(groups, axis=0)
    lane_g = lax.broadcasted_iota(jnp.int32, (32, LP), 1)
    inside = (lane_g >= 64) & (lane_g < 64 + POS // 2)
    glow = jnp.where(inside, pltpu.roll(gfull, 64, 1), 0.0)[:, 0 : LX - 512]
    ghigh = jnp.where(inside, pltpu.roll(gfull, LP + 64 - POS // 2, 1), 0.0)[:, 0 : LX - 512]
    packed = cz[...]
    halves = packed[:, :, 512:].astype(F32)
    conv_top = dot(
        jnp.concatenate(split2(gfull), axis=0), packed[:, :, 0:LP].reshape(top, LP), NT
    )
    conv_last = None
    for part, rows in ((glow, halves[:, 0:8]), (ghigh, halves[:, 8:16])):
        rows = rows.reshape(ch - top, LX - 512).astype(BF16)
        term = dot(jnp.concatenate(split2(part), axis=0), rows, NT)
        conv_last = term if conv_last is None else conv_last + term
    conv_left = jnp.concatenate(
        [
            conv_top[0:32] + conv_top[32:64],
            conv_last[0:32] + conv_last[32:64],
            jnp.zeros((32, 256 - ch), F32),
        ],
        axis=1,
    )
    for rg in range(4):
        for part in range(2):
            st[2 * rg + part] += conv_left[8 * rg : 8 * rg + 8, 128 * part : 128 * part + 128]

    def rz_copy(s):
        zz = zpeer(s)
        return copy(st.at[pl.ds(zz * tpz, tpz)], rz.at[z], s_rz.at[s], r_rz.at[s], at_z(zz))

    loop(1, nz, lambda s: rz_copy(s).start())
    rz[z] = st[pl.ds(z * tpz, tpz)]
    loop(1, nz, lambda s: xz_copy(s).start())

    far_right.wait_recv()
    gb[1, 0:half, :] = (gr[0, 0:half, :] + rh1[0].astype(F32)).astype(BF16)
    gb[1, half:, :] = gr[0, half:, :].astype(BF16)
    near_right = copy(gb.at[1], rh2.at[0], s_gx.at[2], r_gx.at[2], at_x(right_x))
    near_right.start()
    far_left.wait_recv()
    gb[2, 0:half, :] = gr[1, 0:half, :].astype(BF16)
    gb[2, half:, :] = (gr[1, half:, :] + rh1[1].astype(F32)).astype(BF16)
    near_left = copy(gb.at[2], rh2.at[1], s_gx.at[3], r_gx.at[3], at_x(left_x))
    near_left.start()

    mine = cvf.at[x, k]
    cx_copies = [
        copy(mine, mine, s_cx.at[0], r_cx.at[0], at_x(right_x)),
        copy(mine, mine, s_cx.at[1], r_cx.at[1], at_x(left_x)),
    ]
    for s in range(2):
        cx_copies[s].start()

    sources = (x, left_x, right_x, far_x)

    def cc_copy(s):
        block = cvf.at[sources[s], k]
        return copy(block, block, s_cc.at[s], r_cc.at[s], sibling)

    cc_copy(0).start()

    loop(1, nz, lambda s: rz_copy(s).wait_recv())
    total = rz[0]
    for q in range(1, nz):
        total = total + rz[q]
    ys[y] = total

    def ys_copy(s):
        return copy(ys.at[y], ys.at[y], s_ys.at[s], r_ys.at[s], at_y(lax.rem(y + s, ny)))

    loop(1, ny, lambda s: ys_copy(s).start())

    def local_grad(xx, kk):
        q = xx * 2 + kk
        packed = cvf[xx, kk].reshape(top, LX)
        first = dot(packed[:, 0:LP], ghp[...], NN)
        both = dot(packed[:, 512:], ght[...], NN).reshape(nz, 16, 256)
        last = both[:, 0:8, 0:128] + both[:, 8:16, 128:256]
        part = jnp.concatenate([first, last.reshape(ch - top, 128)], axis=0) + slots(err_ref[:, q])
        cor[:, q] = natural_rows(part)
        chl[q, 0:ch, :] = jnp.concatenate(split2(part), axis=1)

    if ch < 256:
        chl[:, ch:, :] = jnp.zeros((nxk, 256 - ch, 256), BF16)
    loop(1, ny, lambda s: ys_copy(s).wait_recv())
    total = ys[0]
    for q in range(1, ny):
        total = total + ys[q]
    ll[k, z, x] = total

    def lx_copy(s):
        own = ll.at[k, z, x]
        return copy(own, own, s_lx.at[s], r_lx.at[s], at_x(lax.rem(x + s, nx)))

    loop(1, nx, lambda s: lx_copy(s).start())

    local_grad(x, k)

    def lx_wait(s):
        got = ll.at[k, z, lax.rem(x - s + nx, nx)]
        copy(got, got, s_lx.at[s], r_lx.at[s], at_x(lax.rem(x + s, nx))).wait_recv()

    loop(1, nx, lx_wait)

    def lz_copy(s):
        own = ll.at[k, z]
        return copy(own, own, s_lz.at[s], r_lz.at[s], at_z(zpeer(s)))

    loop(1, nz, lambda s: lz_copy(s).start())

    cx_copies[0].wait_recv()
    part0 = cvf.at[left_x, k, pl.ds(0, nz // 2)]
    cx_copies.append(copy(part0, part0, s_cx.at[2], r_cx.at[2], at_x(right_x)))
    cx_copies[2].start()
    cc_copy(1).start()
    cx_copies[1].wait_recv()
    part1 = cvf.at[right_x, k, pl.ds(nz // 2, nz // 2)]
    cx_copies.append(copy(part1, part1, s_cx.at[3], r_cx.at[3], at_x(left_x)))
    cx_copies[3].start()
    cc_copy(2).start()
    local_grad(left_x, k)
    local_grad(right_x, k)

    loop(1, nz, lambda s: xz_copy(s).wait_recv())
    xp[:, 0:128] = jnp.zeros((ch, 128), F32)
    xp[:, 128 + LP :] = jnp.zeros((ch, LX - 128 - LP), F32)
    for zz in range(nz):
        first, last = unpack(xz[zz])
        xp[OWN * zz : OWN * zz + 16, 128 : 128 + LP] = first
        xp[OWN * zz + 16 : OWN * zz + 24, 128 : 128 + LP] = last
    near_right.wait_recv()
    near_left.wait_recv()
    g32[...] += rh2[0].astype(F32) + rh2[1].astype(F32)
    pair_row = lax.broadcasted_iota(jnp.int32, (OWN, 7 * OWN), 0)
    pair_lane = lax.broadcasted_iota(jnp.int32, (OWN, 7 * OWN), 1)
    diagonal = lax.rem(pair_lane, OWN) == pair_row
    tap_row = lax.broadcasted_iota(jnp.int32, (8, 7 * OWN), 0)

    def kernel_terms(zz):
        rows = pl.ds(pl.multiple_of(zz * OWN, 8), OWN)
        maps = jnp.concatenate(shifted(xp[rows, :]), axis=0).astype(BF16)
        gt = g32[rows, :]
        moved = [pltpu.roll(gt * mk[b : b + 1, :], 32 + b - 3, 1) for b in range(7)]
        hi, lo = split2(jnp.concatenate(moved, axis=0))
        pairs = dot(hi, maps, NT) + dot(lo, maps, NT)
        out = jnp.zeros((8, 7 * OWN), F32)
        for b in range(7):
            block = jnp.where(diagonal, pairs[OWN * b : OWN * (b + 1)], 0.0)
            one = jnp.sum(block, axis=0, keepdims=True)
            out = jnp.where(tap_row == b, one, out)
        kgt[zz] = jnp.concatenate([out, jnp.zeros((8, 256 - 7 * OWN), F32)], axis=1)

    loop(0, nz, kernel_terms, 2)

    def rk_copy(s):
        zz = zpeer(s)
        return copy(kgt.at[zz], rk.at[z], s_rk.at[s], r_rk.at[s], at_z(zz))

    loop(1, nz, lambda s: rk_copy(s).start())
    rk[z] = kgt[z]

    for s in range(3):
        cc_copy(s).wait_recv()
        local_grad(sources[s], 1 - k)

    def lz_wait(s):
        got = ll.at[k, lax.rem(z - s + nz, nz)]
        copy(got, got, s_lz.at[s], r_lz.at[s], at_z(zpeer(s))).wait_recv()

    loop(1, nz, lz_wait)
    lk_copy = copy(ll.at[k], ll.at[k], s_lk.at[0], r_lk.at[0], sibling)
    lk_copy.start()

    cx_copies[2].wait_recv()
    cx_copies[3].wait_recv()
    cc_copy(3).start()
    local_grad(far_x, k)

    lk_copy.wait_recv()

    def left_of(q):
        rows = []
        for rg in range(4):
            tiles = [ll[q % 2, t // tpz, q // 2, t % tpz] for t in (2 * rg, 2 * rg + 1)]
            rows.append(jnp.concatenate(tiles, axis=1))
        return jnp.concatenate(rows, axis=0)

    lefts = [left_of(q) for q in range(nxk)]
    wide3 = split3(jnp.concatenate(lefts, axis=1))
    stack3 = jnp.concatenate(wide3, axis=0)
    gram = None
    for part in wide3:
        term = dot(stack3, part, NT)
        term = term[0:32] + term[32:64] + term[64:96]
        gram = term if gram is None else gram + term
    for q in range(nxk):
        lsn[:, q] = natural_rows(lefts[q].T)
    natural = lsn[...].reshape(channels, RANK).T
    nh, nm, nl = split3(natural)
    ls4[...] = jnp.concatenate([nh, nm, nh, nm], axis=0).T
    ls4_store = pltpu.make_async_copy(ls4, ls4_out, s_in.at[7])
    ls4_store.start()

    cc_copy(3).wait_recv()
    local_grad(far_x, 1 - k)
    cor_store = pltpu.make_async_copy(cor, cor_out, s_in.at[6])
    cor_store.start()

    right = None
    for q in range(nxk):
        term = dot(jnp.concatenate(split2(lefts[q]), axis=0), chl[q], NN)
        right = term if q == 0 else right + term
    right = right[0:32] + right[32:64]
    rp[y] = right[:, 0:128] + right[:, 128:256]

    def rp_copy(s):
        return copy(rp.at[y], rp.at[y], s_rp.at[s], r_rp.at[s], at_y(lax.rem(y + s, ny)))

    loop(1, ny, lambda s: rp_copy(s).start())

    loop(1, nz, lambda s: rk_copy(s).wait_recv())
    total = rk[0]
    for q in range(1, nz):
        total = total + rk[q]
    yk[y] = total

    def yk_copy(s):
        return copy(yk.at[y], yk.at[y], s_yk.at[s], r_yk.at[s], at_y(lax.rem(y + s, ny)))

    loop(1, ny, lambda s: yk_copy(s).start())

    row_id = lax.broadcasted_iota(jnp.int32, (RANK, RANK), 0)
    lane_id = lax.broadcasted_iota(jnp.int32, (RANK, RANK), 1)
    same = row_id == lane_id
    aug = jnp.concatenate([gram, same.astype(F32)], axis=1)
    row_col = lax.broadcasted_iota(jnp.int32, (RANK, 2 * RANK), 0)

    def full(v):
        return jnp.broadcast_to(v, (RANK, 2 * RANK))

    for i in range(0, RANK, 2):
        c0 = full(aug[:, i : i + 1])
        c1 = full(aug[:, i + 1 : i + 2])
        r0 = full(aug[i : i + 1, :])
        r1 = full(aug[i + 1 : i + 2, :])
        p00 = full(c0[i : i + 1, :])
        p01 = full(c1[i : i + 1, :])
        p11 = full(c1[i + 1 : i + 2, :])
        inv = 1.0 / (p00 * p11 - p01 * p01)
        u0 = (p11 * c0 - p01 * c1) * inv
        u1 = (p00 * c1 - p01 * c0) * inv
        u0 = jnp.where(row_col > i + 1, u0, jnp.where(row_col == i + 1, p01 / p00, 0.0))
        u1 = jnp.where(row_col > i + 1, u1, 0.0)
        aug = aug - u0 * r0 - u1 * r1
    diag = jnp.sum(jnp.where(same, aug[:, 0:RANK], 0.0), axis=1, keepdims=True)
    scale = lax.rsqrt(diag)
    scale = scale * (1.5 - 0.5 * diag * scale * scale)
    linv = aug[:, RANK:] * scale
    ih, im, il = split3(linv)
    left[...] = dot(
        jnp.concatenate([ih, ih, ih, im, im, il], axis=1),
        jnp.concatenate([nh, nm, nl, nh, nm, nh], axis=0),
        NN,
    )
    left_store = pltpu.make_async_copy(left, left_out, s_in.at[8])
    left_store.start()

    inverse = dot(linv.T, linv, NN, HIGH) * (1.0 / workers)
    ah, am, al = split3(jnp.concatenate([linv, inverse], axis=0))
    final_left = jnp.concatenate([ah, ah, ah, am, am, al], axis=1)

    loop(1, ny, lambda s: rp_copy(s).wait_recv())
    total = rp[0]
    for q in range(1, ny):
        total = total + rp[q]
    th, tm, tl = split3(total)
    solved = dot(final_left, jnp.concatenate([th, tm, tl, th, tm, th], axis=0), NN)
    right_out[...] = solved[0:RANK]
    wh, wl = split2(solved[RANK:])
    w_out[...] = jnp.concatenate([wh, wh, wl, wl], axis=0)

    loop(1, ny, lambda s: yk_copy(s).wait_recv())
    total = yk[0]
    for q in range(1, ny):
        total = total + yk[q]
    for a in range(7):
        kg_out[a] = total[0:7, OWN * a : OWN * (a + 1)]

    for one in (cor_store, ls4_store, left_store):
        one.wait()
    loop(1, nz, lambda s: cz_copy(s).wait_send())
    loop(1, nz, lambda s: xz_copy(s).wait_send())
    es_copy.wait_send()
    for one in (in_r, in_gh, in_w):
        one.wait_send()
    loop(1, nx, lambda s: cs_copy(s).wait_send())
    gt_copy.wait_send()
    loop(1, nz, lambda s: rz_copy(s).wait_send())
    loop(1, ny, lambda s: ys_copy(s).wait_send())
    loop(1, nx, lambda s: lx_copy(s).wait_send())
    loop(1, nz, lambda s: lz_copy(s).wait_send())
    lk_copy.wait_send()
    loop(1, ny, lambda s: rp_copy(s).wait_send())
    loop(1, nz, lambda s: rk_copy(s).wait_send())
    loop(1, ny, lambda s: yk_copy(s).wait_send())
    for s in range(4):
        cx_copies[s].wait_send()
        cc_copy(s).wait_send()
    for one in (far_right, far_left, near_right, near_left):
        one.wait_send()


def finish(
    kg_hbm, left_hbm, right_hbm, w_hbm, ls_hbm, cor_hbm, kg_out, left_out, right_out, err_out,
    w_ref, ls_ref, cor_ref, kg_ref, left_ref, right_ref, load_sems, store_sems, small_sems,
):
    count = load_sems.shape[0] - 1
    width = cor_ref.shape[0] // count
    rows = ls_ref.shape[0] // count
    small = (
        (kg_hbm, kg_ref, kg_out),
        (left_hbm, left_ref, left_out),
        (right_hbm, right_ref, right_out),
    )
    small_loads = [
        pltpu.make_async_copy(a, b, small_sems.at[i, 0]) for i, (a, b, _) in enumerate(small)
    ]
    small_stores = [
        pltpu.make_async_copy(b, c, small_sems.at[i, 1]) for i, (_, b, c) in enumerate(small)
    ]
    w_load = pltpu.make_async_copy(w_hbm, w_ref, load_sems.at[count, 0])
    w_load.start()
    loads = []
    for i in range(count):
        at, lines = pl.ds(i * width, width), pl.ds(i * rows, rows)
        loads.append(
            (
                pltpu.make_async_copy(ls_hbm.at[lines], ls_ref.at[lines], load_sems.at[i, 0]),
                pltpu.make_async_copy(cor_hbm.at[at], cor_ref.at[at], load_sems.at[i, 1]),
            )
        )
        for one in loads[i]:
            one.start()
    for one in small_loads:
        one.start()
    w_load.wait()
    stores = []
    for i in range(count):
        for one in loads[i]:
            one.wait()
        at, lines = slice(i * width, (i + 1) * width), slice(i * rows, (i + 1) * rows)
        approx = dot(ls_ref[lines, :], w_ref[...], NN)
        cor_ref[at] = cor_ref[at] - approx.reshape((width,) + cor_ref.shape[1:])
        part = pl.ds(i * width, width)
        stores.append(
            pltpu.make_async_copy(cor_ref.at[part], err_out.at[part], store_sems.at[i])
        )
        stores[i].start()
        if i == 0:
            for load, store in zip(small_loads, small_stores):
                load.wait()
                store.start()
    for one in stores + small_stores:
        one.wait()


def on_device(ny, nz, nx, block_input, depth_kernel, w_expand, grad_hidden, error_old, right_init):
    nxk = 2 * nx
    ch = OWN * nz
    channels = nz * nxk * OWN
    tpz = 8 // nz
    hid = right_init.shape[0]
    vmem = pltpu.VMEM
    scratch = [
        vmem((SIDE, SIDE, OWN), BF16),
        vmem((7, 7, channels), F32),
        vmem((channels, 128), BF16),
        vmem((nz, nxk, OWN, 128), F32),
        vmem((RANK, 128), F32),
        vmem((LP, 128), BF16),
        vmem((LP, 128), BF16),
        vmem((LX - 512, 256), BF16),
        vmem((channels, 128), BF16),
        vmem((RANK, 128), F32),
        vmem((nz, nx, 2, OWN, 256), F32),
        vmem((LP, OWN), F32),
        vmem((OWN, LX), F32),
        vmem((OWN, LP), F32),
        vmem((nz, 16, LX), BF16),
        vmem((nz, 16, LX), BF16),
        vmem((ch, LX), F32),
        vmem((8, LP), F32),
        vmem((64, channels), F32),
        vmem((OWN, 64), F32),
        vmem((nx, 2, nz, 16, LX), BF16),
        vmem((2, ch, LP), F32),
        vmem((3, ch, LP), BF16),
        vmem((2, ch // 2, LP), BF16),
        vmem((2, ch, LP), BF16),
        vmem((ch, LP), F32),
        vmem((nx, 2, 8, 8, 128), F32),
        vmem((2, 10, 8, 128), F32),
        vmem((nx, 8, 8, 128), F32),
        vmem((nx, 2, 18, 8, 128), F32),
        vmem((2, 10, 8, 128), F32),
        vmem((8, 8, 128), F32),
        vmem((nz, tpz, 8, 128), F32),
        vmem((ny, tpz, 8, 128), F32),
        vmem((2, nz, nx, tpz, 8, 128), F32),
        vmem((nxk, 256, 256), BF16),
        vmem((ny, RANK, 128), F32),
        vmem((nz, 8, 256), F32),
        vmem((nz, 8, 256), F32),
        vmem((ny, 8, 256), F32),
        vmem((nz, nxk, OWN, RANK), F32),
        vmem((channels, 4 * RANK), BF16),
        vmem((nz, nxk, OWN, 128), F32),
        vmem((RANK, channels), F32),
    ]
    sems = [pltpu.SemaphoreType.DMA((9,))]
    for count in (nz, nz, 2, nx, 1, nz, ny, nx, nz, 1, ny, nz, ny, 4, 4, 4, 4):
        sems += [pltpu.SemaphoreType.DMA((count,))] * 2
    spec = pl.BlockSpec(memory_space=pltpu.VMEM)
    far = pl.BlockSpec(memory_space=pl.ANY)
    cor_shape = jax.ShapeDtypeStruct((nz, nxk, OWN, 128), F32)
    mids = (
        jax.ShapeDtypeStruct((7, 7, OWN), F32),
        jax.ShapeDtypeStruct((RANK, channels), F32),
        jax.ShapeDtypeStruct((RANK, 128), F32),
        jax.ShapeDtypeStruct((4 * RANK, 128), BF16),
        jax.ShapeDtypeStruct((channels, 4 * RANK), BF16),
        cor_shape,
    )
    parts = pl.pallas_call(
        functools.partial(kernel, ny, nz, nx),
        out_shape=mids,
        in_specs=[pl.BlockSpec(memory_space=pl.ANY)] * 6,
        out_specs=(spec, far, spec, spec, far, far),
        scratch_shapes=scratch + sems,
        compiler_params=pltpu.CompilerParams(
            collective_id=0, has_side_effects=True, vmem_limit_bytes=60 * 1024 * 1024
        ),
        cost_estimate=pl.CostEstimate(
            flops=600_000_000, bytes_accessed=4_000_000, transcendentals=0
        ),
    )(
        block_input.reshape(SIDE, SIDE, OWN),
        depth_kernel,
        w_expand,
        grad_hidden.reshape(POS, 128),
        error_old.reshape(nz, nxk, OWN, 128),
        right_init.T,
    )
    steps = min(4, nz)
    kg, left, right, err = pl.pallas_call(
        finish,
        out_shape=mids[0:3] + (cor_shape,),
        in_specs=[far] * 6,
        out_specs=(far,) * 4,
        scratch_shapes=[
            vmem((4 * RANK, 128), BF16),
            vmem((channels, 4 * RANK), BF16),
            vmem((nz, nxk, OWN, 128), F32),
            vmem((7, 7, OWN), F32),
            vmem((RANK, channels), F32),
            vmem((RANK, 128), F32),
            pltpu.SemaphoreType.DMA((steps + 1, 2)),
            pltpu.SemaphoreType.DMA((steps,)),
            pltpu.SemaphoreType.DMA((3, 2)),
        ],
        compiler_params=pltpu.CompilerParams(vmem_limit_bytes=60 * 1024 * 1024),
        cost_estimate=pl.CostEstimate(
            flops=60_000_000, bytes_accessed=2_500_000, transcendentals=0
        ),
    )(*parts)
    return (
        kg,
        left.T,
        right.T,
        err.reshape(1, channels, 128),
    )


def solution(mesh, nx=NX):
    ny = mesh.shape["outer"]
    nz = mesh.shape["chip"] // (2 * nx)
    placed = (
        P("outer", None, None, "chip"),
        P(),
        P(None, "chip"),
        P("outer", None, None, "chip"),
        P("outer", None, "chip"),
        P("chip", None),
    )
    return jax.shard_map(
        functools.partial(on_device, ny, nz, nx),
        mesh=mesh,
        in_specs=placed,
        out_specs=(P(None, None, "chip"), P(), P("chip", None), P("outer", None, "chip")),
        check_vma=False,
    )
```

```python
import functools

import jax
import jax.numpy as jnp
from jax import lax
from jax.experimental import pallas as pl
from jax.experimental.pallas import tpu as pltpu
from jax.sharding import PartitionSpec as P

F32 = jnp.float32
BF16 = jnp.bfloat16
HIGH = lax.Precision.HIGHEST
MESH = pl.DeviceIdType.MESH

NX = 4
SIDE = 24
POS = SIDE * SIDE
LP = 640
LX = 896
OWN = 24
RANK = 32


def dot(a, b, dims, precision=None):
    return lax.dot_general(a, b, (dims, ((), ())), precision=precision, preferred_element_type=F32)


NN = ((1,), (0,))
NT = ((1,), (1,))
TN = ((0,), (0,))


def loop(lo, hi, body, unroll=1):
    def step(i, carry):
        body(i)
        return carry

    lax.fori_loop(lo, hi, step, 0, unroll=unroll)


def split2(v):
    hi = v.astype(BF16)
    return hi, (v - hi.astype(F32)).astype(BF16)


def split3(v):
    hi = v.astype(BF16)
    rest = v - hi.astype(F32)
    mid = rest.astype(BF16)
    return hi, mid, (rest - mid.astype(F32)).astype(BF16)


def kernel(
    ny, nz, nx,
    x_hbm, k_hbm, w_hbm, gh_hbm, err_hbm, r_hbm,
    kg_out, left_out, right_out, w_out, ls4_out, cor_out,
    x_ref, k_ref, w_ref, err_ref, r_ref,
    ghp, ghs, ght, ws, rs, wf, x2, xo, conv24, cz, xz, xp, mk, kflat, kt, cvf, gr, gb, rh1, rh2, g32,
    eg, gg, es, cs, cg, gt, st, rz, ys, ll, chl, rp, kgt, rk, yk, lsn, ls4, cor, left,
    s_in,
    s_cz, r_cz, s_xz, r_xz, s_es, r_es, s_cs, r_cs, s_cg, r_cg, s_gt, r_gt, s_rz, r_rz, s_ys, r_ys, s_lx, r_lx, s_lz, r_lz,
    s_lk, r_lk, s_rp, r_rp, s_rk, r_rk, s_yk, r_yk, s_in2, r_in2, s_gx, r_gx, s_cx, r_cx, s_cc, r_cc,
):
    nxk = 2 * nx
    ch = OWN * nz
    channels = ch * nxk
    tpz = 8 // nz
    half = ch // 2
    top = 16 * nz
    workers = ny
    y = lax.axis_index("outer")
    chip = lax.axis_index("chip")
    z = chip // nxk
    xk = lax.rem(chip, nxk)
    x = xk // 2
    k = lax.rem(xk, 2)

    def zpeer(s):
        return lax.rem(z + s, nz)

    def at_z(zz):
        return (y, zz * nxk + xk)

    def at_x(xx):
        return (y, z * nxk + xx * 2 + k)

    right_x = lax.rem(x + 1, nx)
    left_x = lax.rem(x + nx - 1, nx)
    far_x = lax.rem(x + 2, nx)

    def at_y(yy):
        return (yy, chip)

    sibling = (y, z * nxk + x * 2 + (1 - k))

    def copy(src, dst, ssem, rsem, dev):
        return pltpu.make_async_remote_copy(
            src_ref=src, dst_ref=dst, send_sem=ssem, recv_sem=rsem,
            device_id=dev, device_id_type=MESH,
        )

    def slots(v):
        return jnp.concatenate(
            [v[:, 0:16].reshape(top, v.shape[2]), v[:, 16:24].reshape(ch - top, v.shape[2])], axis=0
        )

    def natural_rows(v):
        return jnp.concatenate(
            [v[0:top].reshape(nz, 16, v.shape[1]), v[top:ch].reshape(nz, 8, v.shape[1])], axis=1
        )

    load_x = pltpu.make_async_copy(x_hbm, x_ref, s_in.at[0])
    load_r = pltpu.make_async_copy(r_hbm, r_ref, s_in.at[1])
    load_err = pltpu.make_async_copy(err_hbm, err_ref, s_in.at[2])
    load_gh = pltpu.make_async_copy(gh_hbm, ghp.at[pl.ds(0, POS)], s_in.at[3])
    load_w = pltpu.make_async_copy(w_hbm, w_ref, s_in.at[4])
    load_k = pltpu.make_async_copy(k_hbm, k_ref, s_in.at[5])
    for load in (load_x, load_r, load_err, load_gh, load_w, load_k):
        load.start()

    barrier = pltpu.get_barrier_semaphore()

    def greet(dev):
        pl.semaphore_signal(barrier, inc=1, device_id=dev, device_id_type=MESH)

    loop(1, nz, lambda s: greet(at_z(zpeer(s))))
    loop(1, nx, lambda s: greet(at_x(lax.rem(x + s, nx))))
    greet(sibling)
    loop(1, ny, lambda s: greet(at_y(lax.rem(y + s, ny))))

    x2[POS:, :] = jnp.zeros((LP - POS, OWN), F32)
    load_x.wait()
    for i in range(SIDE):
        x2[SIDE * i : SIDE * (i + 1), :] = x_ref[i].astype(F32)
    eye = (
        lax.broadcasted_iota(jnp.int32, (32, OWN), 0)
        == lax.broadcasted_iota(jnp.int32, (32, OWN), 1)
    )
    own = dot(eye.astype(F32).astype(BF16), x2[...].astype(BF16), NT)[0:OWN]
    xo[:, 0:128] = jnp.zeros((OWN, 128), F32)
    xo[:, 128 : 128 + LP] = own
    xo[:, 128 + LP :] = jnp.zeros((OWN, LX - 128 - LP), F32)
    load_k.wait()
    for a in range(7):
        kflat[8 * a : 8 * a + 7, :] = k_ref[a]
        kflat[8 * a + 7 : 8 * a + 8, :] = jnp.zeros((1, channels), F32)
    kflat[56:64, :] = jnp.zeros((8, channels), F32)
    row = lax.broadcasted_iota(jnp.int32, (OWN, channels), 0)
    lane = lax.broadcasted_iota(jnp.int32, (OWN, channels), 1)
    pick = (lane - row == chip * OWN).astype(F32).astype(BF16)
    three = jnp.concatenate(split3(kflat[...]), axis=0)
    taps3 = dot(pick, three, NT)
    kt[...] = taps3[:, 0:64] + taps3[:, 64:128] + taps3[:, 128:192]
    pos = lax.broadcasted_iota(jnp.int32, (8, LP), 1)
    col = lax.rem(pos, SIDE) + lax.broadcasted_iota(jnp.int32, (8, LP), 0) - 3
    mk[...] = ((col >= 0) & (col < SIDE) & (pos < POS)).astype(F32)

    def shifted(v):
        return [pltpu.roll(v, LX - (96 + SIDE * (a - 3)), 1)[:, 0:LP] for a in range(7)]

    for t in range(OWN // 8):
        rows = slice(8 * t, 8 * t + 8)
        taps = kt[rows, :]
        moved = shifted(xo[rows, :])
        out = None
        for b in range(7):
            part = None
            for a in range(7):
                term = taps[:, 8 * a + b : 8 * a + b + 1] * moved[a]
                part = term if a == 0 else part + term
            part = pltpu.roll(part, LP - (32 + b - 3), 1) * mk[b : b + 1, :]
            out = part if b == 0 else out + part
        conv24[rows, :] = out

    lane_x = lax.broadcasted_iota(jnp.int32, (16, LX), 1)

    def pack(v):
        wide = jnp.concatenate([v, jnp.zeros((OWN, LX - LP), F32)], axis=1)
        last = wide[16:24]
        early = jnp.where(lane_x[0:8] < POS // 2, last, 0.0)
        late = jnp.where(lane_x[0:8] < POS // 2, 0.0, last)
        tail = jnp.concatenate(
            [pltpu.roll(early, POS, 1), pltpu.roll(late, POS // 2, 1)], axis=0
        )
        return (wide[0:16] + tail).astype(BF16)

    def unpack(v):
        v = v.astype(F32)
        early = pltpu.roll(v[0:8], LX - POS, 1)
        late = pltpu.roll(v[8:16], LX - POS // 2, 1)
        last = jnp.where(
            lane_x[0:8] < POS // 2, early, jnp.where(lane_x[0:8] < POS, late, 0.0)
        )
        return jnp.where(lane_x < POS, v, 0.0)[:, 0:LP], last[:, 0:LP]

    cz[z] = pack(conv24[...])

    def cz_copy(s):
        return copy(cz.at[z], cz.at[z], s_cz.at[s], r_cz.at[s], at_z(zpeer(s)))

    xz[z] = pack(own)

    pl.semaphore_wait(barrier, (nz - 1) + (nx - 1) + (ny - 1) + 1)

    loop(1, nz, lambda s: cz_copy(s).start())

    in_gh = copy(gh_hbm, ghs.at[pl.ds(0, POS)], s_in2.at[0], r_in2.at[0], sibling)
    in_r = copy(r_hbm, rs, s_in2.at[1], r_in2.at[1], sibling)
    in_w = copy(w_hbm, ws, s_in2.at[2], r_in2.at[2], sibling)
    for one in (in_r, in_gh, in_w):
        one.start()


    def xz_copy(s):
        return copy(xz.at[z], xz.at[z], s_xz.at[s], r_xz.at[s], at_z(zpeer(s)))


    load_r.wait()
    load_err.wait()
    rh, rl = split2(r_ref[...])
    four = jnp.concatenate(
        [jnp.concatenate([rh, rh], axis=1), jnp.concatenate([rl, rl], axis=1)], axis=0
    )
    for q in range(nxk):
        eh, el = split2(slots(err_ref[:, q]))
        rows = jnp.concatenate([eh, el], axis=1)
        if ch < 256:
            rows = jnp.concatenate([rows, jnp.zeros((256 - ch, 256), BF16)], axis=0)
        e = dot(four, rows, NT)
        e = e[0:32] + e[32:64]
        for rg in range(4):
            for part in range(2):
                eg[q // 2, q % 2, 2 * rg + part] = e[8 * rg : 8 * rg + 8, 128 * part : 128 * part + 128]

    es_copy = copy(eg.at[:, 1 - k], es, s_es.at[0], r_es.at[0], sibling)
    es_copy.start()

    ghp[POS:, :] = jnp.zeros((LP - POS, 128), BF16)
    ghs[POS:, :] = jnp.zeros((LP - POS, 128), BF16)

    load_gh.wait()
    halves_of = jnp.concatenate([ghp[0 : POS // 2, :], ghp[POS // 2 : POS, :]], axis=1)
    ght[...] = jnp.concatenate(
        [
            jnp.zeros((64, 256), BF16),
            halves_of,
            jnp.zeros((LX - 512 - 64 - POS // 2, 256), BF16),
        ],
        axis=0,
    )
    in_gh.wait_recv()
    in_r.wait_recv()
    sh, sl = split2(rs[...])
    both = jnp.concatenate([ghp[...], ghs[...]], axis=1)
    g = dot(
        jnp.concatenate([rh, sh, rl, sl], axis=1), jnp.concatenate([both, both], axis=1), NT
    )
    for rg in range(4):
        for j in range(5):
            gg[rg // 2, (rg % 2) * 5 + j] = g[8 * rg : 8 * rg + 8, 128 * j : 128 * j + 128]

    cg[x] = gg[k]

    def cg_copy(s):
        return copy(cg.at[x], cg.at[x], s_cg.at[s], r_cg.at[s], at_x(lax.rem(x + s, nx)))

    loop(1, nx, lambda s: cg_copy(s).start())

    es_copy.wait_recv()

    def chip_sum(xx):
        cs[xx, 0] = eg[xx, k] + es[xx]

    loop(0, nx, chip_sum)
    cs[x, 1] = cs[x, 0]

    def cs_copy(s):
        xx = lax.rem(x + s, nx)
        return copy(cs.at[xx, 0], cs.at[x, 1], s_cs.at[s], r_cs.at[s], at_x(xx))

    loop(1, nx, lambda s: cs_copy(s).start())

    load_w.wait()
    in_w.wait_recv()
    wf[:, :, :, :, 0:128] = w_ref[...].astype(F32).reshape(nz, nx, 2, OWN, 128)
    wf[:, :, :, :, 128:256] = ws[...].astype(F32).reshape(nz, nx, 2, OWN, 128)

    def grad_rows(xx):
        rows = wf[:, xx, k].reshape(ch, 256).astype(BF16)
        return dot(rows, jnp.concatenate([ghp[...], ghs[...]], axis=1), NT)

    gb[0] = grad_rows(far_x).astype(BF16)
    far_right = copy(
        gb.at[0, pl.ds(0, half)], rh1.at[0], s_gx.at[0], r_gx.at[0], at_x(right_x)
    )
    far_left = copy(
        gb.at[0, pl.ds(half, half)], rh1.at[1], s_gx.at[1], r_gx.at[1], at_x(left_x)
    )
    far_right.start()
    far_left.start()
    gr[0] = grad_rows(right_x)
    gr[1] = grad_rows(left_x)
    g32[...] = grad_rows(x)

    def cg_wait(s):
        got = cg.at[lax.rem(x - s + nx, nx)]
        copy(got, got, s_cg.at[s], r_cg.at[s], at_x(lax.rem(x + s, nx))).wait_recv()

    loop(1, nx, cg_wait)
    total = cg[0]
    for q in range(1, nx):
        total = total + cg[q]
    gt[k] = total
    gt_copy = copy(gt.at[k], gt.at[k], s_gt.at[0], r_gt.at[0], sibling)
    gt_copy.start()

    loop(1, nx, lambda s: cs_copy(s).wait_recv())
    total = cs[0, 1]
    for q in range(1, nx):
        total = total + cs[q, 1]
    st[...] = total

    loop(1, nz, lambda s: cz_copy(s).wait_recv())
    cvf[x, k] = cz[...]

    gt_copy.wait_recv()
    groups = []
    for rg in range(4):
        groups.append(
            jnp.concatenate([gt[rg // 2, (rg % 2) * 5 + j] for j in range(5)], axis=1)
        )
    gfull = jnp.concatenate(groups, axis=0)
    lane_g = lax.broadcasted_iota(jnp.int32, (32, LP), 1)
    inside = (lane_g >= 64) & (lane_g < 64 + POS // 2)
    glow = jnp.where(inside, pltpu.roll(gfull, 64, 1), 0.0)[:, 0 : LX - 512]
    ghigh = jnp.where(inside, pltpu.roll(gfull, LP + 64 - POS // 2, 1), 0.0)[:, 0 : LX - 512]
    packed = cz[...]
    halves = packed[:, :, 512:].astype(F32)
    conv_top = dot(
        jnp.concatenate(split2(gfull), axis=0), packed[:, :, 0:LP].reshape(top, LP), NT
    )
    conv_last = None
    for part, rows in ((glow, halves[:, 0:8]), (ghigh, halves[:, 8:16])):
        rows = rows.reshape(ch - top, LX - 512).astype(BF16)
        term = dot(jnp.concatenate(split2(part), axis=0), rows, NT)
        conv_last = term if conv_last is None else conv_last + term
    conv_left = jnp.concatenate(
        [
            conv_top[0:32] + conv_top[32:64],
            conv_last[0:32] + conv_last[32:64],
            jnp.zeros((32, 256 - ch), F32),
        ],
        axis=1,
    )
    for rg in range(4):
        for part in range(2):
            st[2 * rg + part] += conv_left[8 * rg : 8 * rg + 8, 128 * part : 128 * part + 128]

    def rz_copy(s):
        zz = zpeer(s)
        return copy(st.at[pl.ds(zz * tpz, tpz)], rz.at[z], s_rz.at[s], r_rz.at[s], at_z(zz))

    loop(1, nz, lambda s: rz_copy(s).start())
    rz[z] = st[pl.ds(z * tpz, tpz)]
    loop(1, nz, lambda s: xz_copy(s).start())

    far_right.wait_recv()
    gb[1, 0:half, :] = (gr[0, 0:half, :] + rh1[0].astype(F32)).astype(BF16)
    gb[1, half:, :] = gr[0, half:, :].astype(BF16)
    near_right = copy(gb.at[1], rh2.at[0], s_gx.at[2], r_gx.at[2], at_x(right_x))
    near_right.start()
    far_left.wait_recv()
    gb[2, 0:half, :] = gr[1, 0:half, :].astype(BF16)
    gb[2, half:, :] = (gr[1, half:, :] + rh1[1].astype(F32)).astype(BF16)
    near_left = copy(gb.at[2], rh2.at[1], s_gx.at[3], r_gx.at[3], at_x(left_x))
    near_left.start()

    mine = cvf.at[x, k]
    cx_copies = [
        copy(mine, mine, s_cx.at[0], r_cx.at[0], at_x(right_x)),
        copy(mine, mine, s_cx.at[1], r_cx.at[1], at_x(left_x)),
    ]
    for s in range(2):
        cx_copies[s].start()

    sources = (x, left_x, right_x, far_x)

    def cc_copy(s):
        block = cvf.at[sources[s], k]
        return copy(block, block, s_cc.at[s], r_cc.at[s], sibling)

    cc_copy(0).start()

    loop(1, nz, lambda s: rz_copy(s).wait_recv())
    total = rz[0]
    for q in range(1, nz):
        total = total + rz[q]
    ys[y] = total

    def ys_copy(s):
        return copy(ys.at[y], ys.at[y], s_ys.at[s], r_ys.at[s], at_y(lax.rem(y + s, ny)))

    loop(1, ny, lambda s: ys_copy(s).start())

    def local_grad(xx, kk):
        q = xx * 2 + kk
        packed = cvf[xx, kk].reshape(top, LX)
        first = dot(packed[:, 0:LP], ghp[...], NN)
        both = dot(packed[:, 512:], ght[...], NN).reshape(nz, 16, 256)
        last = both[:, 0:8, 0:128] + both[:, 8:16, 128:256]
        part = jnp.concatenate([first, last.reshape(ch - top, 128)], axis=0) + slots(err_ref[:, q])
        cor[:, q] = natural_rows(part)
        chl[q, 0:ch, :] = jnp.concatenate(split2(part), axis=1)

    if ch < 256:
        chl[:, ch:, :] = jnp.zeros((nxk, 256 - ch, 256), BF16)
    loop(1, ny, lambda s: ys_copy(s).wait_recv())
    total = ys[0]
    for q in range(1, ny):
        total = total + ys[q]
    ll[k, z, x] = total

    def lx_copy(s):
        own = ll.at[k, z, x]
        return copy(own, own, s_lx.at[s], r_lx.at[s], at_x(lax.rem(x + s, nx)))

    loop(1, nx, lambda s: lx_copy(s).start())

    local_grad(x, k)

    loop(1, nz, lambda s: xz_copy(s).wait_recv())
    xp[:, 0:128] = jnp.zeros((ch, 128), F32)
    xp[:, 128 + LP :] = jnp.zeros((ch, LX - 128 - LP), F32)
    for zz in range(nz):
        first, last = unpack(xz[zz])
        xp[OWN * zz : OWN * zz + 16, 128 : 128 + LP] = first
        xp[OWN * zz + 16 : OWN * zz + 24, 128 : 128 + LP] = last
    near_right.wait_recv()
    near_left.wait_recv()
    g32[...] += rh2[0].astype(F32) + rh2[1].astype(F32)
    pair_row = lax.broadcasted_iota(jnp.int32, (OWN, 7 * OWN), 0)
    pair_lane = lax.broadcasted_iota(jnp.int32, (OWN, 7 * OWN), 1)
    diagonal = lax.rem(pair_lane, OWN) == pair_row
    tap_row = lax.broadcasted_iota(jnp.int32, (8, 7 * OWN), 0)

    def kernel_terms(zz):
        rows = pl.ds(pl.multiple_of(zz * OWN, 8), OWN)
        maps = jnp.concatenate(shifted(xp[rows, :]), axis=0).astype(BF16)
        gt = g32[rows, :]
        moved = [pltpu.roll(gt * mk[b : b + 1, :], 32 + b - 3, 1) for b in range(7)]
        hi, lo = split2(jnp.concatenate(moved, axis=0))
        pairs = dot(hi, maps, NT) + dot(lo, maps, NT)
        out = jnp.zeros((8, 7 * OWN), F32)
        for b in range(7):
            block = jnp.where(diagonal, pairs[OWN * b : OWN * (b + 1)], 0.0)
            one = jnp.sum(block, axis=0, keepdims=True)
            out = jnp.where(tap_row == b, one, out)
        kgt[zz] = jnp.concatenate([out, jnp.zeros((8, 256 - 7 * OWN), F32)], axis=1)

    loop(0, nz, kernel_terms, 2)

    def rk_copy(s):
        zz = zpeer(s)
        return copy(kgt.at[zz], rk.at[z], s_rk.at[s], r_rk.at[s], at_z(zz))

    loop(1, nz, lambda s: rk_copy(s).start())
    rk[z] = kgt[z]

    def lx_wait(s):
        got = ll.at[k, z, lax.rem(x - s + nx, nx)]
        copy(got, got, s_lx.at[s], r_lx.at[s], at_x(lax.rem(x + s, nx))).wait_recv()

    loop(1, nx, lx_wait)

    def lz_copy(s):
        own = ll.at[k, z]
        return copy(own, own, s_lz.at[s], r_lz.at[s], at_z(zpeer(s)))

    loop(1, nz, lambda s: lz_copy(s).start())

    cx_copies[0].wait_recv()
    part0 = cvf.at[left_x, k, pl.ds(0, nz // 2)]
    cx_copies.append(copy(part0, part0, s_cx.at[2], r_cx.at[2], at_x(right_x)))
    cx_copies[2].start()
    cc_copy(1).start()
    cx_copies[1].wait_recv()
    part1 = cvf.at[right_x, k, pl.ds(nz // 2, nz // 2)]
    cx_copies.append(copy(part1, part1, s_cx.at[3], r_cx.at[3], at_x(left_x)))
    cx_copies[3].start()
    cc_copy(2).start()
    local_grad(left_x, k)
    local_grad(right_x, k)

    for s in range(3):
        cc_copy(s).wait_recv()
        local_grad(sources[s], 1 - k)

    loop(1, nz, lambda s: rk_copy(s).wait_recv())
    total = rk[0]
    for q in range(1, nz):
        total = total + rk[q]
    yk[y] = total

    def yk_copy(s):
        return copy(yk.at[y], yk.at[y], s_yk.at[s], r_yk.at[s], at_y(lax.rem(y + s, ny)))

    loop(1, ny, lambda s: yk_copy(s).start())

    def lz_wait(s):
        got = ll.at[k, lax.rem(z - s + nz, nz)]
        copy(got, got, s_lz.at[s], r_lz.at[s], at_z(zpeer(s))).wait_recv()

    loop(1, nz, lz_wait)
    lk_copy = copy(ll.at[k], ll.at[k], s_lk.at[0], r_lk.at[0], sibling)
    lk_copy.start()

    cx_copies[2].wait_recv()
    cx_copies[3].wait_recv()
    cc_copy(3).start()
    local_grad(far_x, k)

    lk_copy.wait_recv()

    def left_of(q):
        rows = []
        for rg in range(4):
            tiles = [ll[q % 2, t // tpz, q // 2, t % tpz] for t in (2 * rg, 2 * rg + 1)]
            rows.append(jnp.concatenate(tiles, axis=1))
        return jnp.concatenate(rows, axis=0)

    lefts = [left_of(q) for q in range(nxk)]
    wide3 = split3(jnp.concatenate(lefts, axis=1))
    stack3 = jnp.concatenate(wide3, axis=0)
    gram = None
    for part in wide3:
        term = dot(stack3, part, NT)
        term = term[0:32] + term[32:64] + term[64:96]
        gram = term if gram is None else gram + term
    for q in range(nxk):
        lsn[:, q] = natural_rows(lefts[q].T)
    natural = lsn[...].reshape(channels, RANK).T
    nh, nm, nl = split3(natural)
    ls4[...] = jnp.concatenate([nh, nm, nh, nm], axis=0).T
    ls4_store = pltpu.make_async_copy(ls4, ls4_out, s_in.at[7])
    ls4_store.start()

    cc_copy(3).wait_recv()
    local_grad(far_x, 1 - k)
    cor_store = pltpu.make_async_copy(cor, cor_out, s_in.at[6])
    cor_store.start()

    right = None
    for q in range(nxk):
        term = dot(jnp.concatenate(split2(lefts[q]), axis=0), chl[q], NN)
        right = term if q == 0 else right + term
    right = right[0:32] + right[32:64]
    rp[y] = right[:, 0:128] + right[:, 128:256]

    def rp_copy(s):
        return copy(rp.at[y], rp.at[y], s_rp.at[s], r_rp.at[s], at_y(lax.rem(y + s, ny)))

    loop(1, ny, lambda s: rp_copy(s).start())

    row_id = lax.broadcasted_iota(jnp.int32, (RANK, RANK), 0)
    lane_id = lax.broadcasted_iota(jnp.int32, (RANK, RANK), 1)
    same = row_id == lane_id
    aug = jnp.concatenate([gram, same.astype(F32)], axis=1)
    row_col = lax.broadcasted_iota(jnp.int32, (RANK, 2 * RANK), 0)

    def full(v):
        return jnp.broadcast_to(v, (RANK, 2 * RANK))

    for i in range(0, RANK, 2):
        c0 = full(aug[:, i : i + 1])
        c1 = full(aug[:, i + 1 : i + 2])
        r0 = full(aug[i : i + 1, :])
        r1 = full(aug[i + 1 : i + 2, :])
        p00 = full(c0[i : i + 1, :])
        p01 = full(c1[i : i + 1, :])
        p11 = full(c1[i + 1 : i + 2, :])
        inv = 1.0 / (p00 * p11 - p01 * p01)
        u0 = (p11 * c0 - p01 * c1) * inv
        u1 = (p00 * c1 - p01 * c0) * inv
        u0 = jnp.where(row_col > i + 1, u0, jnp.where(row_col == i + 1, p01 / p00, 0.0))
        u1 = jnp.where(row_col > i + 1, u1, 0.0)
        aug = aug - u0 * r0 - u1 * r1
    diag = jnp.sum(jnp.where(same, aug[:, 0:RANK], 0.0), axis=1, keepdims=True)
    scale = lax.rsqrt(diag)
    scale = scale * (1.5 - 0.5 * diag * scale * scale)
    linv = aug[:, RANK:] * scale
    ih, im, il = split3(linv)
    left[...] = dot(
        jnp.concatenate([ih, ih, ih, im, im, il], axis=1),
        jnp.concatenate([nh, nm, nl, nh, nm, nh], axis=0),
        NN,
    )
    left_store = pltpu.make_async_copy(left, left_out, s_in.at[8])
    left_store.start()

    inverse = dot(linv.T, linv, NN, HIGH) * (1.0 / workers)
    ah, am, al = split3(jnp.concatenate([linv, inverse], axis=0))
    final_left = jnp.concatenate([ah, ah, ah, am, am, al], axis=1)

    loop(1, ny, lambda s: rp_copy(s).wait_recv())
    total = rp[0]
    for q in range(1, ny):
        total = total + rp[q]
    th, tm, tl = split3(total)
    solved = dot(final_left, jnp.concatenate([th, tm, tl, th, tm, th], axis=0), NN)
    right_out[...] = solved[0:RANK]
    wh, wl = split2(solved[RANK:])
    w_out[...] = jnp.concatenate([wh, wh, wl, wl], axis=0)

    loop(1, ny, lambda s: yk_copy(s).wait_recv())
    total = yk[0]
    for q in range(1, ny):
        total = total + yk[q]
    for a in range(7):
        kg_out[a] = total[0:7, OWN * a : OWN * (a + 1)]

    for one in (cor_store, ls4_store, left_store):
        one.wait()
    loop(1, nz, lambda s: cz_copy(s).wait_send())
    loop(1, nz, lambda s: xz_copy(s).wait_send())
    es_copy.wait_send()
    for one in (in_r, in_gh, in_w):
        one.wait_send()
    loop(1, nx, lambda s: cs_copy(s).wait_send())
    loop(1, nx, lambda s: cg_copy(s).wait_send())
    gt_copy.wait_send()
    loop(1, nz, lambda s: rz_copy(s).wait_send())
    loop(1, ny, lambda s: ys_copy(s).wait_send())
    loop(1, nx, lambda s: lx_copy(s).wait_send())
    loop(1, nz, lambda s: lz_copy(s).wait_send())
    lk_copy.wait_send()
    loop(1, ny, lambda s: rp_copy(s).wait_send())
    loop(1, nz, lambda s: rk_copy(s).wait_send())
    loop(1, ny, lambda s: yk_copy(s).wait_send())
    for s in range(4):
        cx_copies[s].wait_send()
        cc_copy(s).wait_send()
    for one in (far_right, far_left, near_right, near_left):
        one.wait_send()


def finish(kg_ref, left_ref, right_ref, w_ref, ls_ref, cor_ref, kg_out, left_out, right_out, err_out):
    kg_out[...] = kg_ref[...]
    left_out[...] = left_ref[...]
    right_out[...] = right_ref[...]
    approx = dot(ls_ref[...], w_ref[...], NN)
    err_out[...] = cor_ref[...] - approx.reshape(cor_ref.shape)


def on_device(ny, nz, nx, block_input, depth_kernel, w_expand, grad_hidden, error_old, right_init):
    nxk = 2 * nx
    ch = OWN * nz
    channels = nz * nxk * OWN
    tpz = 8 // nz
    hid = right_init.shape[0]
    vmem = pltpu.VMEM
    scratch = [
        vmem((SIDE, SIDE, OWN), BF16),
        vmem((7, 7, channels), F32),
        vmem((channels, 128), BF16),
        vmem((nz, nxk, OWN, 128), F32),
        vmem((RANK, 128), F32),
        vmem((LP, 128), BF16),
        vmem((LP, 128), BF16),
        vmem((LX - 512, 256), BF16),
        vmem((channels, 128), BF16),
        vmem((RANK, 128), F32),
        vmem((nz, nx, 2, OWN, 256), F32),
        vmem((LP, OWN), F32),
        vmem((OWN, LX), F32),
        vmem((OWN, LP), F32),
        vmem((nz, 16, LX), BF16),
        vmem((nz, 16, LX), BF16),
        vmem((ch, LX), F32),
        vmem((8, LP), F32),
        vmem((64, channels), F32),
        vmem((OWN, 64), F32),
        vmem((nx, 2, nz, 16, LX), BF16),
        vmem((2, ch, LP), F32),
        vmem((3, ch, LP), BF16),
        vmem((2, ch // 2, LP), BF16),
        vmem((2, ch, LP), BF16),
        vmem((ch, LP), F32),
        vmem((nx, 2, 8, 8, 128), F32),
        vmem((2, 10, 8, 128), F32),
        vmem((nx, 8, 8, 128), F32),
        vmem((nx, 2, 8, 8, 128), F32),
        vmem((nx, 10, 8, 128), F32),
        vmem((2, 10, 8, 128), F32),
        vmem((8, 8, 128), F32),
        vmem((nz, tpz, 8, 128), F32),
        vmem((ny, tpz, 8, 128), F32),
        vmem((2, nz, nx, tpz, 8, 128), F32),
        vmem((nxk, 256, 256), BF16),
        vmem((ny, RANK, 128), F32),
        vmem((nz, 8, 256), F32),
        vmem((nz, 8, 256), F32),
        vmem((ny, 8, 256), F32),
        vmem((nz, nxk, OWN, RANK), F32),
        vmem((channels, 4 * RANK), BF16),
        vmem((nz, nxk, OWN, 128), F32),
        vmem((RANK, channels), F32),
    ]
    sems = [pltpu.SemaphoreType.DMA((9,))]
    for count in (nz, nz, 2, nx, nx, 1, nz, ny, nx, nz, 1, ny, nz, ny, 4, 4, 4, 4):
        sems += [pltpu.SemaphoreType.DMA((count,))] * 2
    spec = pl.BlockSpec(memory_space=pltpu.VMEM)
    far = pl.BlockSpec(memory_space=pl.ANY)
    cor_shape = jax.ShapeDtypeStruct((nz, nxk, OWN, 128), F32)
    mids = (
        jax.ShapeDtypeStruct((7, 7, OWN), F32),
        jax.ShapeDtypeStruct((RANK, channels), F32),
        jax.ShapeDtypeStruct((RANK, 128), F32),
        jax.ShapeDtypeStruct((4 * RANK, 128), BF16),
        jax.ShapeDtypeStruct((channels, 4 * RANK), BF16),
        cor_shape,
    )
    parts = pl.pallas_call(
        functools.partial(kernel, ny, nz, nx),
        out_shape=mids,
        in_specs=[pl.BlockSpec(memory_space=pl.ANY)] * 6,
        out_specs=(spec, far, spec, spec, far, far),
        scratch_shapes=scratch + sems,
        compiler_params=pltpu.CompilerParams(
            collective_id=0, has_side_effects=True, vmem_limit_bytes=60 * 1024 * 1024
        ),
        cost_estimate=pl.CostEstimate(
            flops=600_000_000, bytes_accessed=4_000_000, transcendentals=0
        ),
    )(
        block_input.reshape(SIDE, SIDE, OWN),
        depth_kernel,
        w_expand,
        grad_hidden.reshape(POS, 128),
        error_old.reshape(nz, nxk, OWN, 128),
        right_init.T,
    )
    kg, left, right, err = pl.pallas_call(
        finish,
        out_shape=mids[0:3] + (cor_shape,),
        in_specs=[spec] * 6,
        out_specs=(spec,) * 4,
        compiler_params=pltpu.CompilerParams(vmem_limit_bytes=60 * 1024 * 1024),
        cost_estimate=pl.CostEstimate(
            flops=60_000_000, bytes_accessed=2_500_000, transcendentals=0
        ),
    )(*parts)
    return (
        kg,
        left.T,
        right.T,
        err.reshape(1, channels, 128),
    )


def solution(mesh, nx=NX):
    ny = mesh.shape["outer"]
    nz = mesh.shape["chip"] // (2 * nx)
    placed = (
        P("outer", None, None, "chip"),
        P(),
        P(None, "chip"),
        P("outer", None, None, "chip"),
        P("outer", None, "chip"),
        P("chip", None),
    )
    return jax.shard_map(
        functools.partial(on_device, ny, nz, nx),
        mesh=mesh,
        in_specs=placed,
        out_specs=(P(None, None, "chip"), P(), P("chip", None), P("outer", None, "chip")),
        check_vma=False,
    )
```

```python
import functools

import jax
import jax.numpy as jnp
from jax import lax
from jax.experimental import pallas as pl
from jax.experimental.pallas import tpu as pltpu
from jax.sharding import PartitionSpec as P

F32 = jnp.float32
BF16 = jnp.bfloat16
HIGH = lax.Precision.HIGHEST
MESH = pl.DeviceIdType.MESH

NX = 4
SIDE = 24
POS = SIDE * SIDE
LP = 640
LX = 896
OWN = 24
RANK = 32


def dot(a, b, dims, precision=None):
    return lax.dot_general(a, b, (dims, ((), ())), precision=precision, preferred_element_type=F32)


NN = ((1,), (0,))
NT = ((1,), (1,))
TN = ((0,), (0,))


def loop(lo, hi, body, unroll=1):
    def step(i, carry):
        body(i)
        return carry

    lax.fori_loop(lo, hi, step, 0, unroll=unroll)


def each_peer(count, body):
    for s in sorted(range(1, count), key=lambda s: -min(s, count - s)):
        body(s)


def split2(v):
    hi = v.astype(BF16)
    return hi, (v - hi.astype(F32)).astype(BF16)


def split3(v):
    hi = v.astype(BF16)
    rest = v - hi.astype(F32)
    mid = rest.astype(BF16)
    return hi, mid, (rest - mid.astype(F32)).astype(BF16)


def kernel(
    ny, nz, nx,
    x_hbm, k_hbm, w_hbm, gh_hbm, err_hbm, r_hbm,
    kg_out, left_out, right_out, w_out, ls4_out, cor_out,
    x_ref, k_ref, w_ref, err_ref, r_ref,
    ghp, ghs, ght, ws, rs, wf, x2, xo, conv24, cz, xz, xp, mk, kflat, kt, cvf, gr, gb, rh1, rh2, g32,
    eg, gg, es, cs, cg, gt, st, rz, ys, ll, chl, rp, kgt, rk, yk, lsn, ls4, cor, left,
    s_in,
    s_cz, r_cz, s_xz, r_xz, s_es, r_es, s_cs, r_cs, s_cg, r_cg, s_gt, r_gt, s_rz, r_rz, s_ys, r_ys, s_lx, r_lx, s_lz, r_lz,
    s_lk, r_lk, s_rp, r_rp, s_rk, r_rk, s_yk, r_yk, s_in2, r_in2, s_gx, r_gx, s_cx, r_cx, s_cc, r_cc,
):
    nxk = 2 * nx
    ch = OWN * nz
    channels = ch * nxk
    tpz = 8 // nz
    half = ch // 2
    top = 16 * nz
    workers = ny
    y = lax.axis_index("outer")
    chip = lax.axis_index("chip")
    z = chip // nxk
    xk = lax.rem(chip, nxk)
    x = xk // 2
    k = lax.rem(xk, 2)

    def zpeer(s):
        return lax.rem(z + s, nz)

    def at_z(zz):
        return (y, zz * nxk + xk)

    def at_x(xx):
        return (y, z * nxk + xx * 2 + k)

    right_x = lax.rem(x + 1, nx)
    left_x = lax.rem(x + nx - 1, nx)
    far_x = lax.rem(x + 2, nx)

    def at_y(yy):
        return (yy, chip)

    sibling = (y, z * nxk + x * 2 + (1 - k))

    def copy(src, dst, ssem, rsem, dev):
        return pltpu.make_async_remote_copy(
            src_ref=src, dst_ref=dst, send_sem=ssem, recv_sem=rsem,
            device_id=dev, device_id_type=MESH,
        )

    def slots(v):
        return jnp.concatenate(
            [v[:, 0:16].reshape(top, v.shape[2]), v[:, 16:24].reshape(ch - top, v.shape[2])], axis=0
        )

    def natural_rows(v):
        return jnp.concatenate(
            [v[0:top].reshape(nz, 16, v.shape[1]), v[top:ch].reshape(nz, 8, v.shape[1])], axis=1
        )

    load_x = pltpu.make_async_copy(x_hbm, x_ref, s_in.at[0])
    load_r = pltpu.make_async_copy(r_hbm, r_ref, s_in.at[1])
    load_err = pltpu.make_async_copy(err_hbm, err_ref, s_in.at[2])
    load_gh = pltpu.make_async_copy(gh_hbm, ghp.at[pl.ds(0, POS)], s_in.at[3])
    load_w = pltpu.make_async_copy(w_hbm, w_ref, s_in.at[4])
    load_k = pltpu.make_async_copy(k_hbm, k_ref, s_in.at[5])
    for load in (load_x, load_r, load_err, load_gh, load_w, load_k):
        load.start()

    barrier = pltpu.get_barrier_semaphore()

    def greet(dev):
        pl.semaphore_signal(barrier, inc=1, device_id=dev, device_id_type=MESH)

    loop(1, nz, lambda s: greet(at_z(zpeer(s))))
    loop(1, nx, lambda s: greet(at_x(lax.rem(x + s, nx))))
    greet(sibling)
    loop(1, ny, lambda s: greet(at_y(lax.rem(y + s, ny))))

    x2[POS:, :] = jnp.zeros((LP - POS, OWN), F32)
    load_x.wait()
    for i in range(SIDE):
        x2[SIDE * i : SIDE * (i + 1), :] = x_ref[i].astype(F32)
    eye = (
        lax.broadcasted_iota(jnp.int32, (32, OWN), 0)
        == lax.broadcasted_iota(jnp.int32, (32, OWN), 1)
    )
    own = dot(eye.astype(F32).astype(BF16), x2[...].astype(BF16), NT)[0:OWN]
    xo[:, 0:128] = jnp.zeros((OWN, 128), F32)
    xo[:, 128 : 128 + LP] = own
    xo[:, 128 + LP :] = jnp.zeros((OWN, LX - 128 - LP), F32)
    load_k.wait()
    for a in range(7):
        kflat[8 * a : 8 * a + 7, :] = k_ref[a]
        kflat[8 * a + 7 : 8 * a + 8, :] = jnp.zeros((1, channels), F32)
    kflat[56:64, :] = jnp.zeros((8, channels), F32)
    row = lax.broadcasted_iota(jnp.int32, (OWN, channels), 0)
    lane = lax.broadcasted_iota(jnp.int32, (OWN, channels), 1)
    pick = (lane - row == chip * OWN).astype(F32).astype(BF16)
    three = jnp.concatenate(split3(kflat[...]), axis=0)
    taps3 = dot(pick, three, NT)
    kt[...] = taps3[:, 0:64] + taps3[:, 64:128] + taps3[:, 128:192]
    pos = lax.broadcasted_iota(jnp.int32, (8, LP), 1)
    col = lax.rem(pos, SIDE) + lax.broadcasted_iota(jnp.int32, (8, LP), 0) - 3
    mk[...] = ((col >= 0) & (col < SIDE) & (pos < POS)).astype(F32)

    def shifted(v):
        return [pltpu.roll(v, LX - (96 + SIDE * (a - 3)), 1)[:, 0:LP] for a in range(7)]

    for t in range(OWN // 8):
        rows = slice(8 * t, 8 * t + 8)
        taps = kt[rows, :]
        moved = shifted(xo[rows, :])
        out = None
        for b in range(7):
            part = None
            for a in range(7):
                term = taps[:, 8 * a + b : 8 * a + b + 1] * moved[a]
                part = term if a == 0 else part + term
            part = pltpu.roll(part, LP - (32 + b - 3), 1) * mk[b : b + 1, :]
            out = part if b == 0 else out + part
        conv24[rows, :] = out

    lane_x = lax.broadcasted_iota(jnp.int32, (16, LX), 1)

    def pack(v):
        wide = jnp.concatenate([v, jnp.zeros((OWN, LX - LP), F32)], axis=1)
        last = wide[16:24]
        early = jnp.where(lane_x[0:8] < POS // 2, last, 0.0)
        late = jnp.where(lane_x[0:8] < POS // 2, 0.0, last)
        tail = jnp.concatenate(
            [pltpu.roll(early, POS, 1), pltpu.roll(late, POS // 2, 1)], axis=0
        )
        return (wide[0:16] + tail).astype(BF16)

    def unpack(v):
        v = v.astype(F32)
        early = pltpu.roll(v[0:8], LX - POS, 1)
        late = pltpu.roll(v[8:16], LX - POS // 2, 1)
        last = jnp.where(
            lane_x[0:8] < POS // 2, early, jnp.where(lane_x[0:8] < POS, late, 0.0)
        )
        return jnp.where(lane_x < POS, v, 0.0)[:, 0:LP], last[:, 0:LP]

    cz[z] = pack(conv24[...])

    def cz_copy(s):
        return copy(cz.at[z], cz.at[z], s_cz.at[s], r_cz.at[s], at_z(zpeer(s)))

    xz[z] = pack(own)

    pl.semaphore_wait(barrier, (nz - 1) + (nx - 1) + (ny - 1) + 1)

    each_peer(nz, lambda s: cz_copy(s).start())

    in_gh = copy(gh_hbm, ghs.at[pl.ds(0, POS)], s_in2.at[0], r_in2.at[0], sibling)
    in_r = copy(r_hbm, rs, s_in2.at[1], r_in2.at[1], sibling)
    in_w = copy(w_hbm, ws, s_in2.at[2], r_in2.at[2], sibling)
    for one in (in_r, in_gh, in_w):
        one.start()


    def xz_copy(s):
        return copy(xz.at[z], xz.at[z], s_xz.at[s], r_xz.at[s], at_z(zpeer(s)))


    load_r.wait()
    load_err.wait()
    rh, rl = split2(r_ref[...])
    four = jnp.concatenate(
        [jnp.concatenate([rh, rh], axis=1), jnp.concatenate([rl, rl], axis=1)], axis=0
    )
    for q in range(nxk):
        eh, el = split2(slots(err_ref[:, q]))
        rows = jnp.concatenate([eh, el], axis=1)
        if ch < 256:
            rows = jnp.concatenate([rows, jnp.zeros((256 - ch, 256), BF16)], axis=0)
        e = dot(four, rows, NT)
        e = e[0:32] + e[32:64]
        for rg in range(4):
            for part in range(2):
                eg[q // 2, q % 2, 2 * rg + part] = e[8 * rg : 8 * rg + 8, 128 * part : 128 * part + 128]

    es_copy = copy(eg.at[:, 1 - k], es, s_es.at[0], r_es.at[0], sibling)
    es_copy.start()

    ghp[POS:, :] = jnp.zeros((LP - POS, 128), BF16)
    ghs[POS:, :] = jnp.zeros((LP - POS, 128), BF16)

    load_gh.wait()
    halves_of = jnp.concatenate([ghp[0 : POS // 2, :], ghp[POS // 2 : POS, :]], axis=1)
    ght[...] = jnp.concatenate(
        [
            jnp.zeros((64, 256), BF16),
            halves_of,
            jnp.zeros((LX - 512 - 64 - POS // 2, 256), BF16),
        ],
        axis=0,
    )
    in_gh.wait_recv()
    in_r.wait_recv()
    sh, sl = split2(rs[...])
    both = jnp.concatenate([ghp[...], ghs[...]], axis=1)
    g = dot(
        jnp.concatenate([rh, sh, rl, sl], axis=1), jnp.concatenate([both, both], axis=1), NT
    )
    for rg in range(4):
        for j in range(5):
            gg[rg // 2, (rg % 2) * 5 + j] = g[8 * rg : 8 * rg + 8, 128 * j : 128 * j + 128]

    cg[x] = gg[k]

    def cg_copy(s):
        return copy(cg.at[x], cg.at[x], s_cg.at[s], r_cg.at[s], at_x(lax.rem(x + s, nx)))

    each_peer(nx, lambda s: cg_copy(s).start())

    es_copy.wait_recv()

    def chip_sum(xx):
        cs[xx, 0] = eg[xx, k] + es[xx]

    loop(0, nx, chip_sum)
    cs[x, 1] = cs[x, 0]

    def cs_copy(s):
        xx = lax.rem(x + s, nx)
        return copy(cs.at[xx, 0], cs.at[x, 1], s_cs.at[s], r_cs.at[s], at_x(xx))

    each_peer(nx, lambda s: cs_copy(s).start())

    load_w.wait()
    in_w.wait_recv()
    wf[:, :, :, :, 0:128] = w_ref[...].astype(F32).reshape(nz, nx, 2, OWN, 128)
    wf[:, :, :, :, 128:256] = ws[...].astype(F32).reshape(nz, nx, 2, OWN, 128)

    def grad_rows(xx):
        rows = wf[:, xx, k].reshape(ch, 256).astype(BF16)
        return dot(rows, jnp.concatenate([ghp[...], ghs[...]], axis=1), NT)

    gb[0] = grad_rows(far_x).astype(BF16)
    far_right = copy(
        gb.at[0, pl.ds(0, half)], rh1.at[0], s_gx.at[0], r_gx.at[0], at_x(right_x)
    )
    far_left = copy(
        gb.at[0, pl.ds(half, half)], rh1.at[1], s_gx.at[1], r_gx.at[1], at_x(left_x)
    )
    far_right.start()
    far_left.start()
    gr[0] = grad_rows(right_x)
    gr[1] = grad_rows(left_x)
    g32[...] = grad_rows(x)

    def cg_wait(s):
        got = cg.at[lax.rem(x - s + nx, nx)]
        copy(got, got, s_cg.at[s], r_cg.at[s], at_x(lax.rem(x + s, nx))).wait_recv()

    loop(1, nx, cg_wait)
    total = cg[0]
    for q in range(1, nx):
        total = total + cg[q]
    gt[k] = total
    gt_copy = copy(gt.at[k], gt.at[k], s_gt.at[0], r_gt.at[0], sibling)
    gt_copy.start()

    loop(1, nx, lambda s: cs_copy(s).wait_recv())
    total = cs[0, 1]
    for q in range(1, nx):
        total = total + cs[q, 1]
    st[...] = total

    loop(1, nz, lambda s: cz_copy(s).wait_recv())
    cvf[x, k] = cz[...]

    gt_copy.wait_recv()
    groups = []
    for rg in range(4):
        groups.append(
            jnp.concatenate([gt[rg // 2, (rg % 2) * 5 + j] for j in range(5)], axis=1)
        )
    gfull = jnp.concatenate(groups, axis=0)
    lane_g = lax.broadcasted_iota(jnp.int32, (32, LP), 1)
    inside = (lane_g >= 64) & (lane_g < 64 + POS // 2)
    glow = jnp.where(inside, pltpu.roll(gfull, 64, 1), 0.0)[:, 0 : LX - 512]
    ghigh = jnp.where(inside, pltpu.roll(gfull, LP + 64 - POS // 2, 1), 0.0)[:, 0 : LX - 512]
    packed = cz[...]
    halves = packed[:, :, 512:].astype(F32)
    conv_top = dot(
        jnp.concatenate(split2(gfull), axis=0), packed[:, :, 0:LP].reshape(top, LP), NT
    )
    conv_last = None
    for part, rows in ((glow, halves[:, 0:8]), (ghigh, halves[:, 8:16])):
        rows = rows.reshape(ch - top, LX - 512).astype(BF16)
        term = dot(jnp.concatenate(split2(part), axis=0), rows, NT)
        conv_last = term if conv_last is None else conv_last + term
    conv_left = jnp.concatenate(
        [
            conv_top[0:32] + conv_top[32:64],
            conv_last[0:32] + conv_last[32:64],
            jnp.zeros((32, 256 - ch), F32),
        ],
        axis=1,
    )
    for rg in range(4):
        for part in range(2):
            st[2 * rg + part] += conv_left[8 * rg : 8 * rg + 8, 128 * part : 128 * part + 128]

    def rz_copy(s):
        zz = zpeer(s)
        return copy(st.at[pl.ds(zz * tpz, tpz)], rz.at[z], s_rz.at[s], r_rz.at[s], at_z(zz))

    each_peer(nz, lambda s: rz_copy(s).start())
    rz[z] = st[pl.ds(z * tpz, tpz)]
    loop(1, nz, lambda s: xz_copy(s).start())

    far_right.wait_recv()
    gb[1, 0:half, :] = (gr[0, 0:half, :] + rh1[0].astype(F32)).astype(BF16)
    gb[1, half:, :] = gr[0, half:, :].astype(BF16)
    near_right = copy(gb.at[1], rh2.at[0], s_gx.at[2], r_gx.at[2], at_x(right_x))
    near_right.start()
    far_left.wait_recv()
    gb[2, 0:half, :] = gr[1, 0:half, :].astype(BF16)
    gb[2, half:, :] = (gr[1, half:, :] + rh1[1].astype(F32)).astype(BF16)
    near_left = copy(gb.at[2], rh2.at[1], s_gx.at[3], r_gx.at[3], at_x(left_x))
    near_left.start()

    mine = cvf.at[x, k]
    cx_copies = [
        copy(mine, mine, s_cx.at[0], r_cx.at[0], at_x(right_x)),
        copy(mine, mine, s_cx.at[1], r_cx.at[1], at_x(left_x)),
    ]
    for s in range(2):
        cx_copies[s].start()

    sources = (x, left_x, right_x, far_x)

    def cc_copy(s):
        block = cvf.at[sources[s], k]
        return copy(block, block, s_cc.at[s], r_cc.at[s], sibling)

    cc_copy(0).start()

    each_peer(nz, lambda s: rz_copy(s).wait_recv())
    total = rz[0]
    for q in range(1, nz):
        total = total + rz[q]
    ys[y] = total

    def ys_copy(s):
        return copy(ys.at[y], ys.at[y], s_ys.at[s], r_ys.at[s], at_y(lax.rem(y + s, ny)))

    each_peer(ny, lambda s: ys_copy(s).start())

    def local_grad(xx, kk):
        q = xx * 2 + kk
        packed = cvf[xx, kk].reshape(top, LX)
        first = dot(packed[:, 0:LP], ghp[...], NN)
        both = dot(packed[:, 512:], ght[...], NN).reshape(nz, 16, 256)
        last = both[:, 0:8, 0:128] + both[:, 8:16, 128:256]
        part = jnp.concatenate([first, last.reshape(ch - top, 128)], axis=0) + slots(err_ref[:, q])
        cor[:, q] = natural_rows(part)
        chl[q, 0:ch, :] = jnp.concatenate(split2(part), axis=1)

    if ch < 256:
        chl[:, ch:, :] = jnp.zeros((nxk, 256 - ch, 256), BF16)
    each_peer(ny, lambda s: ys_copy(s).wait_recv())
    total = ys[0]
    for q in range(1, ny):
        total = total + ys[q]
    ll[k, z, x] = total

    def lx_copy(s):
        own = ll.at[k, z, x]
        return copy(own, own, s_lx.at[s], r_lx.at[s], at_x(lax.rem(x + s, nx)))

    each_peer(nx, lambda s: lx_copy(s).start())

    local_grad(x, k)

    loop(1, nz, lambda s: xz_copy(s).wait_recv())
    xp[:, 0:128] = jnp.zeros((ch, 128), F32)
    xp[:, 128 + LP :] = jnp.zeros((ch, LX - 128 - LP), F32)
    for zz in range(nz):
        first, last = unpack(xz[zz])
        xp[OWN * zz : OWN * zz + 16, 128 : 128 + LP] = first
        xp[OWN * zz + 16 : OWN * zz + 24, 128 : 128 + LP] = last
    near_right.wait_recv()
    near_left.wait_recv()
    g32[...] += rh2[0].astype(F32) + rh2[1].astype(F32)
    pair_row = lax.broadcasted_iota(jnp.int32, (OWN, 7 * OWN), 0)
    pair_lane = lax.broadcasted_iota(jnp.int32, (OWN, 7 * OWN), 1)
    diagonal = lax.rem(pair_lane, OWN) == pair_row
    tap_row = lax.broadcasted_iota(jnp.int32, (8, 7 * OWN), 0)

    def kernel_terms(zz):
        rows = pl.ds(pl.multiple_of(zz * OWN, 8), OWN)
        maps = jnp.concatenate(shifted(xp[rows, :]), axis=0).astype(BF16)
        gt = g32[rows, :]
        moved = [pltpu.roll(gt * mk[b : b + 1, :], 32 + b - 3, 1) for b in range(7)]
        hi, lo = split2(jnp.concatenate(moved, axis=0))
        pairs = dot(hi, maps, NT) + dot(lo, maps, NT)
        out = jnp.zeros((8, 7 * OWN), F32)
        for b in range(7):
            block = jnp.where(diagonal, pairs[OWN * b : OWN * (b + 1)], 0.0)
            one = jnp.sum(block, axis=0, keepdims=True)
            out = jnp.where(tap_row == b, one, out)
        kgt[zz] = jnp.concatenate([out, jnp.zeros((8, 256 - 7 * OWN), F32)], axis=1)

    loop(0, nz, kernel_terms, 2)

    def rk_copy(s):
        zz = zpeer(s)
        return copy(kgt.at[zz], rk.at[z], s_rk.at[s], r_rk.at[s], at_z(zz))

    each_peer(nz, lambda s: rk_copy(s).start())
    rk[z] = kgt[z]

    def lx_wait(s):
        got = ll.at[k, z, lax.rem(x - s + nx, nx)]
        copy(got, got, s_lx.at[s], r_lx.at[s], at_x(lax.rem(x + s, nx))).wait_recv()

    loop(1, nx, lx_wait)

    def lz_copy(s):
        own = ll.at[k, z]
        return copy(own, own, s_lz.at[s], r_lz.at[s], at_z(zpeer(s)))

    each_peer(nz, lambda s: lz_copy(s).start())

    cx_copies[0].wait_recv()
    part0 = cvf.at[left_x, k, pl.ds(0, nz // 2)]
    cx_copies.append(copy(part0, part0, s_cx.at[2], r_cx.at[2], at_x(right_x)))
    cx_copies[2].start()
    cc_copy(1).start()
    cx_copies[1].wait_recv()
    part1 = cvf.at[right_x, k, pl.ds(nz // 2, nz // 2)]
    cx_copies.append(copy(part1, part1, s_cx.at[3], r_cx.at[3], at_x(left_x)))
    cx_copies[3].start()
    cc_copy(2).start()
    local_grad(left_x, k)
    local_grad(right_x, k)

    for s in range(3):
        cc_copy(s).wait_recv()
        local_grad(sources[s], 1 - k)

    loop(1, nz, lambda s: rk_copy(s).wait_recv())
    total = rk[0]
    for q in range(1, nz):
        total = total + rk[q]
    yk[y] = total

    def yk_copy(s):
        return copy(yk.at[y], yk.at[y], s_yk.at[s], r_yk.at[s], at_y(lax.rem(y + s, ny)))

    each_peer(ny, lambda s: yk_copy(s).start())

    def lz_wait(s):
        got = ll.at[k, lax.rem(z - s + nz, nz)]
        copy(got, got, s_lz.at[s], r_lz.at[s], at_z(zpeer(s))).wait_recv()

    loop(1, nz, lz_wait)
    lk_copy = copy(ll.at[k], ll.at[k], s_lk.at[0], r_lk.at[0], sibling)
    lk_copy.start()

    cx_copies[2].wait_recv()
    cx_copies[3].wait_recv()
    cc_copy(3).start()
    local_grad(far_x, k)

    lk_copy.wait_recv()

    def left_of(q):
        rows = []
        for rg in range(4):
            tiles = [ll[q % 2, t // tpz, q // 2, t % tpz] for t in (2 * rg, 2 * rg + 1)]
            rows.append(jnp.concatenate(tiles, axis=1))
        return jnp.concatenate(rows, axis=0)

    lefts = [left_of(q) for q in range(nxk)]
    wide3 = split3(jnp.concatenate(lefts, axis=1))
    stack3 = jnp.concatenate(wide3, axis=0)
    gram = None
    for part in wide3:
        term = dot(stack3, part, NT)
        term = term[0:32] + term[32:64] + term[64:96]
        gram = term if gram is None else gram + term
    for q in range(nxk):
        lsn[:, q] = natural_rows(lefts[q].T)
    natural = lsn[...].reshape(channels, RANK).T
    nh, nm, nl = split3(natural)
    ls4[...] = jnp.concatenate([nh, nm, nh, nm], axis=0).T
    ls4_store = pltpu.make_async_copy(ls4, ls4_out, s_in.at[7])
    ls4_store.start()

    cc_copy(3).wait_recv()
    local_grad(far_x, 1 - k)
    cor_store = pltpu.make_async_copy(cor, cor_out, s_in.at[6])
    cor_store.start()

    right = None
    for q in range(nxk):
        term = dot(jnp.concatenate(split2(lefts[q]), axis=0), chl[q], NN)
        right = term if q == 0 else right + term
    right = right[0:32] + right[32:64]
    rp[y] = right[:, 0:128] + right[:, 128:256]

    def rp_copy(s):
        return copy(rp.at[y], rp.at[y], s_rp.at[s], r_rp.at[s], at_y(lax.rem(y + s, ny)))

    each_peer(ny, lambda s: rp_copy(s).start())

    row_id = lax.broadcasted_iota(jnp.int32, (RANK, RANK), 0)
    lane_id = lax.broadcasted_iota(jnp.int32, (RANK, RANK), 1)
    same = row_id == lane_id
    aug = jnp.concatenate([gram, same.astype(F32)], axis=1)
    row_col = lax.broadcasted_iota(jnp.int32, (RANK, 2 * RANK), 0)

    def full(v):
        return jnp.broadcast_to(v, (RANK, 2 * RANK))

    for i in range(0, RANK, 2):
        c0 = full(aug[:, i : i + 1])
        c1 = full(aug[:, i + 1 : i + 2])
        r0 = full(aug[i : i + 1, :])
        r1 = full(aug[i + 1 : i + 2, :])
        p00 = full(c0[i : i + 1, :])
        p01 = full(c1[i : i + 1, :])
        p11 = full(c1[i + 1 : i + 2, :])
        inv = 1.0 / (p00 * p11 - p01 * p01)
        u0 = (p11 * c0 - p01 * c1) * inv
        u1 = (p00 * c1 - p01 * c0) * inv
        u0 = jnp.where(row_col > i + 1, u0, jnp.where(row_col == i + 1, p01 / p00, 0.0))
        u1 = jnp.where(row_col > i + 1, u1, 0.0)
        aug = aug - u0 * r0 - u1 * r1
    diag = jnp.sum(jnp.where(same, aug[:, 0:RANK], 0.0), axis=1, keepdims=True)
    scale = lax.rsqrt(diag)
    scale = scale * (1.5 - 0.5 * diag * scale * scale)
    linv = aug[:, RANK:] * scale
    ih, im, il = split3(linv)
    left[...] = dot(
        jnp.concatenate([ih, ih, ih, im, im, il], axis=1),
        jnp.concatenate([nh, nm, nl, nh, nm, nh], axis=0),
        NN,
    )
    left_store = pltpu.make_async_copy(left, left_out, s_in.at[8])
    left_store.start()

    inverse = dot(linv.T, linv, NN, HIGH) * (1.0 / workers)
    ah, am, al = split3(jnp.concatenate([linv, inverse], axis=0))
    final_left = jnp.concatenate([ah, ah, ah, am, am, al], axis=1)

    each_peer(ny, lambda s: rp_copy(s).wait_recv())
    total = rp[0]
    for q in range(1, ny):
        total = total + rp[q]
    th, tm, tl = split3(total)
    solved = dot(final_left, jnp.concatenate([th, tm, tl, th, tm, th], axis=0), NN)
    right_out[...] = solved[0:RANK]
    wh, wl = split2(solved[RANK:])
    w_out[...] = jnp.concatenate([wh, wh, wl, wl], axis=0)

    loop(1, ny, lambda s: yk_copy(s).wait_recv())
    total = yk[0]
    for q in range(1, ny):
        total = total + yk[q]
    for a in range(7):
        kg_out[a] = total[0:7, OWN * a : OWN * (a + 1)]

    for one in (cor_store, ls4_store, left_store):
        one.wait()
    loop(1, nz, lambda s: cz_copy(s).wait_send())
    loop(1, nz, lambda s: xz_copy(s).wait_send())
    es_copy.wait_send()
    for one in (in_r, in_gh, in_w):
        one.wait_send()
    loop(1, nx, lambda s: cs_copy(s).wait_send())
    loop(1, nx, lambda s: cg_copy(s).wait_send())
    gt_copy.wait_send()
    loop(1, nz, lambda s: rz_copy(s).wait_send())
    loop(1, ny, lambda s: ys_copy(s).wait_send())
    loop(1, nx, lambda s: lx_copy(s).wait_send())
    loop(1, nz, lambda s: lz_copy(s).wait_send())
    lk_copy.wait_send()
    loop(1, ny, lambda s: rp_copy(s).wait_send())
    loop(1, nz, lambda s: rk_copy(s).wait_send())
    loop(1, ny, lambda s: yk_copy(s).wait_send())
    for s in range(4):
        cx_copies[s].wait_send()
        cc_copy(s).wait_send()
    for one in (far_right, far_left, near_right, near_left):
        one.wait_send()


def finish(kg_ref, left_ref, right_ref, w_ref, ls_ref, cor_ref, kg_out, left_out, right_out, err_out):
    kg_out[...] = kg_ref[...]
    left_out[...] = left_ref[...]
    right_out[...] = right_ref[...]
    approx = dot(ls_ref[...], w_ref[...], NN)
    err_out[...] = cor_ref[...] - approx.reshape(cor_ref.shape)


def on_device(ny, nz, nx, block_input, depth_kernel, w_expand, grad_hidden, error_old, right_init):
    nxk = 2 * nx
    ch = OWN * nz
    channels = nz * nxk * OWN
    tpz = 8 // nz
    hid = right_init.shape[0]
    vmem = pltpu.VMEM
    scratch = [
        vmem((SIDE, SIDE, OWN), BF16),
        vmem((7, 7, channels), F32),
        vmem((channels, 128), BF16),
        vmem((nz, nxk, OWN, 128), F32),
        vmem((RANK, 128), F32),
        vmem((LP, 128), BF16),
        vmem((LP, 128), BF16),
        vmem((LX - 512, 256), BF16),
        vmem((channels, 128), BF16),
        vmem((RANK, 128), F32),
        vmem((nz, nx, 2, OWN, 256), F32),
        vmem((LP, OWN), F32),
        vmem((OWN, LX), F32),
        vmem((OWN, LP), F32),
        vmem((nz, 16, LX), BF16),
        vmem((nz, 16, LX), BF16),
        vmem((ch, LX), F32),
        vmem((8, LP), F32),
        vmem((64, channels), F32),
        vmem((OWN, 64), F32),
        vmem((nx, 2, nz, 16, LX), BF16),
        vmem((2, ch, LP), F32),
        vmem((3, ch, LP), BF16),
        vmem((2, ch // 2, LP), BF16),
        vmem((2, ch, LP), BF16),
        vmem((ch, LP), F32),
        vmem((nx, 2, 8, 8, 128), F32),
        vmem((2, 10, 8, 128), F32),
        vmem((nx, 8, 8, 128), F32),
        vmem((nx, 2, 8, 8, 128), F32),
        vmem((nx, 10, 8, 128), F32),
        vmem((2, 10, 8, 128), F32),
        vmem((8, 8, 128), F32),
        vmem((nz, tpz, 8, 128), F32),
        vmem((ny, tpz, 8, 128), F32),
        vmem((2, nz, nx, tpz, 8, 128), F32),
        vmem((nxk, 256, 256), BF16),
        vmem((ny, RANK, 128), F32),
        vmem((nz, 8, 256), F32),
        vmem((nz, 8, 256), F32),
        vmem((ny, 8, 256), F32),
        vmem((nz, nxk, OWN, RANK), F32),
        vmem((channels, 4 * RANK), BF16),
        vmem((nz, nxk, OWN, 128), F32),
        vmem((RANK, channels), F32),
    ]
    sems = [pltpu.SemaphoreType.DMA((9,))]
    for count in (nz, nz, 2, nx, nx, 1, nz, ny, nx, nz, 1, ny, nz, ny, 4, 4, 4, 4):
        sems += [pltpu.SemaphoreType.DMA((count,))] * 2
    spec = pl.BlockSpec(memory_space=pltpu.VMEM)
    far = pl.BlockSpec(memory_space=pl.ANY)
    cor_shape = jax.ShapeDtypeStruct((nz, nxk, OWN, 128), F32)
    mids = (
        jax.ShapeDtypeStruct((7, 7, OWN), F32),
        jax.ShapeDtypeStruct((RANK, channels), F32),
        jax.ShapeDtypeStruct((RANK, 128), F32),
        jax.ShapeDtypeStruct((4 * RANK, 128), BF16),
        jax.ShapeDtypeStruct((channels, 4 * RANK), BF16),
        cor_shape,
    )
    parts = pl.pallas_call(
        functools.partial(kernel, ny, nz, nx),
        out_shape=mids,
        in_specs=[pl.BlockSpec(memory_space=pl.ANY)] * 6,
        out_specs=(spec, far, spec, spec, far, far),
        scratch_shapes=scratch + sems,
        compiler_params=pltpu.CompilerParams(
            collective_id=0, has_side_effects=True, vmem_limit_bytes=60 * 1024 * 1024
        ),
        cost_estimate=pl.CostEstimate(
            flops=600_000_000, bytes_accessed=4_000_000, transcendentals=0
        ),
    )(
        block_input.reshape(SIDE, SIDE, OWN),
        depth_kernel,
        w_expand,
        grad_hidden.reshape(POS, 128),
        error_old.reshape(nz, nxk, OWN, 128),
        right_init.T,
    )
    kg, left, right, err = pl.pallas_call(
        finish,
        out_shape=mids[0:3] + (cor_shape,),
        in_specs=[spec] * 6,
        out_specs=(spec,) * 4,
        compiler_params=pltpu.CompilerParams(vmem_limit_bytes=60 * 1024 * 1024),
        cost_estimate=pl.CostEstimate(
            flops=60_000_000, bytes_accessed=2_500_000, transcendentals=0
        ),
    )(*parts)
    return (
        kg,
        left.T,
        right.T,
        err.reshape(1, channels, 128),
    )


def solution(mesh, nx=NX):
    ny = mesh.shape["outer"]
    nz = mesh.shape["chip"] // (2 * nx)
    placed = (
        P("outer", None, None, "chip"),
        P(),
        P(None, "chip"),
        P("outer", None, None, "chip"),
        P("outer", None, "chip"),
        P("chip", None),
    )
    return jax.shard_map(
        functools.partial(on_device, ny, nz, nx),
        mesh=mesh,
        in_specs=placed,
        out_specs=(P(None, None, "chip"), P(), P("chip", None), P("outer", None, "chip")),
        check_vma=False,
    )
```

```python
import functools

import jax
import jax.numpy as jnp
from jax import lax
from jax.experimental import pallas as pl
from jax.experimental.pallas import tpu as pltpu
from jax.sharding import PartitionSpec as P

F32 = jnp.float32
BF16 = jnp.bfloat16
HIGH = lax.Precision.HIGHEST
MESH = pl.DeviceIdType.MESH

NX = 4
SIDE = 24
POS = SIDE * SIDE
LP = 640
LX = 896
OWN = 24
RANK = 32


def dot(a, b, dims, precision=None):
    return lax.dot_general(a, b, (dims, ((), ())), precision=precision, preferred_element_type=F32)


NN = ((1,), (0,))
NT = ((1,), (1,))
TN = ((0,), (0,))


def loop(lo, hi, body, unroll=1):
    def step(i, carry):
        body(i)
        return carry

    lax.fori_loop(lo, hi, step, 0, unroll=unroll)


def split2(v):
    hi = v.astype(BF16)
    return hi, (v - hi.astype(F32)).astype(BF16)


def split3(v):
    hi = v.astype(BF16)
    rest = v - hi.astype(F32)
    mid = rest.astype(BF16)
    return hi, mid, (rest - mid.astype(F32)).astype(BF16)


def kernel(
    ny, nz, nx,
    x_hbm, k_hbm, w_hbm, gh_hbm, err_hbm, r_hbm,
    kg_out, left_out, right_out, w_out, ls4_out, cor_out,
    x_ref, k_ref, w_ref, err_ref, r_ref,
    ghp, ghs, ght, ws, rs, wf, x2, xo, conv24, cz, xz, xp, mk, kflat, kt, cvf, gr, gb, rh1, rh2, g32,
    eg, gg, es, cs, cg, gt, st, rz, ys, ll, chl, rp, kgt, rk, yk, lsn, ls4, cor, left,
    s_in,
    s_cz, r_cz, s_xz, r_xz, s_es, r_es, s_cs, r_cs, s_cg, r_cg, s_gt, r_gt, s_rz, r_rz, s_ys, r_ys, s_lx, r_lx, s_lz, r_lz,
    s_lk, r_lk, s_rp, r_rp, s_rk, r_rk, s_yk, r_yk, s_in2, r_in2, s_gx, r_gx, s_cx, r_cx, s_cc, r_cc,
):
    nxk = 2 * nx
    ch = OWN * nz
    channels = ch * nxk
    tpz = 8 // nz
    half = ch // 2
    top = 16 * nz
    workers = ny
    y = lax.axis_index("outer")
    chip = lax.axis_index("chip")
    z = chip // nxk
    xk = lax.rem(chip, nxk)
    x = xk // 2
    k = lax.rem(xk, 2)

    def zpeer(s):
        return lax.rem(z + s, nz)

    def at_z(zz):
        return (y, zz * nxk + xk)

    def at_x(xx):
        return (y, z * nxk + xx * 2 + k)

    right_x = lax.rem(x + 1, nx)
    left_x = lax.rem(x + nx - 1, nx)
    far_x = lax.rem(x + 2, nx)

    def at_y(yy):
        return (yy, chip)

    sibling = (y, z * nxk + x * 2 + (1 - k))

    def copy(src, dst, ssem, rsem, dev):
        return pltpu.make_async_remote_copy(
            src_ref=src, dst_ref=dst, send_sem=ssem, recv_sem=rsem,
            device_id=dev, device_id_type=MESH,
        )

    def slots(v):
        return jnp.concatenate(
            [v[:, 0:16].reshape(top, v.shape[2]), v[:, 16:24].reshape(ch - top, v.shape[2])], axis=0
        )

    def natural_rows(v):
        return jnp.concatenate(
            [v[0:top].reshape(nz, 16, v.shape[1]), v[top:ch].reshape(nz, 8, v.shape[1])], axis=1
        )

    load_x = pltpu.make_async_copy(x_hbm, x_ref, s_in.at[0])
    load_r = pltpu.make_async_copy(r_hbm, r_ref, s_in.at[1])
    load_err = pltpu.make_async_copy(err_hbm, err_ref, s_in.at[2])
    load_gh = pltpu.make_async_copy(gh_hbm, ghp.at[pl.ds(0, POS)], s_in.at[3])
    load_w = pltpu.make_async_copy(w_hbm, w_ref, s_in.at[4])
    load_k = pltpu.make_async_copy(k_hbm, k_ref, s_in.at[5])
    for load in (load_x, load_r, load_err, load_gh, load_w, load_k):
        load.start()

    barrier = pltpu.get_barrier_semaphore()

    def greet(dev):
        pl.semaphore_signal(barrier, inc=1, device_id=dev, device_id_type=MESH)

    loop(1, nz, lambda s: greet(at_z(zpeer(s))))
    loop(1, nx, lambda s: greet(at_x(lax.rem(x + s, nx))))
    greet(sibling)
    loop(1, ny, lambda s: greet(at_y(lax.rem(y + s, ny))))

    x2[POS:, :] = jnp.zeros((LP - POS, OWN), F32)
    load_x.wait()
    for i in range(SIDE):
        x2[SIDE * i : SIDE * (i + 1), :] = x_ref[i].astype(F32)
    eye = (
        lax.broadcasted_iota(jnp.int32, (32, OWN), 0)
        == lax.broadcasted_iota(jnp.int32, (32, OWN), 1)
    )
    own = dot(eye.astype(F32).astype(BF16), x2[...].astype(BF16), NT)[0:OWN]
    xo[:, 0:128] = jnp.zeros((OWN, 128), F32)
    xo[:, 128 : 128 + LP] = own
    xo[:, 128 + LP :] = jnp.zeros((OWN, LX - 128 - LP), F32)
    load_k.wait()
    for a in range(7):
        kflat[8 * a : 8 * a + 7, :] = k_ref[a]
        kflat[8 * a + 7 : 8 * a + 8, :] = jnp.zeros((1, channels), F32)
    kflat[56:64, :] = jnp.zeros((8, channels), F32)
    row = lax.broadcasted_iota(jnp.int32, (OWN, channels), 0)
    lane = lax.broadcasted_iota(jnp.int32, (OWN, channels), 1)
    pick = (lane - row == chip * OWN).astype(F32).astype(BF16)
    three = jnp.concatenate(split3(kflat[...]), axis=0)
    taps3 = dot(pick, three, NT)
    kt[...] = taps3[:, 0:64] + taps3[:, 64:128] + taps3[:, 128:192]
    pos = lax.broadcasted_iota(jnp.int32, (8, LP), 1)
    col = lax.rem(pos, SIDE) + lax.broadcasted_iota(jnp.int32, (8, LP), 0) - 3
    mk[...] = ((col >= 0) & (col < SIDE) & (pos < POS)).astype(F32)

    def shifted(v):
        return [pltpu.roll(v, LX - (96 + SIDE * (a - 3)), 1)[:, 0:LP] for a in range(7)]

    for t in range(OWN // 8):
        rows = slice(8 * t, 8 * t + 8)
        taps = kt[rows, :]
        moved = shifted(xo[rows, :])
        out = None
        for b in range(7):
            part = None
            for a in range(7):
                term = taps[:, 8 * a + b : 8 * a + b + 1] * moved[a]
                part = term if a == 0 else part + term
            part = pltpu.roll(part, LP - (32 + b - 3), 1) * mk[b : b + 1, :]
            out = part if b == 0 else out + part
        conv24[rows, :] = out

    lane_x = lax.broadcasted_iota(jnp.int32, (16, LX), 1)

    def pack(v):
        wide = jnp.concatenate([v, jnp.zeros((OWN, LX - LP), F32)], axis=1)
        last = wide[16:24]
        early = jnp.where(lane_x[0:8] < POS // 2, last, 0.0)
        late = jnp.where(lane_x[0:8] < POS // 2, 0.0, last)
        tail = jnp.concatenate(
            [pltpu.roll(early, POS, 1), pltpu.roll(late, POS // 2, 1)], axis=0
        )
        return (wide[0:16] + tail).astype(BF16)

    def unpack(v):
        v = v.astype(F32)
        early = pltpu.roll(v[0:8], LX - POS, 1)
        late = pltpu.roll(v[8:16], LX - POS // 2, 1)
        last = jnp.where(
            lane_x[0:8] < POS // 2, early, jnp.where(lane_x[0:8] < POS, late, 0.0)
        )
        return jnp.where(lane_x < POS, v, 0.0)[:, 0:LP], last[:, 0:LP]

    cz[z] = pack(conv24[...])

    def cz_copy(s):
        return copy(cz.at[z], cz.at[z], s_cz.at[s], r_cz.at[s], at_z(zpeer(s)))

    xz[z] = pack(own)

    pl.semaphore_wait(barrier, (nz - 1) + (nx - 1) + (ny - 1) + 1)

    loop(1, nz, lambda s: cz_copy(s).start())

    in_gh = copy(gh_hbm, ghs.at[pl.ds(0, POS)], s_in2.at[0], r_in2.at[0], sibling)
    in_r = copy(r_hbm, rs, s_in2.at[1], r_in2.at[1], sibling)
    in_w = copy(w_hbm, ws, s_in2.at[2], r_in2.at[2], sibling)
    for one in (in_r, in_gh, in_w):
        one.start()


    def xz_copy(s):
        return copy(xz.at[z], xz.at[z], s_xz.at[s], r_xz.at[s], at_z(zpeer(s)))


    load_r.wait()
    load_err.wait()
    rh, rl = split2(r_ref[...])
    four = jnp.concatenate(
        [jnp.concatenate([rh, rh], axis=1), jnp.concatenate([rl, rl], axis=1)], axis=0
    )
    for q in range(nxk):
        eh, el = split2(slots(err_ref[:, q]))
        rows = jnp.concatenate([eh, el], axis=1)
        if ch < 256:
            rows = jnp.concatenate([rows, jnp.zeros((256 - ch, 256), BF16)], axis=0)
        e = dot(four, rows, NT)
        e = e[0:32] + e[32:64]
        for rg in range(4):
            for part in range(2):
                eg[q // 2, q % 2, 2 * rg + part] = e[8 * rg : 8 * rg + 8, 128 * part : 128 * part + 128]

    es_copy = copy(eg.at[:, 1 - k], es, s_es.at[0], r_es.at[0], sibling)
    es_copy.start()

    ghp[POS:, :] = jnp.zeros((LP - POS, 128), BF16)
    ghs[POS:, :] = jnp.zeros((LP - POS, 128), BF16)

    load_gh.wait()
    halves_of = jnp.concatenate([ghp[0 : POS // 2, :], ghp[POS // 2 : POS, :]], axis=1)
    ght[...] = jnp.concatenate(
        [
            jnp.zeros((64, 256), BF16),
            halves_of,
            jnp.zeros((LX - 512 - 64 - POS // 2, 256), BF16),
        ],
        axis=0,
    )
    in_gh.wait_recv()
    in_r.wait_recv()
    sh, sl = split2(rs[...])
    both = jnp.concatenate([ghp[...], ghs[...]], axis=1)
    g = dot(
        jnp.concatenate([rh, sh, rl, sl], axis=1), jnp.concatenate([both, both], axis=1), NT
    )
    for rg in range(4):
        for j in range(5):
            gg[rg // 2, (rg % 2) * 5 + j] = g[8 * rg : 8 * rg + 8, 128 * j : 128 * j + 128]

    cg[x] = gg[k]

    def cg_copy(s):
        return copy(cg.at[x], cg.at[x], s_cg.at[s], r_cg.at[s], at_x(lax.rem(x + s, nx)))

    loop(1, nx, lambda s: cg_copy(s).start())

    es_copy.wait_recv()

    def chip_sum(xx):
        cs[xx, 0] = eg[xx, k] + es[xx]

    loop(0, nx, chip_sum)
    cs[x, 1] = cs[x, 0]

    def cs_copy(s):
        xx = lax.rem(x + s, nx)
        return copy(cs.at[xx, 0], cs.at[x, 1], s_cs.at[s], r_cs.at[s], at_x(xx))

    loop(1, nx, lambda s: cs_copy(s).start())

    load_w.wait()
    in_w.wait_recv()
    wf[:, :, :, :, 0:128] = w_ref[...].astype(F32).reshape(nz, nx, 2, OWN, 128)
    wf[:, :, :, :, 128:256] = ws[...].astype(F32).reshape(nz, nx, 2, OWN, 128)

    def grad_rows(xx):
        rows = wf[:, xx, k].reshape(ch, 256).astype(BF16)
        return dot(rows, jnp.concatenate([ghp[...], ghs[...]], axis=1), NT)

    gb[0] = grad_rows(far_x).astype(BF16)
    far_right = copy(
        gb.at[0, pl.ds(0, half)], rh1.at[0], s_gx.at[0], r_gx.at[0], at_x(right_x)
    )
    far_left = copy(
        gb.at[0, pl.ds(half, half)], rh1.at[1], s_gx.at[1], r_gx.at[1], at_x(left_x)
    )
    far_right.start()
    far_left.start()
    gr[0] = grad_rows(right_x)
    gr[1] = grad_rows(left_x)
    g32[...] = grad_rows(x)

    def cg_wait(s):
        got = cg.at[lax.rem(x - s + nx, nx)]
        copy(got, got, s_cg.at[s], r_cg.at[s], at_x(lax.rem(x + s, nx))).wait_recv()

    loop(1, nx, cg_wait)
    total = cg[0]
    for q in range(1, nx):
        total = total + cg[q]
    gt[k] = total
    gt_copy = copy(gt.at[k], gt.at[k], s_gt.at[0], r_gt.at[0], sibling)
    gt_copy.start()

    loop(1, nx, lambda s: cs_copy(s).wait_recv())
    total = cs[0, 1]
    for q in range(1, nx):
        total = total + cs[q, 1]
    st[...] = total

    loop(1, nz, lambda s: cz_copy(s).wait_recv())
    cvf[x, k] = cz[...]

    gt_copy.wait_recv()
    groups = []
    for rg in range(4):
        groups.append(
            jnp.concatenate([gt[rg // 2, (rg % 2) * 5 + j] for j in range(5)], axis=1)
        )
    gfull = jnp.concatenate(groups, axis=0)
    lane_g = lax.broadcasted_iota(jnp.int32, (32, LP), 1)
    inside = (lane_g >= 64) & (lane_g < 64 + POS // 2)
    glow = jnp.where(inside, pltpu.roll(gfull, 64, 1), 0.0)[:, 0 : LX - 512]
    ghigh = jnp.where(inside, pltpu.roll(gfull, LP + 64 - POS // 2, 1), 0.0)[:, 0 : LX - 512]
    packed = cz[...]
    halves = packed[:, :, 512:].astype(F32)
    conv_top = dot(
        jnp.concatenate(split2(gfull), axis=0), packed[:, :, 0:LP].reshape(top, LP), NT
    )
    conv_last = None
    for part, rows in ((glow, halves[:, 0:8]), (ghigh, halves[:, 8:16])):
        rows = rows.reshape(ch - top, LX - 512).astype(BF16)
        term = dot(jnp.concatenate(split2(part), axis=0), rows, NT)
        conv_last = term if conv_last is None else conv_last + term
    conv_left = jnp.concatenate(
        [
            conv_top[0:32] + conv_top[32:64],
            conv_last[0:32] + conv_last[32:64],
            jnp.zeros((32, 256 - ch), F32),
        ],
        axis=1,
    )
    for rg in range(4):
        for part in range(2):
            st[2 * rg + part] += conv_left[8 * rg : 8 * rg + 8, 128 * part : 128 * part + 128]

    def rz_copy(s):
        zz = zpeer(s)
        return copy(st.at[pl.ds(zz * tpz, tpz)], rz.at[z], s_rz.at[s], r_rz.at[s], at_z(zz))

    loop(1, nz, lambda s: rz_copy(s).start())
    rz[z] = st[pl.ds(z * tpz, tpz)]
    loop(1, nz, lambda s: xz_copy(s).start())

    far_right.wait_recv()
    gb[1, 0:half, :] = (gr[0, 0:half, :] + rh1[0].astype(F32)).astype(BF16)
    gb[1, half:, :] = gr[0, half:, :].astype(BF16)
    near_right = copy(gb.at[1], rh2.at[0], s_gx.at[2], r_gx.at[2], at_x(right_x))
    near_right.start()
    far_left.wait_recv()
    gb[2, 0:half, :] = gr[1, 0:half, :].astype(BF16)
    gb[2, half:, :] = (gr[1, half:, :] + rh1[1].astype(F32)).astype(BF16)
    near_left = copy(gb.at[2], rh2.at[1], s_gx.at[3], r_gx.at[3], at_x(left_x))
    near_left.start()

    mine = cvf.at[x, k]
    cx_copies = [
        copy(mine, mine, s_cx.at[0], r_cx.at[0], at_x(right_x)),
        copy(mine, mine, s_cx.at[1], r_cx.at[1], at_x(left_x)),
    ]
    for s in range(2):
        cx_copies[s].start()

    sources = (x, left_x, right_x, far_x)

    def cc_copy(s):
        block = cvf.at[sources[s], k]
        return copy(block, block, s_cc.at[s], r_cc.at[s], sibling)

    cc_copy(0).start()

    loop(1, nz, lambda s: rz_copy(s).wait_recv())
    total = rz[0]
    for q in range(1, nz):
        total = total + rz[q]
    ys[y] = total

    def ys_copy(s):
        return copy(ys.at[y], ys.at[y], s_ys.at[s], r_ys.at[s], at_y(lax.rem(y + s, ny)))

    loop(1, ny, lambda s: ys_copy(s).start())

    def local_grad(xx, kk):
        q = xx * 2 + kk
        packed = cvf[xx, kk].reshape(top, LX)
        first = dot(packed[:, 0:LP], ghp[...], NN)
        both = dot(packed[:, 512:], ght[...], NN).reshape(nz, 16, 256)
        last = both[:, 0:8, 0:128] + both[:, 8:16, 128:256]
        part = jnp.concatenate([first, last.reshape(ch - top, 128)], axis=0) + slots(err_ref[:, q])
        cor[:, q] = natural_rows(part)
        chl[q, 0:ch, :] = jnp.concatenate(split2(part), axis=1)

    if ch < 256:
        chl[:, ch:, :] = jnp.zeros((nxk, 256 - ch, 256), BF16)
    loop(1, ny, lambda s: ys_copy(s).wait_recv())
    total = ys[0]
    for q in range(1, ny):
        total = total + ys[q]
    ll[k, z, x] = total

    def lx_copy(s):
        own = ll.at[k, z, x]
        return copy(own, own, s_lx.at[s], r_lx.at[s], at_x(lax.rem(x + s, nx)))

    loop(1, nx, lambda s: lx_copy(s).start())

    local_grad(x, k)

    loop(1, nz, lambda s: xz_copy(s).wait_recv())
    xp[:, 0:128] = jnp.zeros((ch, 128), F32)
    xp[:, 128 + LP :] = jnp.zeros((ch, LX - 128 - LP), F32)
    for zz in range(nz):
        first, last = unpack(xz[zz])
        xp[OWN * zz : OWN * zz + 16, 128 : 128 + LP] = first
        xp[OWN * zz + 16 : OWN * zz + 24, 128 : 128 + LP] = last
    near_right.wait_recv()
    near_left.wait_recv()
    g32[...] += rh2[0].astype(F32) + rh2[1].astype(F32)
    pair_row = lax.broadcasted_iota(jnp.int32, (OWN, 7 * OWN), 0)
    pair_lane = lax.broadcasted_iota(jnp.int32, (OWN, 7 * OWN), 1)
    diagonal = lax.rem(pair_lane, OWN) == pair_row
    tap_row = lax.broadcasted_iota(jnp.int32, (8, 7 * OWN), 0)

    def kernel_terms(zz):
        rows = pl.ds(pl.multiple_of(zz * OWN, 8), OWN)
        maps = jnp.concatenate(shifted(xp[rows, :]), axis=0).astype(BF16)
        gt = g32[rows, :]
        moved = [pltpu.roll(gt * mk[b : b + 1, :], 32 + b - 3, 1) for b in range(7)]
        hi, lo = split2(jnp.concatenate(moved, axis=0))
        pairs = dot(hi, maps, NT) + dot(lo, maps, NT)
        out = jnp.zeros((8, 7 * OWN), F32)
        for b in range(7):
            block = jnp.where(diagonal, pairs[OWN * b : OWN * (b + 1)], 0.0)
            one = jnp.sum(block, axis=0, keepdims=True)
            out = jnp.where(tap_row == b, one, out)
        kgt[zz] = jnp.concatenate([out, jnp.zeros((8, 256 - 7 * OWN), F32)], axis=1)

    loop(0, nz, kernel_terms, 2)

    def rk_copy(s):
        zz = zpeer(s)
        return copy(kgt.at[zz], rk.at[z], s_rk.at[s], r_rk.at[s], at_z(zz))

    loop(1, nz, lambda s: rk_copy(s).start())
    rk[z] = kgt[z]

    def lx_wait(s):
        got = ll.at[k, z, lax.rem(x - s + nx, nx)]
        copy(got, got, s_lx.at[s], r_lx.at[s], at_x(lax.rem(x + s, nx))).wait_recv()

    loop(1, nx, lx_wait)

    def lz_copy(s):
        own = ll.at[k, z]
        return copy(own, own, s_lz.at[s], r_lz.at[s], at_z(zpeer(s)))

    loop(1, nz, lambda s: lz_copy(s).start())

    cx_copies[0].wait_recv()
    part0 = cvf.at[left_x, k, pl.ds(0, nz // 2)]
    cx_copies.append(copy(part0, part0, s_cx.at[2], r_cx.at[2], at_x(right_x)))
    cx_copies[2].start()
    cc_copy(1).start()
    cx_copies[1].wait_recv()
    part1 = cvf.at[right_x, k, pl.ds(nz // 2, nz // 2)]
    cx_copies.append(copy(part1, part1, s_cx.at[3], r_cx.at[3], at_x(left_x)))
    cx_copies[3].start()
    cc_copy(2).start()
    local_grad(left_x, k)
    local_grad(right_x, k)

    for s in range(3):
        cc_copy(s).wait_recv()
        local_grad(sources[s], 1 - k)

    loop(1, nz, lambda s: rk_copy(s).wait_recv())
    total = rk[0]
    for q in range(1, nz):
        total = total + rk[q]
    yk[y] = total

    def yk_copy(s):
        return copy(yk.at[y], yk.at[y], s_yk.at[s], r_yk.at[s], at_y(lax.rem(y + s, ny)))

    loop(1, ny, lambda s: yk_copy(s).start())

    def lz_wait(s):
        got = ll.at[k, lax.rem(z - s + nz, nz)]
        copy(got, got, s_lz.at[s], r_lz.at[s], at_z(zpeer(s))).wait_recv()

    loop(1, nz, lz_wait)
    lk_copy = copy(ll.at[k], ll.at[k], s_lk.at[0], r_lk.at[0], sibling)
    lk_copy.start()

    cx_copies[2].wait_recv()
    cx_copies[3].wait_recv()
    cc_copy(3).start()
    local_grad(far_x, k)

    lk_copy.wait_recv()

    def left_of(q):
        rows = []
        for rg in range(4):
            tiles = [ll[q % 2, t // tpz, q // 2, t % tpz] for t in (2 * rg, 2 * rg + 1)]
            rows.append(jnp.concatenate(tiles, axis=1))
        return jnp.concatenate(rows, axis=0)

    lefts = [left_of(q) for q in range(nxk)]
    wide3 = split3(jnp.concatenate(lefts, axis=1))
    stack3 = jnp.concatenate(wide3, axis=0)
    gram = None
    for part in wide3:
        term = dot(stack3, part, NT)
        term = term[0:32] + term[32:64] + term[64:96]
        gram = term if gram is None else gram + term
    cc_copy(3).wait_recv()
    local_grad(far_x, 1 - k)
    cor_store = pltpu.make_async_copy(cor, cor_out, s_in.at[6])
    cor_store.start()

    right = None
    for q in range(nxk):
        term = dot(jnp.concatenate(split2(lefts[q]), axis=0), chl[q], NN)
        right = term if q == 0 else right + term
    right = right[0:32] + right[32:64]
    rp[y] = right[:, 0:128] + right[:, 128:256]

    def rp_copy(s):
        return copy(rp.at[y], rp.at[y], s_rp.at[s], r_rp.at[s], at_y(lax.rem(y + s, ny)))

    loop(1, ny, lambda s: rp_copy(s).start())

    for q in range(nxk):
        lsn[:, q] = natural_rows(lefts[q].T)
    natural = lsn[...].reshape(channels, RANK).T
    nh, nm, nl = split3(natural)
    ls4[...] = jnp.concatenate([nh, nm, nh, nm], axis=0).T
    ls4_store = pltpu.make_async_copy(ls4, ls4_out, s_in.at[7])
    ls4_store.start()

    row_id = lax.broadcasted_iota(jnp.int32, (RANK, RANK), 0)
    lane_id = lax.broadcasted_iota(jnp.int32, (RANK, RANK), 1)
    same = row_id == lane_id
    aug = jnp.concatenate([gram, same.astype(F32)], axis=1)
    row_col = lax.broadcasted_iota(jnp.int32, (RANK, 2 * RANK), 0)

    def full(v):
        return jnp.broadcast_to(v, (RANK, 2 * RANK))

    for i in range(0, RANK, 2):
        c0 = full(aug[:, i : i + 1])
        c1 = full(aug[:, i + 1 : i + 2])
        r0 = full(aug[i : i + 1, :])
        r1 = full(aug[i + 1 : i + 2, :])
        p00 = full(c0[i : i + 1, :])
        p01 = full(c1[i : i + 1, :])
        p11 = full(c1[i + 1 : i + 2, :])
        inv = 1.0 / (p00 * p11 - p01 * p01)
        u0 = (p11 * c0 - p01 * c1) * inv
        u1 = (p00 * c1 - p01 * c0) * inv
        u0 = jnp.where(row_col > i + 1, u0, jnp.where(row_col == i + 1, p01 / p00, 0.0))
        u1 = jnp.where(row_col > i + 1, u1, 0.0)
        aug = aug - u0 * r0 - u1 * r1
    diag = jnp.sum(jnp.where(same, aug[:, 0:RANK], 0.0), axis=1, keepdims=True)
    scale = lax.rsqrt(diag)
    scale = scale * (1.5 - 0.5 * diag * scale * scale)
    linv = aug[:, RANK:] * scale
    ih, im, il = split3(linv)
    left[...] = dot(
        jnp.concatenate([ih, ih, ih, im, im, il], axis=1),
        jnp.concatenate([nh, nm, nl, nh, nm, nh], axis=0),
        NN,
    )
    left_store = pltpu.make_async_copy(left, left_out, s_in.at[8])
    left_store.start()

    inverse = dot(linv.T, linv, NN, HIGH) * (1.0 / workers)
    ah, am, al = split3(jnp.concatenate([linv, inverse], axis=0))
    final_left = jnp.concatenate([ah, ah, ah, am, am, al], axis=1)

    loop(1, ny, lambda s: rp_copy(s).wait_recv())
    total = rp[0]
    for q in range(1, ny):
        total = total + rp[q]
    th, tm, tl = split3(total)
    solved = dot(final_left, jnp.concatenate([th, tm, tl, th, tm, th], axis=0), NN)
    right_out[...] = solved[0:RANK]
    wh, wl = split2(solved[RANK:])
    w_out[...] = jnp.concatenate([wh, wh, wl, wl], axis=0)

    loop(1, ny, lambda s: yk_copy(s).wait_recv())
    total = yk[0]
    for q in range(1, ny):
        total = total + yk[q]
    for a in range(7):
        kg_out[a] = total[0:7, OWN * a : OWN * (a + 1)]

    for one in (cor_store, ls4_store, left_store):
        one.wait()
    loop(1, nz, lambda s: cz_copy(s).wait_send())
    loop(1, nz, lambda s: xz_copy(s).wait_send())
    es_copy.wait_send()
    for one in (in_r, in_gh, in_w):
        one.wait_send()
    loop(1, nx, lambda s: cs_copy(s).wait_send())
    loop(1, nx, lambda s: cg_copy(s).wait_send())
    gt_copy.wait_send()
    loop(1, nz, lambda s: rz_copy(s).wait_send())
    loop(1, ny, lambda s: ys_copy(s).wait_send())
    loop(1, nx, lambda s: lx_copy(s).wait_send())
    loop(1, nz, lambda s: lz_copy(s).wait_send())
    lk_copy.wait_send()
    loop(1, ny, lambda s: rp_copy(s).wait_send())
    loop(1, nz, lambda s: rk_copy(s).wait_send())
    loop(1, ny, lambda s: yk_copy(s).wait_send())
    for s in range(4):
        cx_copies[s].wait_send()
        cc_copy(s).wait_send()
    for one in (far_right, far_left, near_right, near_left):
        one.wait_send()


def finish(kg_ref, left_ref, right_ref, w_ref, ls_ref, cor_ref, kg_out, left_out, right_out, err_out):
    kg_out[...] = kg_ref[...]
    left_out[...] = left_ref[...]
    right_out[...] = right_ref[...]
    approx = dot(ls_ref[...], w_ref[...], NN)
    err_out[...] = cor_ref[...] - approx.reshape(cor_ref.shape)


def on_device(ny, nz, nx, block_input, depth_kernel, w_expand, grad_hidden, error_old, right_init):
    nxk = 2 * nx
    ch = OWN * nz
    channels = nz * nxk * OWN
    tpz = 8 // nz
    hid = right_init.shape[0]
    vmem = pltpu.VMEM
    scratch = [
        vmem((SIDE, SIDE, OWN), BF16),
        vmem((7, 7, channels), F32),
        vmem((channels, 128), BF16),
        vmem((nz, nxk, OWN, 128), F32),
        vmem((RANK, 128), F32),
        vmem((LP, 128), BF16),
        vmem((LP, 128), BF16),
        vmem((LX - 512, 256), BF16),
        vmem((channels, 128), BF16),
        vmem((RANK, 128), F32),
        vmem((nz, nx, 2, OWN, 256), F32),
        vmem((LP, OWN), F32),
        vmem((OWN, LX), F32),
        vmem((OWN, LP), F32),
        vmem((nz, 16, LX), BF16),
        vmem((nz, 16, LX), BF16),
        vmem((ch, LX), F32),
        vmem((8, LP), F32),
        vmem((64, channels), F32),
        vmem((OWN, 64), F32),
        vmem((nx, 2, nz, 16, LX), BF16),
        vmem((2, ch, LP), F32),
        vmem((3, ch, LP), BF16),
        vmem((2, ch // 2, LP), BF16),
        vmem((2, ch, LP), BF16),
        vmem((ch, LP), F32),
        vmem((nx, 2, 8, 8, 128), F32),
        vmem((2, 10, 8, 128), F32),
        vmem((nx, 8, 8, 128), F32),
        vmem((nx, 2, 8, 8, 128), F32),
        vmem((nx, 10, 8, 128), F32),
        vmem((2, 10, 8, 128), F32),
        vmem((8, 8, 128), F32),
        vmem((nz, tpz, 8, 128), F32),
        vmem((ny, tpz, 8, 128), F32),
        vmem((2, nz, nx, tpz, 8, 128), F32),
        vmem((nxk, 256, 256), BF16),
        vmem((ny, RANK, 128), F32),
        vmem((nz, 8, 256), F32),
        vmem((nz, 8, 256), F32),
        vmem((ny, 8, 256), F32),
        vmem((nz, nxk, OWN, RANK), F32),
        vmem((channels, 4 * RANK), BF16),
        vmem((nz, nxk, OWN, 128), F32),
        vmem((RANK, channels), F32),
    ]
    sems = [pltpu.SemaphoreType.DMA((9,))]
    for count in (nz, nz, 2, nx, nx, 1, nz, ny, nx, nz, 1, ny, nz, ny, 4, 4, 4, 4):
        sems += [pltpu.SemaphoreType.DMA((count,))] * 2
    spec = pl.BlockSpec(memory_space=pltpu.VMEM)
    far = pl.BlockSpec(memory_space=pl.ANY)
    cor_shape = jax.ShapeDtypeStruct((nz, nxk, OWN, 128), F32)
    mids = (
        jax.ShapeDtypeStruct((7, 7, OWN), F32),
        jax.ShapeDtypeStruct((RANK, channels), F32),
        jax.ShapeDtypeStruct((RANK, 128), F32),
        jax.ShapeDtypeStruct((4 * RANK, 128), BF16),
        jax.ShapeDtypeStruct((channels, 4 * RANK), BF16),
        cor_shape,
    )
    parts = pl.pallas_call(
        functools.partial(kernel, ny, nz, nx),
        out_shape=mids,
        in_specs=[pl.BlockSpec(memory_space=pl.ANY)] * 6,
        out_specs=(spec, far, spec, spec, far, far),
        scratch_shapes=scratch + sems,
        compiler_params=pltpu.CompilerParams(
            collective_id=0, has_side_effects=True, vmem_limit_bytes=60 * 1024 * 1024
        ),
        cost_estimate=pl.CostEstimate(
            flops=600_000_000, bytes_accessed=4_000_000, transcendentals=0
        ),
    )(
        block_input.reshape(SIDE, SIDE, OWN),
        depth_kernel,
        w_expand,
        grad_hidden.reshape(POS, 128),
        error_old.reshape(nz, nxk, OWN, 128),
        right_init.T,
    )
    kg, left, right, err = pl.pallas_call(
        finish,
        out_shape=mids[0:3] + (cor_shape,),
        in_specs=[spec] * 6,
        out_specs=(spec,) * 4,
        compiler_params=pltpu.CompilerParams(vmem_limit_bytes=60 * 1024 * 1024),
        cost_estimate=pl.CostEstimate(
            flops=60_000_000, bytes_accessed=2_500_000, transcendentals=0
        ),
    )(*parts)
    return (
        kg,
        left.T,
        right.T,
        err.reshape(1, channels, 128),
    )


def solution(mesh, nx=NX):
    ny = mesh.shape["outer"]
    nz = mesh.shape["chip"] // (2 * nx)
    placed = (
        P("outer", None, None, "chip"),
        P(),
        P(None, "chip"),
        P("outer", None, None, "chip"),
        P("outer", None, "chip"),
        P("chip", None),
    )
    return jax.shard_map(
        functools.partial(on_device, ny, nz, nx),
        mesh=mesh,
        in_specs=placed,
        out_specs=(P(None, None, "chip"), P(), P("chip", None), P("outer", None, "chip")),
        check_vma=False,
    )
```
